32 devices in a mesh: dp: 8 (over z, x), group: 4 (over y, core).
Axes of the slice: x: 2, y: 2, z: 4, core: 2. Of those that a mesh axis runs over, the one named last changes fastest.
Arguments:
- image_emb: bfloat16 [8192, 1152], P(('dp', 'group')), may hold values from -0.17675781 to 0.17675781
- text_emb: float32 [8192, 1152], P(('dp', 'group')), may hold values from -0.17677669 to 0.17677669
- text_accum: float32 [8192, 1152], P(('dp', 'group')), may hold values from -6 to 6
- pair_ids: int32 [8192], P(('dp', 'group')), may hold values from 0 to 127
- log_scale: float32 [1], replicated, may hold values from 1 to 2
- bias: float32 [1], replicated, may hold values from -3 to 0
Outputs:
- row_loss: float32 [8192], P(('dp', 'group'))
- image_grad: bfloat16 [8192, 1152], P(('dp', 'group'))
- text_grad: float32 [8192, 1152], P(('dp', 'group'))
The draws below stay inside these ranges and needn't reach their ends.
Inputs may be any that keep to these rules, and one draw needn't show every extreme that they name: `pair_ids`: two examples form a positive pair exactly where their ids are equal.
All inputs are finite; a program needn't handle non-finite values.
Results may differ from the reference program's by a relative error of at most 0.0059.
Values may be sent and summed in bfloat16 or wider, within the bound.
No kernel may reach another device: no remote copies, remote signals or barrier semaphores. Data moves between devices by JAX's collectives and lax.ppermute only.
A program may use at most 64 MiB of HBM per device.

```python
import jax
import jax.numpy as jnp
from jax import lax

D = 1152
TOK_DEV = 256
SHIFTS = 2
TOKENS = 8192


def set_ends(values, own_key, low, largest):
    longest = values.shape.index(max(values.shape))
    spots = []
    for shift in (0, 1):
        where = [jax.random.randint(jax.random.fold_in(own_key, axis), (), 0, length) for axis, length in enumerate(values.shape)]
        where[longest] = (where[longest] + shift) % values.shape[longest]
        spots.append(tuple(where))
    return values.at[spots[0]].set(low).at[spots[1]].set(largest)


def levels(own_key, extent, shards, least, top_value):
    def one(axis_at, blocks):
        draws = jax.random.uniform(jax.random.fold_in(jax.random.fold_in(own_key, 6), axis_at), (blocks,), jnp.float32, least / len(shards), top_value / len(shards))
        return jnp.repeat(jnp.exp(draws), extent[axis_at] // blocks).reshape((-1,) + (1,) * (len(extent) - axis_at - 1))

    gain = one(*shards[0])
    for cut in shards[1:]:
        gain = gain * one(*cut)
    return gain


def centred(stream_key, extent, deviation, most, cuts=(), kind=jnp.bfloat16):
    drawn = jax.random.normal(stream_key, extent, jnp.float32) * deviation
    if len(cuts) > 0:
        drawn = levels(stream_key, extent, cuts, -0.22, 0.18) * drawn
    return jnp.clip(drawn, min=-most, max=most).astype(kind)


def setup_inputs(seed: int = 0) -> dict:
    keys = jax.random.split(jax.random.key(seed), 7)
    image_emb = centred(keys[0], (TOKENS, D), (D ** -0.5), 0.17675781, ((0, 32),))
    text_emb = centred(keys[1], (TOKENS, D), (D ** -0.5), 0.17677669, ((0, 32),), jnp.float32)
    text_accum = centred(keys[2], (TOKENS, D), 1.0, 6.0, ((0, 32),), jnp.float32)
    pair_ids = set_ends(jax.random.randint(keys[3], (TOKENS,), 0, TOK_DEV // 2), jax.random.fold_in(keys[3], 1), 0, (TOK_DEV // 2) - 1).astype(jnp.int32)
    log_scale = jnp.clip(jax.random.uniform(keys[4], (1,), jnp.float32, 1.0, 2.0), 1.0, 2.0)
    bias = jnp.clip(jax.random.uniform(keys[5], (1,), jnp.float32, -3.0, 0.0), -3.0, 0.0)
    return {"image_emb": image_emb, "text_emb": text_emb, "text_accum": text_accum, "pair_ids": pair_ids, "log_scale": log_scale, "bias": bias}


def block_terms(image_block, text_block, image_ids, text_ids, scale, shift):
    logits = scale * lax.dot_general(image_block, text_block, (((1,), (1,)), ((), ())), preferred_element_type=jnp.float32) + shift
    signs = jnp.where(image_ids[:, None] == text_ids[None, :], 1.0, -1.0).astype(jnp.float32)
    loss = jnp.sum(jax.nn.softplus(-signs * logits), axis=1)
    coef = (-signs * jax.nn.sigmoid(-signs * logits) * scale).astype(jnp.bfloat16)
    image_part = jnp.dot(coef, text_block, preferred_element_type=jnp.float32)
    text_part = lax.dot_general(coef, image_block, (((0,), (0,)), ((), ())), preferred_element_type=jnp.float32)
    return loss, image_part, text_part


def reference(image_emb, text_emb, text_accum, pair_ids, log_scale, bias):
    blocks = TOKENS // TOK_DEV
    scale = jnp.exp(log_scale[0])
    shift = bias[0]
    text_low = text_emb.astype(jnp.bfloat16)
    images = image_emb.reshape(blocks, TOK_DEV, D)
    texts = text_low.reshape(blocks, TOK_DEV, D)
    id_rows = pair_ids.reshape(blocks, TOK_DEV)

    def one_block(index):
        image_block = images[index]
        image_ids = id_rows[index]
        loss = jnp.zeros((TOK_DEV,), jnp.float32)
        image_sum = jnp.zeros((TOK_DEV, D), jnp.float32)
        text_parts = []
        for step in range(SHIFTS + 1):
            other = (index - step) % blocks
            part_loss, image_part, text_part = block_terms(image_block, texts[other], image_ids, id_rows[other], scale, shift)
            loss = loss + part_loss
            image_sum = image_sum + image_part
            text_parts.append(text_part)
        return loss, image_sum.astype(jnp.bfloat16), jnp.stack(text_parts)

    losses, image_grads, text_parts = lax.map(one_block, jnp.arange(blocks, dtype=jnp.int32))
    row_loss = (losses / ((SHIFTS + 1) * TOK_DEV)).reshape(TOKENS)
    total = text_accum.reshape(blocks, TOK_DEV, D)
    for step in range(SHIFTS + 1):
        total = total + jnp.roll(text_parts[:, step], -step, axis=0)
    text_grad = jnp.roll(total, SHIFTS, axis=0).reshape(TOKENS, D)
    return row_loss, image_grads.reshape(TOKENS, D), text_grad
```

```python
import jax
import jax.numpy as jnp
from jax import lax
from jax.sharding import PartitionSpec as P

SHIFTS = 2
AXES = ("dp", "group")


def rows_of(a, b):
    return lax.dot_general(a, b, (((1,), (1,)), ((), ())), preferred_element_type=jnp.float32)


def back(coef, images):
    return lax.dot_general(coef, images, (((0,), (0,)), ((), ())), preferred_element_type=jnp.float32)


def pair(images, texts, image_ids, text_ids, scale, shift):
    logits = scale * rows_of(images, texts) + shift
    signs = jnp.where(image_ids[:, None] == text_ids[None, :], 1.0, -1.0).astype(jnp.float32)
    margin = -signs * logits
    coef = (-signs * jax.nn.sigmoid(margin) * scale).astype(jnp.bfloat16)
    return margin, coef


def body(image_emb, text_emb, text_accum, pair_ids, log_scale, bias):
    count = lax.axis_size(AXES)
    rows = image_emb.shape[0]
    even = lax.axis_index("group") % 2 == 0
    scale = jnp.exp(log_scale[0])
    shift = bias[0]

    def send(value, route):
        return lax.ppermute(value, AXES, route)

    skip = [(i, (i + 2) % count) for i in range(count)]
    swap = [(i, i ^ 1) for i in range(count)]
    to_odd = [(i, i + 1) for i in range(0, count, 2)]
    to_even = [(i + 1, i) for i in range(0, count, 2)]

    texts = text_emb.astype(jnp.bfloat16)
    mate_ids = send(pair_ids, swap)
    texts_2 = send(texts, skip)
    mate_images = send(image_emb, swap)
    texts_in = send(texts, to_odd)
    both_ids = send(jnp.concatenate([pair_ids, mate_ids]), skip)
    ids_2 = both_ids[:rows]
    ids_1 = jnp.where(even, both_ids[rows:], mate_ids)

    margin_0, coef_0 = pair(image_emb, texts, pair_ids, pair_ids, scale, shift)
    _, mate_coef = pair(mate_images, texts, mate_ids, pair_ids, scale, shift)
    mate_coef = jnp.where(even, mate_coef, jnp.zeros_like(mate_coef))
    outgoing = text_accum + back(coef_0, image_emb) + back(mate_coef, mate_images)
    arrived = send(outgoing.astype(jnp.bfloat16), skip)

    margin_2, coef_2 = pair(image_emb, texts_2, pair_ids, ids_2, scale, shift)
    _, mate_coef = pair(mate_images, texts_2, mate_ids, ids_2, scale, shift)
    mate_coef = jnp.where(even, jnp.zeros_like(mate_coef), mate_coef)
    late = back(coef_2, image_emb) + back(mate_coef, mate_images)

    texts_1 = jnp.where(even, send(texts_2, to_even), texts_in)
    margin_1, coef_1 = pair(image_emb, texts_1, pair_ids, ids_1, scale, shift)

    loss = sum(jnp.sum(jax.nn.softplus(m), axis=1) for m in (margin_0, margin_1, margin_2))
    image_grad = (
        jnp.dot(coef_0, texts, preferred_element_type=jnp.float32)
        + jnp.dot(coef_1, texts_1, preferred_element_type=jnp.float32)
        + jnp.dot(coef_2, texts_2, preferred_element_type=jnp.float32)
    )
    text_grad = arrived.astype(jnp.float32) + late
    return (loss / ((SHIFTS + 1) * rows), image_grad.astype(jnp.bfloat16), text_grad)


def solution(mesh):
    in_specs = (P(AXES, None), P(AXES, None), P(AXES, None), P(AXES), P(), P())
    out_specs = (P(AXES), P(AXES, None), P(AXES, None))
    return jax.shard_map(body, mesh=mesh, in_specs=in_specs, out_specs=out_specs, check_vma=False)
```

```python
import jax
import jax.numpy as jnp
from jax import lax
from jax.experimental import pallas as pl
from jax.experimental.pallas import tpu as pltpu
from jax.sharding import PartitionSpec as P

SHIFTS = 2
AXES = ("dp", "group")
PAD = 16
CHUNKS = 4
VMEM = pl.BlockSpec(memory_space=pltpu.VMEM)
SMEM = pl.BlockSpec(memory_space=pltpu.SMEM)
HBM = pl.BlockSpec(memory_space=pltpu.HBM)


def dot(a, b, contract):
    return lax.dot_general(a, b, ((contract[:1], contract[1:]), ((), ())), preferred_element_type=jnp.float32)


def ids_of(text, at, rows):
    parts = text[at:, :rows].astype(jnp.float32).astype(jnp.int32)
    return parts[0:1] + parts[1:2] * 256 + parts[2:3] * 65536 + parts[3:4] * 16777216


def pair(images, texts, image_ids, text_ids, params):
    raw = dot(images, texts, (1, 1))
    rows = raw.shape[0]
    scale = jnp.exp(jnp.full((1, rows), params[0], jnp.float32))
    logits = scale * raw + params[1]
    same = jnp.broadcast_to(image_ids, (rows, rows)).T == text_ids
    margin = jnp.where(same, -logits, logits)
    tail = jnp.exp(-jnp.abs(margin))
    loss = jnp.maximum(margin, 0.0) + jnp.log1p(tail)
    sigmoid = jnp.where(margin >= 0, 1.0, tail) / (1.0 + tail)
    coef = jnp.where(same, -sigmoid, sigmoid) * scale
    return jnp.sum(loss.T, axis=0, keepdims=True), coef


def low(coef):
    return coef.astype(jnp.bfloat16)


def cast_kernel(ids, text, out, staged, sems):
    rows, width = text.shape
    step = rows // CHUNKS
    copies = [
        pltpu.make_async_copy(text.at[pl.ds(k * step, step)], staged.at[pl.ds(k * step, step)], sems.at[k])
        for k in range(CHUNKS)
    ]
    for copy in copies:
        copy.start()
    row = lax.broadcasted_iota(jnp.int32, (PAD, rows), 0)
    spread = jnp.broadcast_to(ids[...], (PAD, rows))
    parts = jnp.zeros((PAD, rows), jnp.int32)
    for k in range(4):
        parts = jnp.where(row == k, (spread >> (8 * k)) & 255, parts)
    out[rows:, :] = jnp.zeros((PAD, width), out.dtype)
    out[rows:, :rows] = parts.astype(jnp.float32).astype(out.dtype)
    for k, copy in enumerate(copies):
        copy.wait()
        out[k * step:(k + 1) * step, :] = staged[k * step:(k + 1) * step, :].astype(out.dtype)


def own_kernel(flags, params, ids, mate_ids, image, mate_a, mate_b, text, accum, out, image_sum, loss):
    rows = image.shape[0]
    own_loss, coef = pair(image[...], text[:rows, :], ids[...], ids[...], params)
    loss[...] = own_loss
    total = accum[...] + dot(low(coef.T), image[...], (1, 0))

    @pl.when(flags[0] == 0)
    def _():
        mate = jnp.concatenate([mate_a[...], mate_b[...]], axis=0)
        _, mate_coef = pair(mate, text[:rows, :], mate_ids[...], ids[...], params)
        out[...] = (total + dot(low(mate_coef.T), mate, (1, 0))).astype(out.dtype)

    @pl.when(flags[0] == 1)
    def _():
        out[...] = total.astype(out.dtype)

    image_sum[...] = dot(low(coef), text[:rows, :], (1, 0))


def relay_kernel(flags, token, text, far, out_a, out_b):
    cut = out_a.shape[0]

    def fill(source):
        out_a[...] = source[:cut, :]
        out_b[...] = source[cut:, :]

    pl.when(flags[0] == 0)(lambda: fill(text))
    pl.when(flags[0] == 1)(lambda: fill(far))


def far_kernel(flags, params, ids, mate_ids, image, mate_a, mate_b, far, image_in, loss_in, late, image_sum, loss):
    rows = image.shape[0]
    far_ids = ids_of(far, rows, rows)
    more, coef = pair(image[...], far[:rows, :], ids[...], far_ids, params)
    loss[...] = loss_in[...] + more
    image_sum[...] = image_in[...] + dot(low(coef), far[:rows, :], (1, 0))
    part = dot(low(coef.T), image[...], (1, 0))

    @pl.when(flags[0] == 0)
    def _():
        late[...] = part

    @pl.when(flags[0] == 1)
    def _():
        mate = jnp.concatenate([mate_a[...], mate_b[...]], axis=0)
        _, mate_coef = pair(mate, far[:rows, :], mate_ids[...], far_ids, params)
        late[...] = part + dot(low(mate_coef.T), mate, (1, 0))


def near_kernel(params, ids, image, near_a, near_b, image_in, loss_in, image_grad, loss):
    rows = image.shape[0]
    rest = rows - near_a.shape[0]
    near = jnp.concatenate([near_a[...], near_b[:rest, :]], axis=0)
    more, coef = pair(image[...], near, ids[...], ids_of(near_b, rest, rows), params)
    loss[...] = (loss_in[...] + more) * (1.0 / ((SHIFTS + 1) * rows))
    image_grad[...] = (image_in[...] + dot(low(coef), near, (1, 0))).astype(image_grad.dtype)


def call(kernel, name, outs, scalars, *operands):
    return pl.pallas_call(
        kernel,
        out_shape=[jax.ShapeDtypeStruct(s, d) for s, d in outs],
        in_specs=[SMEM] * len(scalars) + [VMEM] * len(operands),
        out_specs=[VMEM] * len(outs),
        compiler_params=pltpu.CompilerParams(vmem_limit_bytes=32 * 1024 * 1024),
        cost_estimate=pl.CostEstimate(flops=0, bytes_accessed=0, transcendentals=0),
        name=name,
    )(*scalars, *operands)


def body(image_emb, text_emb, text_accum, pair_ids, log_scale, bias):
    count = lax.axis_size(AXES)
    rows, width = image_emb.shape
    half = rows // 2
    f32, bf16 = jnp.float32, jnp.bfloat16
    flags = (lax.axis_index("group") % 2).astype(jnp.int32).reshape(1)
    params = jnp.concatenate([log_scale, bias])
    ids = pair_ids.reshape(1, rows)

    skip = [(i, (i + 2) % count) for i in range(count)]
    swap = [(i, i ^ 1) for i in range(count)]

    def ahead(value):
        return lax.ppermute(value, AXES, skip)

    def across(value):
        return lax.ppermute(value, AXES, swap)

    text = pl.pallas_call(
        cast_kernel,
        out_shape=jax.ShapeDtypeStruct((rows + PAD, width), bf16),
        in_specs=[VMEM, HBM],
        out_specs=VMEM,
        scratch_shapes=[pltpu.VMEM((rows, width), f32), pltpu.SemaphoreType.DMA((CHUNKS,))],
        cost_estimate=pl.CostEstimate(flops=0, bytes_accessed=0, transcendentals=0),
        name="cast",
    )(ids, text_emb)
    far = ahead(text)

    image, text = lax.optimization_barrier((image_emb, text))
    mate_a, mate_b = across(image[:half]), across(image[half:])
    mate_ids = across(ids)

    outgoing, image_sum, loss = call(
        own_kernel, "own", [((rows, width), bf16), ((rows, width), f32), ((1, rows), f32)],
        (flags, params), ids, mate_ids, image_emb, mate_a, mate_b, text, text_accum,
    )
    arrived = ahead(outgoing)

    passed_a, passed_b = call(
        relay_kernel, "relay", [((half, width), bf16), ((rows + PAD - half, width), bf16)],
        (flags,), loss, text, far,
    )
    near_a, near_b = across(passed_a), across(passed_b)
    late, image_sum, loss = call(
        far_kernel, "far", [((rows, width), f32), ((rows, width), f32), ((1, rows), f32)],
        (flags, params), ids, mate_ids, image_emb, mate_a, mate_b, far, image_sum, loss,
    )
    image_grad, loss = call(
        near_kernel, "near", [((rows, width), bf16), ((1, rows), f32)],
        (params,), ids, image_emb, near_a, near_b, image_sum, loss,
    )
    late, image_grad = lax.optimization_barrier((late, image_grad))
    text_grad = arrived.astype(f32) + late
    return (loss.reshape(rows), image_grad, text_grad)


def solution(mesh):
    in_specs = (P(AXES, None), P(AXES, None), P(AXES, None), P(AXES), P(), P())
    out_specs = (P(AXES), P(AXES, None), P(AXES, None))
    return jax.shard_map(body, mesh=mesh, in_specs=in_specs, out_specs=out_specs, check_vma=False)
```

```python
import jax
import jax.numpy as jnp
from jax import lax
from jax.experimental import pallas as pl
from jax.experimental.pallas import tpu as pltpu
from jax.sharding import PartitionSpec as P

SHIFTS = 2
AXES = ("dp", "group")
PAD = 16
CHUNKS = 4
VMEM = pl.BlockSpec(memory_space=pltpu.VMEM)
SMEM = pl.BlockSpec(memory_space=pltpu.SMEM)
HBM = pl.BlockSpec(memory_space=pltpu.HBM)


def dot(a, b, contract):
    return lax.dot_general(a, b, ((contract[:1], contract[1:]), ((), ())), preferred_element_type=jnp.float32)


def ids_of(text, at, rows):
    parts = text[at:, :rows].astype(jnp.float32).astype(jnp.int32)
    return parts[0:1] + parts[1:2] * 256 + parts[2:3] * 65536 + parts[3:4] * 16777216


def pair(images, texts, image_ids, text_ids, params):
    raw = dot(images, texts, (1, 1))
    rows = raw.shape[0]
    scale = jnp.exp(jnp.full((1, rows), params[0], jnp.float32))
    logits = scale * raw + params[1]
    same = jnp.broadcast_to(image_ids, (rows, rows)).T == text_ids
    margin = jnp.where(same, -logits, logits)
    tail = jnp.exp(-jnp.abs(margin))
    loss = jnp.maximum(margin, 0.0) + jnp.log1p(tail)
    sigmoid = jnp.where(margin >= 0, 1.0, tail) / (1.0 + tail)
    coef = jnp.where(same, -sigmoid, sigmoid) * scale
    return jnp.sum(loss.T, axis=0, keepdims=True), coef


def low(coef):
    return coef.astype(jnp.bfloat16)


def cast_kernel(ids, text, out, staged, ids_in, sems, ids_sem):
    rows, width = text.shape
    step = rows // CHUNKS
    ids_copy = pltpu.make_async_copy(ids, ids_in, ids_sem)
    copies = [
        pltpu.make_async_copy(text.at[pl.ds(k * step, step)], staged.at[pl.ds(k * step, step)], sems.at[k])
        for k in range(CHUNKS)
    ]
    for copy in copies:
        copy.start()
    ids_copy.start()
    out[rows:, :] = jnp.zeros((PAD, width), out.dtype)
    for k, copy in enumerate(copies):
        copy.wait()
        out[k * step:(k + 1) * step, :] = staged[k * step:(k + 1) * step, :].astype(out.dtype)
    ids_copy.wait()
    row = lax.broadcasted_iota(jnp.int32, (PAD, rows), 0)
    spread = jnp.broadcast_to(ids_in[...], (PAD, rows))
    parts = jnp.zeros((PAD, rows), jnp.int32)
    for k in range(4):
        parts = jnp.where(row == k, (spread >> (8 * k)) & 255, parts)
    out[rows:, :rows] = parts.astype(jnp.float32).astype(out.dtype)


def add_kernel(arrived, late, out, staged, sems):
    rows = arrived.shape[0]
    step = rows // CHUNKS
    copies = []
    for k in range(CHUNKS):
        part = pl.ds(k * step, step)
        staged[part, :] = arrived[part, :].astype(staged.dtype) + late[part, :]
        copies.append(pltpu.make_async_copy(staged.at[part], out.at[part], sems.at[k]))
        copies[-1].start()
    for copy in copies:
        copy.wait()


def own_kernel(flags, params, ids, mate_ids, image, mate_a, mate_b, text, accum, out, image_sum, loss):
    rows = image.shape[0]
    own_loss, coef = pair(image[...], text[:rows, :], ids[...], ids[...], params)
    loss[...] = own_loss
    total = accum[...] + dot(low(coef.T), image[...], (1, 0))

    @pl.when(flags[0] == 0)
    def _():
        mate = jnp.concatenate([mate_a[...], mate_b[...]], axis=0)
        _, mate_coef = pair(mate, text[:rows, :], mate_ids[...], ids[...], params)
        out[...] = (total + dot(low(mate_coef.T), mate, (1, 0))).astype(out.dtype)

    @pl.when(flags[0] == 1)
    def _():
        out[...] = total.astype(out.dtype)

    image_sum[...] = dot(low(coef), text[:rows, :], (1, 0))


def relay_kernel(flags, token, text, far, out_a, out_b):
    cut = out_a.shape[0]

    def fill(source):
        out_a[...] = source[:cut, :]
        out_b[...] = source[cut:, :]

    pl.when(flags[0] == 0)(lambda: fill(text))
    pl.when(flags[0] == 1)(lambda: fill(far))


def far_kernel(flags, params, ids, mate_ids, image, mate_a, mate_b, far, image_in, loss_in, late, image_sum, loss):
    rows = image.shape[0]
    far_ids = ids_of(far, rows, rows)
    more, coef = pair(image[...], far[:rows, :], ids[...], far_ids, params)
    loss[...] = loss_in[...] + more
    image_sum[...] = image_in[...] + dot(low(coef), far[:rows, :], (1, 0))
    part = dot(low(coef.T), image[...], (1, 0))

    @pl.when(flags[0] == 0)
    def _():
        late[...] = part

    @pl.when(flags[0] == 1)
    def _():
        mate = jnp.concatenate([mate_a[...], mate_b[...]], axis=0)
        _, mate_coef = pair(mate, far[:rows, :], mate_ids[...], far_ids, params)
        late[...] = part + dot(low(mate_coef.T), mate, (1, 0))


def near_kernel(params, ids, image, near_a, near_b, image_in, loss_in, image_grad, loss):
    rows = image.shape[0]
    rest = rows - near_a.shape[0]
    near = jnp.concatenate([near_a[...], near_b[:rest, :]], axis=0)
    more, coef = pair(image[...], near, ids[...], ids_of(near_b, rest, rows), params)
    loss[...] = (loss_in[...] + more) * (1.0 / ((SHIFTS + 1) * rows))
    image_grad[...] = (image_in[...] + dot(low(coef), near, (1, 0))).astype(image_grad.dtype)


def call(kernel, name, outs, scalars, *operands):
    return pl.pallas_call(
        kernel,
        out_shape=[jax.ShapeDtypeStruct(s, d) for s, d in outs],
        in_specs=[SMEM] * len(scalars) + [VMEM] * len(operands),
        out_specs=[VMEM] * len(outs),
        compiler_params=pltpu.CompilerParams(vmem_limit_bytes=16 * 1024 * 1024),
        cost_estimate=pl.CostEstimate(flops=0, bytes_accessed=0, transcendentals=0),
        name=name,
    )(*scalars, *operands)


def body(image_emb, text_emb, text_accum, pair_ids, log_scale, bias):
    count = lax.axis_size(AXES)
    rows, width = image_emb.shape
    half = rows // 2
    f32, bf16 = jnp.float32, jnp.bfloat16
    flags = (lax.axis_index("group") % 2).astype(jnp.int32).reshape(1)
    params = jnp.concatenate([log_scale, bias])
    ids = pair_ids.reshape(1, rows)

    skip = [(i, (i + 2) % count) for i in range(count)]
    swap = [(i, i ^ 1) for i in range(count)]

    def ahead(value):
        return lax.ppermute(value, AXES, skip)

    def across(value):
        return lax.ppermute(value, AXES, swap)

    text = pl.pallas_call(
        cast_kernel,
        out_shape=jax.ShapeDtypeStruct((rows + PAD, width), bf16),
        in_specs=[HBM, HBM],
        out_specs=VMEM,
        scratch_shapes=[
            pltpu.VMEM((rows, width), f32),
            pltpu.VMEM((1, rows), jnp.int32),
            pltpu.SemaphoreType.DMA((CHUNKS,)),
            pltpu.SemaphoreType.DMA,
        ],
        compiler_params=pltpu.CompilerParams(vmem_limit_bytes=16 * 1024 * 1024),
        cost_estimate=pl.CostEstimate(flops=0, bytes_accessed=0, transcendentals=0),
        name="cast",
    )(ids, text_emb)
    far = ahead(text)

    image, text = lax.optimization_barrier((image_emb, text))
    mate_a, mate_b = across(image[:half]), across(image[half:])
    mate_ids = across(ids)

    outgoing, image_sum, loss = call(
        own_kernel, "own", [((rows, width), bf16), ((rows, width), f32), ((1, rows), f32)],
        (flags, params), ids, mate_ids, image_emb, mate_a, mate_b, text, text_accum,
    )
    arrived = ahead(outgoing)

    passed_a, passed_b = call(
        relay_kernel, "relay", [((half, width), bf16), ((rows + PAD - half, width), bf16)],
        (flags,), loss, text, far,
    )
    near_a, near_b = across(passed_a), across(passed_b)
    late, image_sum, loss = call(
        far_kernel, "far", [((rows, width), f32), ((rows, width), f32), ((1, rows), f32)],
        (flags, params), ids, mate_ids, image_emb, mate_a, mate_b, far, image_sum, loss,
    )
    image_grad, loss = call(
        near_kernel, "near", [((rows, width), bf16), ((1, rows), f32)],
        (params,), ids, image_emb, near_a, near_b, image_sum, loss,
    )
    late, image_grad = lax.optimization_barrier((late, image_grad))
    text_grad = pl.pallas_call(
        add_kernel,
        out_shape=jax.ShapeDtypeStruct((rows, width), f32),
        in_specs=[VMEM, VMEM],
        out_specs=HBM,
        scratch_shapes=[pltpu.VMEM((rows, width), f32), pltpu.SemaphoreType.DMA((CHUNKS,))],
        compiler_params=pltpu.CompilerParams(vmem_limit_bytes=16 * 1024 * 1024),
        cost_estimate=pl.CostEstimate(flops=0, bytes_accessed=0, transcendentals=0),
        name="add",
    )(arrived, late)
    return (loss.reshape(rows), image_grad, text_grad)


def solution(mesh):
    in_specs = (P(AXES, None), P(AXES, None), P(AXES, None), P(AXES), P(), P())
    out_specs = (P(AXES), P(AXES, None), P(AXES, None))
    return jax.shard_map(body, mesh=mesh, in_specs=in_specs, out_specs=out_specs, check_vma=False)
```

```python
import jax
import jax.numpy as jnp
from jax import lax
from jax.experimental import pallas as pl
from jax.experimental.pallas import tpu as pltpu
from jax.sharding import PartitionSpec as P

SHIFTS = 2
AXES = ("dp", "group")
PAD = 8
CHUNKS = 4
VMEM = pl.BlockSpec(memory_space=pltpu.VMEM)
SMEM = pl.BlockSpec(memory_space=pltpu.SMEM)
HBM = pl.BlockSpec(memory_space=pltpu.HBM)


def dot(a, b, contract):
    return lax.dot_general(a, b, ((contract[:1], contract[1:]), ((), ())), preferred_element_type=jnp.float32)


def ids_of(text, at, rows):
    parts = text[at:, :rows].astype(jnp.float32).astype(jnp.int32)
    return parts[0:1] + parts[1:2] * 256 + parts[2:3] * 65536 + parts[3:4] * 16777216


def pair(images, texts, image_ids, text_ids, params):
    raw = dot(images, texts, (1, 1))
    rows = raw.shape[0]
    scale = jnp.exp(jnp.full((1, rows), params[0], jnp.float32))
    logits = scale * raw + params[1]
    same = jnp.broadcast_to(image_ids, (rows, rows)).T == text_ids
    margin = jnp.where(same, -logits, logits)
    tail = jnp.exp(-jnp.abs(margin))
    loss = jnp.maximum(margin, 0.0) + jnp.log1p(tail)
    sigmoid = jnp.where(margin >= 0, 1.0, tail) / (1.0 + tail)
    coef = jnp.where(same, -sigmoid, sigmoid) * scale
    return jnp.sum(loss.T, axis=0, keepdims=True), coef


def low(coef):
    return coef.astype(jnp.bfloat16)


def cast_kernel(parts, text, out):
    rows, width = text.shape
    out[:rows, :] = text[...].astype(out.dtype)
    out[rows:, :] = jnp.zeros((PAD, width), out.dtype)
    out[rows:, :rows] = parts[...].astype(out.dtype)


def add_kernel(arrived, late, out, staged, sems):
    rows = arrived.shape[0]
    step = rows // CHUNKS
    copies = []
    for k in range(CHUNKS):
        part = pl.ds(k * step, step)
        staged[part, :] = arrived[part, :].astype(staged.dtype) + late[part, :]
        copies.append(pltpu.make_async_copy(staged.at[part], out.at[part], sems.at[k]))
        copies[-1].start()
    for copy in copies:
        copy.wait()


def own_kernel(flags, params, ids, mate_ids, image, mate_a, mate_b, text, accum, out, image_sum, loss):
    rows = image.shape[0]
    own_loss, coef = pair(image[...], text[:rows, :], ids[...], ids[...], params)
    loss[...] = own_loss
    total = accum[...] + dot(low(coef.T), image[...], (1, 0))

    @pl.when(flags[0] == 0)
    def _():
        mate = jnp.concatenate([mate_a[...], mate_b[...]], axis=0)
        _, mate_coef = pair(mate, text[:rows, :], mate_ids[...], ids[...], params)
        out[...] = (total + dot(low(mate_coef.T), mate, (1, 0))).astype(out.dtype)

    @pl.when(flags[0] == 1)
    def _():
        out[...] = total.astype(out.dtype)

    image_sum[...] = dot(low(coef), text[:rows, :], (1, 0))


def relay_kernel(flags, token, text, far, out_a, out_b):
    cut = out_a.shape[0]

    def fill(source):
        out_a[...] = source[:cut, :]
        out_b[...] = source[cut:, :]

    pl.when(flags[0] == 0)(lambda: fill(text))
    pl.when(flags[0] == 1)(lambda: fill(far))


def far_kernel(flags, params, ids, mate_ids, image, mate_a, mate_b, far, image_in, loss_in, late, image_sum, loss):
    rows = image.shape[0]
    far_ids = ids_of(far, rows, rows)
    more, coef = pair(image[...], far[:rows, :], ids[...], far_ids, params)
    loss[...] = loss_in[...] + more
    image_sum[...] = image_in[...] + dot(low(coef), far[:rows, :], (1, 0))
    part = dot(low(coef.T), image[...], (1, 0))

    @pl.when(flags[0] == 0)
    def _():
        late[...] = part

    @pl.when(flags[0] == 1)
    def _():
        mate = jnp.concatenate([mate_a[...], mate_b[...]], axis=0)
        _, mate_coef = pair(mate, far[:rows, :], mate_ids[...], far_ids, params)
        late[...] = part + dot(low(mate_coef.T), mate, (1, 0))


def near_kernel(params, ids, image, near_a, near_b, image_in, loss_in, image_grad, loss):
    rows = image.shape[0]
    rest = rows - near_a.shape[0]
    near = jnp.concatenate([near_a[...], near_b[:rest, :]], axis=0)
    more, coef = pair(image[...], near, ids[...], ids_of(near_b, rest, rows), params)
    loss[...] = (loss_in[...] + more) * (1.0 / ((SHIFTS + 1) * rows))
    image_grad[...] = (image_in[...] + dot(low(coef), near, (1, 0))).astype(image_grad.dtype)


def call(kernel, name, outs, scalars, *operands):
    return pl.pallas_call(
        kernel,
        out_shape=[jax.ShapeDtypeStruct(s, d) for s, d in outs],
        in_specs=[SMEM] * len(scalars) + [VMEM] * len(operands),
        out_specs=[VMEM] * len(outs),
        compiler_params=pltpu.CompilerParams(vmem_limit_bytes=16 * 1024 * 1024),
        cost_estimate=pl.CostEstimate(flops=0, bytes_accessed=0, transcendentals=0),
        name=name,
    )(*scalars, *operands)


def body(image_emb, text_emb, text_accum, pair_ids, log_scale, bias):
    count = lax.axis_size(AXES)
    rows, width = image_emb.shape
    half = rows // 2
    f32, bf16 = jnp.float32, jnp.bfloat16
    flags = (lax.axis_index("group") % 2).astype(jnp.int32).reshape(1)
    params = jnp.concatenate([log_scale, bias])
    ids = pair_ids.reshape(1, rows)

    skip = [(i, (i + 2) % count) for i in range(count)]
    swap = [(i, i ^ 1) for i in range(count)]

    def ahead(value):
        return lax.ppermute(value, AXES, skip)

    def across(value):
        return lax.ppermute(value, AXES, swap)

    shifts = jnp.minimum(8 * jnp.arange(PAD, dtype=jnp.int32), 24)[:, None]
    parts = ((ids >> shifts) & 255).astype(f32)
    (text,) = call(cast_kernel, "cast", [((rows + PAD, width), bf16)], (), parts, text_emb)
    far = ahead(text)

    image, text = lax.optimization_barrier((image_emb, text))
    image_emb = image
    mate_a, mate_b = across(image[:half]), across(image[half:])
    mate_ids = across(ids)

    outgoing, image_sum, loss = call(
        own_kernel, "own", [((rows, width), bf16), ((rows, width), f32), ((1, rows), f32)],
        (flags, params), ids, mate_ids, image_emb, mate_a, mate_b, text, text_accum,
    )
    arrived = ahead(outgoing)

    passed_a, passed_b = call(
        relay_kernel, "relay", [((half, width), bf16), ((rows + PAD - half, width), bf16)],
        (flags,), loss, text, far,
    )
    near_a, near_b = across(passed_a), across(passed_b)
    late, image_sum, loss = call(
        far_kernel, "far", [((rows, width), f32), ((rows, width), f32), ((1, rows), f32)],
        (flags, params), ids, mate_ids, image_emb, mate_a, mate_b, far, image_sum, loss,
    )
    image_grad, loss = call(
        near_kernel, "near", [((rows, width), bf16), ((1, rows), f32)],
        (params,), ids, image_emb, near_a, near_b, image_sum, loss,
    )
    late, image_grad = lax.optimization_barrier((late, image_grad))
    text_grad = pl.pallas_call(
        add_kernel,
        out_shape=jax.ShapeDtypeStruct((rows, width), f32),
        in_specs=[VMEM, VMEM],
        out_specs=HBM,
        scratch_shapes=[pltpu.VMEM((rows, width), f32), pltpu.SemaphoreType.DMA((CHUNKS,))],
        compiler_params=pltpu.CompilerParams(vmem_limit_bytes=16 * 1024 * 1024),
        cost_estimate=pl.CostEstimate(flops=0, bytes_accessed=0, transcendentals=0),
        name="add",
    )(arrived, late)
    return (loss.reshape(rows), image_grad, text_grad)


def solution(mesh):
    in_specs = (P(AXES, None), P(AXES, None), P(AXES, None), P(AXES), P(), P())
    out_specs = (P(AXES), P(AXES, None), P(AXES, None))
    return jax.shard_map(body, mesh=mesh, in_specs=in_specs, out_specs=out_specs, check_vma=False)
```

```python
import jax
import jax.numpy as jnp
from jax import lax
from jax.experimental import pallas as pl
from jax.experimental.pallas import tpu as pltpu
from jax.sharding import PartitionSpec as P

SHIFTS = 2
AXES = ("dp", "group")
PAD = 8
CHUNKS = 4
VMEM = pl.BlockSpec(memory_space=pltpu.VMEM)
SMEM = pl.BlockSpec(memory_space=pltpu.SMEM)
HBM = pl.BlockSpec(memory_space=pltpu.HBM)


def dot(a, b, contract):
    return lax.dot_general(a, b, ((contract[:1], contract[1:]), ((), ())), preferred_element_type=jnp.float32)


def ids_of(text, at, rows):
    parts = text[at:, :rows].astype(jnp.float32).astype(jnp.int32)
    return parts[0:1] + parts[1:2] * 256 + parts[2:3] * 65536 + parts[3:4] * 16777216


def pair(images, texts, image_ids, text_ids, params):
    raw = dot(images, texts, (1, 1))
    rows = raw.shape[0]
    scale = jnp.exp(jnp.full((1, rows), params[0], jnp.float32))
    logits = scale * raw + params[1]
    same = jnp.broadcast_to(image_ids, (rows, rows)).T == text_ids
    margin = jnp.where(same, -logits, logits)
    tail = jnp.exp(-jnp.abs(margin))
    loss = jnp.maximum(margin, 0.0) + jnp.log1p(tail)
    sigmoid = jnp.where(margin >= 0, 1.0, tail) / (1.0 + tail)
    coef = jnp.where(same, -sigmoid, sigmoid) * scale
    return jnp.sum(loss.T, axis=0, keepdims=True), coef


def low(coef):
    return coef.astype(jnp.bfloat16)


def parts_kernel(ids, out):
    row = lax.broadcasted_iota(jnp.int32, out.shape, 0)
    spread = jnp.broadcast_to(ids[...], out.shape)
    parts = jnp.zeros(out.shape, jnp.int32)
    for k in range(4):
        parts = jnp.where(row == k, (spread >> (8 * k)) & 255, parts)
    out[...] = parts.astype(out.dtype)


def cast_kernel(parts, text, out, main, rest):
    rows, cut = text.shape[0], main.shape[0] - PAD
    out[:rows, :] = text[...].astype(out.dtype)
    out[rows:, :] = jnp.zeros((PAD, text.shape[1]), out.dtype)
    out[rows:, :rows] = parts[...].astype(out.dtype)
    main[:cut, :] = out[:cut, :]
    main[cut:, :] = out[rows:, :]
    rest[...] = out[cut:rows, :]


def add_kernel(arrived, late, out, staged, sems):
    rows = arrived.shape[0]
    step = rows // CHUNKS
    copies = []
    for k in range(CHUNKS):
        part = pl.ds(k * step, step)
        staged[part, :] = arrived[part, :].astype(staged.dtype) + late[part, :]
        copies.append(pltpu.make_async_copy(staged.at[part], out.at[part], sems.at[k]))
        copies[-1].start()
    for copy in copies:
        copy.wait()


def own_kernel(flags, params, ids, mate_ids, image, mate_a, mate_b, text, accum, out, image_sum, loss):
    rows = image.shape[0]
    own_loss, coef = pair(image[...], text[:rows, :], ids[...], ids[...], params)
    loss[...] = own_loss
    total = accum[...] + dot(low(coef.T), image[...], (1, 0))

    @pl.when(flags[0] == 0)
    def _():
        mate = jnp.concatenate([mate_a[...], mate_b[...]], axis=0)
        _, mate_coef = pair(mate, text[:rows, :], mate_ids[...], ids[...], params)
        out[...] = (total + dot(low(mate_coef.T), mate, (1, 0))).astype(out.dtype)

    @pl.when(flags[0] == 1)
    def _():
        out[...] = total.astype(out.dtype)

    image_sum[...] = dot(low(coef), text[:rows, :], (1, 0))


def relay_kernel(flags, token, text, far_most, far_main, far_turn, out_a, out_b, far):
    half, rest = out_a.shape[0], far_turn.shape[0]
    cut = far_main.shape[0] - PAD
    far[:cut, :] = far_most[:cut, :] + far_main[:cut, :]
    far[cut:cut + rest, :] = far_most[cut:cut + rest, :] + far_turn[...]
    far[cut + rest:, :] = far_most[cut + rest:, :] + far_main[cut:, :]

    def fill(source):
        out_a[...] = source[:half, :]
        out_b[...] = source[half:, :]

    pl.when(flags[0] == 0)(lambda: fill(text))
    pl.when(flags[0] == 1)(lambda: fill(far))


def far_kernel(flags, params, ids, mate_ids, image, mate_a, mate_b, far, image_in, loss_in, late, image_sum, loss):
    rows = image.shape[0]
    far_ids = ids_of(far, rows, rows)
    more, coef = pair(image[...], far[:rows, :], ids[...], far_ids, params)
    loss[...] = loss_in[...] + more
    image_sum[...] = image_in[...] + dot(low(coef), far[:rows, :], (1, 0))
    part = dot(low(coef.T), image[...], (1, 0))

    @pl.when(flags[0] == 0)
    def _():
        late[...] = part

    @pl.when(flags[0] == 1)
    def _():
        mate = jnp.concatenate([mate_a[...], mate_b[...]], axis=0)
        _, mate_coef = pair(mate, far[:rows, :], mate_ids[...], far_ids, params)
        late[...] = part + dot(low(mate_coef.T), mate, (1, 0))


def near_kernel(params, ids, image, near_a, near_b, image_in, loss_in, image_grad, loss):
    rows = image.shape[0]
    rest = rows - near_a.shape[0]
    near = jnp.concatenate([near_a[...], near_b[:rest, :]], axis=0)
    more, coef = pair(image[...], near, ids[...], ids_of(near_b, rest, rows), params)
    loss[...] = (loss_in[...] + more) * (1.0 / ((SHIFTS + 1) * rows))
    image_grad[...] = (image_in[...] + dot(low(coef), near, (1, 0))).astype(image_grad.dtype)


def call(kernel, name, outs, scalars, *operands, cost=0):
    return pl.pallas_call(
        kernel,
        out_shape=[jax.ShapeDtypeStruct(s, d) for s, d in outs],
        in_specs=[SMEM] * len(scalars) + [VMEM] * len(operands),
        out_specs=[VMEM] * len(outs),
        compiler_params=pltpu.CompilerParams(vmem_limit_bytes=16 * 1024 * 1024),
        cost_estimate=pl.CostEstimate(flops=0, bytes_accessed=cost, transcendentals=0),
        name=name,
    )(*scalars, *operands)


def body(image_emb, text_emb, text_accum, pair_ids, log_scale, bias):
    count = lax.axis_size(AXES)
    rows, width = image_emb.shape
    half = rows // 2
    f32, bf16 = jnp.float32, jnp.bfloat16
    flags = (lax.axis_index("group") % 2).astype(jnp.int32).reshape(1)
    params = jnp.concatenate([log_scale, bias])
    ids = pair_ids.reshape(1, rows)

    skip = [(i, (i + 2) % count) for i in range(count)]
    swap = [(i, i ^ 1) for i in range(count)]

    def ahead(value):
        return lax.ppermute(value, AXES, skip)

    def across(value):
        return lax.ppermute(value, AXES, swap)

    cut = rows - rows // 4
    turn = lax.axis_size("group")
    (parts,) = call(parts_kernel, "parts", [((PAD, rows), f32)], (), ids, cost=PAD << 20)
    text, text_main, text_rest = call(
        cast_kernel, "cast",
        [((rows + PAD, width), bf16), ((cut + PAD, width), bf16), ((rows - cut, width), bf16)],
        (), parts, text_emb,
    )
    far_most = lax.ppermute(text, AXES, skip[:-2])
    far_main = lax.ppermute(text_main, AXES, skip[-2:])
    to_turn = lax.ppermute(text_rest, AXES, [(count - 2, turn), (count - 1, turn + 1)])
    far_turn = lax.ppermute(to_turn, AXES, [(turn, 0), (turn + 1, 1)])

    image, text = lax.optimization_barrier((image_emb, text))
    mate_a, mate_b = across(image[:half]), across(image[half:])
    mate_ids = across(ids)

    outgoing, image_sum, loss = call(
        own_kernel, "own", [((rows, width), bf16), ((rows, width), f32), ((1, rows), f32)],
        (flags, params), ids, mate_ids, image_emb, mate_a, mate_b, text, text_accum,
    )
    arrived = ahead(outgoing)

    passed_a, passed_b, far = call(
        relay_kernel, "relay",
        [((half, width), bf16), ((rows + PAD - half, width), bf16), ((rows + PAD, width), bf16)],
        (flags,), loss, text, far_most, far_main, far_turn,
    )
    near_a, near_b = across(passed_a), across(passed_b)
    late, image_sum, loss = call(
        far_kernel, "far", [((rows, width), f32), ((rows, width), f32), ((1, rows), f32)],
        (flags, params), ids, mate_ids, image_emb, mate_a, mate_b, far, image_sum, loss,
    )
    image_grad, loss = call(
        near_kernel, "near", [((rows, width), bf16), ((1, rows), f32)],
        (params,), ids, image_emb, near_a, near_b, image_sum, loss,
    )
    late, image_grad = lax.optimization_barrier((late, image_grad))
    text_grad = pl.pallas_call(
        add_kernel,
        out_shape=jax.ShapeDtypeStruct((rows, width), f32),
        in_specs=[VMEM, VMEM],
        out_specs=HBM,
        scratch_shapes=[pltpu.VMEM((rows, width), f32), pltpu.SemaphoreType.DMA((CHUNKS,))],
        compiler_params=pltpu.CompilerParams(vmem_limit_bytes=16 * 1024 * 1024),
        cost_estimate=pl.CostEstimate(flops=0, bytes_accessed=0, transcendentals=0),
        name="add",
    )(arrived, late)
    return (loss.reshape(rows), image_grad, text_grad)


def solution(mesh):
    in_specs = (P(AXES, None), P(AXES, None), P(AXES, None), P(AXES), P(), P())
    out_specs = (P(AXES), P(AXES, None), P(AXES, None))
    return jax.shard_map(body, mesh=mesh, in_specs=in_specs, out_specs=out_specs, check_vma=False)
```

```python
import functools

import jax
import jax.numpy as jnp
from jax import lax
from jax.experimental import pallas as pl
from jax.experimental.pallas import tpu as pltpu
from jax.sharding import PartitionSpec as P

SHIFTS = 2
AXES = ("dp", "group")
PAD = 8
CHUNKS = 4
VMEM = pl.BlockSpec(memory_space=pltpu.VMEM)
SMEM = pl.BlockSpec(memory_space=pltpu.SMEM)
HBM = pl.BlockSpec(memory_space=pltpu.HBM)


def dot(a, b, contract):
    return lax.dot_general(a, b, ((contract[:1], contract[1:]), ((), ())), preferred_element_type=jnp.float32)


def ids_of(text, at, rows):
    parts = text[at:, :rows].astype(jnp.float32).astype(jnp.int32)
    return parts[0:1] + parts[1:2] * 256 + parts[2:3] * 65536 + parts[3:4] * 16777216


def pair(images, texts, image_ids, text_ids, params):
    raw = dot(images, texts, (1, 1))
    rows = raw.shape[0]
    scale = jnp.exp(jnp.full((1, rows), params[0], jnp.float32))
    logits = scale * raw + params[1]
    same = jnp.broadcast_to(image_ids, (rows, rows)).T == text_ids
    margin = jnp.where(same, -logits, logits)
    tail = jnp.exp(-jnp.abs(margin))
    loss = jnp.maximum(margin, 0.0) + jnp.log1p(tail)
    sigmoid = jnp.where(margin >= 0, 1.0, tail) / (1.0 + tail)
    coef = jnp.where(same, -sigmoid, sigmoid) * scale
    return jnp.sum(loss.T, axis=0, keepdims=True), coef


def low(coef):
    return coef.astype(jnp.bfloat16)


def cast_kernel(ids, text, out, staged, ids_in, sems, ids_sem):
    rows, width = text.shape
    step = rows // CHUNKS
    ids_copy = pltpu.make_async_copy(ids, ids_in, ids_sem)
    copies = [
        pltpu.make_async_copy(text.at[pl.ds(k * step, step)], staged.at[pl.ds(k * step, step)], sems.at[k])
        for k in range(CHUNKS)
    ]
    for copy in copies:
        copy.start()
    ids_copy.start()
    out[rows:, :] = jnp.zeros((PAD, width), out.dtype)
    for k, copy in enumerate(copies):
        copy.wait()
        out[k * step:(k + 1) * step, :] = staged[k * step:(k + 1) * step, :].astype(out.dtype)
    ids_copy.wait()
    row = lax.broadcasted_iota(jnp.int32, (PAD, rows), 0)
    spread = jnp.broadcast_to(ids_in[...], (PAD, rows))
    parts = jnp.zeros((PAD, rows), jnp.int32)
    for k in range(4):
        parts = jnp.where(row == k, (spread >> (8 * k)) & 255, parts)
    out[rows:, :rows] = parts.astype(jnp.float32).astype(out.dtype)


def add_kernel(start, chunks, arrived, late, *refs):
    out, staged, sems = refs[-3:]
    step = arrived.shape[0] // chunks
    copies = []
    for k in range(chunks):
        here, there = pl.ds(k * step, step), pl.ds(start + k * step, step)
        staged[here, :] = arrived[here, :].astype(staged.dtype) + late[there, :]
        copies.append(pltpu.make_async_copy(staged.at[here], out.at[there], sems.at[k]))
        copies[-1].start()
    for copy in copies:
        copy.wait()


def own_kernel(flags, params, ids, mate_ids, image, mate_a, mate_b, text, accum, out_a, out_b, image_sum, loss):
    rows = image.shape[0]
    own_loss, coef = pair(image[...], text[:rows, :], ids[...], ids[...], params)
    loss[...] = own_loss
    total = accum[...] + dot(low(coef.T), image[...], (1, 0))
    cut = out_a.shape[0]

    def give(value):
        out_a[...] = value[:cut, :].astype(out_a.dtype)
        out_b[...] = value[cut:, :].astype(out_b.dtype)

    @pl.when(flags[0] == 0)
    def _():
        mate = jnp.concatenate([mate_a[...], mate_b[...]], axis=0)
        _, mate_coef = pair(mate, text[:rows, :], mate_ids[...], ids[...], params)
        give(total + dot(low(mate_coef.T), mate, (1, 0)))

    @pl.when(flags[0] == 1)
    def _():
        give(total)

    image_sum[...] = dot(low(coef), text[:rows, :], (1, 0))


def relay_kernel(flags, token, text, far, out_a, out_b):
    cut = out_a.shape[0]

    def fill(source):
        out_a[...] = source[:cut, :]
        out_b[...] = source[cut:, :]

    pl.when(flags[0] == 0)(lambda: fill(text))
    pl.when(flags[0] == 1)(lambda: fill(far))


def far_kernel(flags, params, ids, mate_ids, image, mate_a, mate_b, far, image_in, loss_in, late, image_sum, loss):
    rows = image.shape[0]
    far_ids = ids_of(far, rows, rows)
    more, coef = pair(image[...], far[:rows, :], ids[...], far_ids, params)
    loss[...] = loss_in[...] + more
    image_sum[...] = image_in[...] + dot(low(coef), far[:rows, :], (1, 0))
    part = dot(low(coef.T), image[...], (1, 0))

    @pl.when(flags[0] == 0)
    def _():
        late[...] = part

    @pl.when(flags[0] == 1)
    def _():
        mate = jnp.concatenate([mate_a[...], mate_b[...]], axis=0)
        _, mate_coef = pair(mate, far[:rows, :], mate_ids[...], far_ids, params)
        late[...] = part + dot(low(mate_coef.T), mate, (1, 0))


def near_kernel(params, ids, image, near_a, near_b, image_in, loss_in, image_grad, loss):
    rows = image.shape[0]
    rest = rows - near_a.shape[0]
    near = jnp.concatenate([near_a[...], near_b[:rest, :]], axis=0)
    more, coef = pair(image[...], near, ids[...], ids_of(near_b, rest, rows), params)
    loss[...] = (loss_in[...] + more) * (1.0 / ((SHIFTS + 1) * rows))
    image_grad[...] = (image_in[...] + dot(low(coef), near, (1, 0))).astype(image_grad.dtype)


def call(kernel, name, outs, scalars, *operands):
    return pl.pallas_call(
        kernel,
        out_shape=[jax.ShapeDtypeStruct(s, d) for s, d in outs],
        in_specs=[SMEM] * len(scalars) + [VMEM] * len(operands),
        out_specs=[VMEM] * len(outs),
        compiler_params=pltpu.CompilerParams(vmem_limit_bytes=16 * 1024 * 1024),
        cost_estimate=pl.CostEstimate(flops=0, bytes_accessed=0, transcendentals=0),
        name=name,
    )(*scalars, *operands)


def add_part(name, start, chunks, arrived, late, *before):
    return pl.pallas_call(
        functools.partial(add_kernel, start, chunks),
        out_shape=jax.ShapeDtypeStruct(late.shape, late.dtype),
        in_specs=[VMEM, VMEM] + [HBM] * len(before),
        out_specs=HBM,
        scratch_shapes=[pltpu.VMEM(arrived.shape, late.dtype), pltpu.SemaphoreType.DMA((chunks,))],
        input_output_aliases={2: 0} if before else {},
        compiler_params=pltpu.CompilerParams(vmem_limit_bytes=16 * 1024 * 1024),
        cost_estimate=pl.CostEstimate(flops=0, bytes_accessed=0, transcendentals=0),
        name=name,
    )(arrived, late, *before)


def body(image_emb, text_emb, text_accum, pair_ids, log_scale, bias):
    count = lax.axis_size(AXES)
    rows, width = image_emb.shape
    half = rows // 2
    f32, bf16 = jnp.float32, jnp.bfloat16
    flags = (lax.axis_index("group") % 2).astype(jnp.int32).reshape(1)
    params = jnp.concatenate([log_scale, bias])
    ids = pair_ids.reshape(1, rows)

    skip = [(i, (i + 2) % count) for i in range(count)]
    swap = [(i, i ^ 1) for i in range(count)]

    def ahead(value):
        return lax.ppermute(value, AXES, skip)

    def across(value):
        return lax.ppermute(value, AXES, swap)

    text = pl.pallas_call(
        cast_kernel,
        out_shape=jax.ShapeDtypeStruct((rows + PAD, width), bf16),
        in_specs=[HBM, HBM],
        out_specs=VMEM,
        scratch_shapes=[
            pltpu.VMEM((rows, width), f32),
            pltpu.VMEM((1, rows), jnp.int32),
            pltpu.SemaphoreType.DMA((CHUNKS,)),
            pltpu.SemaphoreType.DMA,
        ],
        compiler_params=pltpu.CompilerParams(vmem_limit_bytes=63 * 1024 * 1024),
        cost_estimate=pl.CostEstimate(flops=0, bytes_accessed=0, transcendentals=0),
        name="cast",
    )(ids, text_emb)
    far = ahead(text)

    image, text = lax.optimization_barrier((image_emb, text))
    image_emb = image
    mate_a, mate_b = across(image[:half]), across(image[half:])
    mate_ids = across(ids)

    cut = rows - rows // 4
    out_a, out_b, image_sum, loss = call(
        own_kernel, "own", [((cut, width), bf16), ((rows - cut, width), bf16), ((rows, width), f32), ((1, rows), f32)],
        (flags, params), ids, mate_ids, image_emb, mate_a, mate_b, text, text_accum,
    )
    arrived_a, arrived_b = ahead(out_a), ahead(out_b)

    passed_a, passed_b = call(
        relay_kernel, "relay", [((half, width), bf16), ((rows + PAD - half, width), bf16)],
        (flags,), loss, text, far,
    )
    near_a, near_b = across(passed_a), across(passed_b)
    late, image_sum, loss = call(
        far_kernel, "far", [((rows, width), f32), ((rows, width), f32), ((1, rows), f32)],
        (flags, params), ids, mate_ids, image_emb, mate_a, mate_b, far, image_sum, loss,
    )
    image_grad, loss = call(
        near_kernel, "near", [((rows, width), bf16), ((1, rows), f32)],
        (params,), ids, image_emb, near_a, near_b, image_sum, loss,
    )
    late, image_grad = lax.optimization_barrier((late, image_grad))
    text_grad = add_part("add_a", 0, CHUNKS, arrived_a, late)
    text_grad = add_part("add_b", cut, 2, arrived_b, late, text_grad)
    return (loss.reshape(rows), image_grad, text_grad)


def solution(mesh):
    in_specs = (P(AXES, None), P(AXES, None), P(AXES, None), P(AXES), P(), P())
    out_specs = (P(AXES), P(AXES, None), P(AXES, None))
    return jax.shard_map(body, mesh=mesh, in_specs=in_specs, out_specs=out_specs, check_vma=False)
```

```python
import functools

import jax
import jax.numpy as jnp
from jax import lax
from jax.experimental import pallas as pl
from jax.experimental.pallas import tpu as pltpu
from jax.sharding import PartitionSpec as P

SHIFTS = 2
AXES = ("dp", "group")
PAD = 8
CHUNKS = 4
VMEM = pl.BlockSpec(memory_space=pltpu.VMEM)
SMEM = pl.BlockSpec(memory_space=pltpu.SMEM)
HBM = pl.BlockSpec(memory_space=pltpu.HBM)


def dot(a, b, contract):
    return lax.dot_general(a, b, ((contract[:1], contract[1:]), ((), ())), preferred_element_type=jnp.float32)


def ids_of(text, at, rows):
    parts = text[at:, :rows].astype(jnp.float32).astype(jnp.int32)
    return parts[0:1] + parts[1:2] * 256 + parts[2:3] * 65536 + parts[3:4] * 16777216


def pair(images, texts, image_ids, text_ids, params):
    raw = dot(images, texts, (1, 1))
    rows = raw.shape[0]
    scale = jnp.exp(jnp.full((1, rows), params[0], jnp.float32))
    logits = scale * raw + params[1]
    same = jnp.broadcast_to(image_ids, (rows, rows)).T == text_ids
    margin = jnp.where(same, -logits, logits)
    tail = jnp.exp(-jnp.abs(margin))
    loss = jnp.maximum(margin, 0.0) + jnp.log1p(tail)
    sigmoid = jnp.where(margin >= 0, 1.0, tail) / (1.0 + tail)
    coef = jnp.where(same, -sigmoid, sigmoid) * scale
    return jnp.sum(loss.T, axis=0, keepdims=True), coef


def low(coef):
    return coef.astype(jnp.bfloat16)


def cast_kernel(ids, text, out, staged, ids_in, sems, ids_sem):
    rows, width = text.shape
    step = rows // CHUNKS
    ids_copy = pltpu.make_async_copy(ids, ids_in, ids_sem)
    copies = [
        pltpu.make_async_copy(text.at[pl.ds(k * step, step)], staged.at[pl.ds(k * step, step)], sems.at[k])
        for k in range(CHUNKS)
    ]
    for copy in copies:
        copy.start()
    ids_copy.start()
    out[rows:, :] = jnp.zeros((PAD, width), out.dtype)
    for k, copy in enumerate(copies):
        copy.wait()
        out[k * step:(k + 1) * step, :] = staged[k * step:(k + 1) * step, :].astype(out.dtype)
    ids_copy.wait()
    row = lax.broadcasted_iota(jnp.int32, (PAD, rows), 0)
    spread = jnp.broadcast_to(ids_in[...], (PAD, rows))
    parts = jnp.zeros((PAD, rows), jnp.int32)
    for k in range(4):
        parts = jnp.where(row == k, (spread >> (8 * k)) & 255, parts)
    out[rows:, :rows] = parts.astype(jnp.float32).astype(out.dtype)


def add_kernel(start, chunks, arrived, late, *refs):
    out, staged, sems = refs[-3:]
    step = arrived.shape[0] // chunks
    copies = []
    for k in range(chunks):
        here, there = pl.ds(k * step, step), pl.ds(start + k * step, step)
        staged[here, :] = arrived[here, :].astype(staged.dtype) + late[there, :]
        copies.append(pltpu.make_async_copy(staged.at[here], out.at[there], sems.at[k]))
        copies[-1].start()
    for copy in copies:
        copy.wait()


def own_kernel(flags, params, ids, mate_ids, image, mate_a, mate_b, text, accum, out_a, out_b, image_sum, loss):
    rows = image.shape[0]
    own_loss, coef = pair(image[...], text[:rows, :], ids[...], ids[...], params)
    loss[...] = own_loss
    total = accum[...] + dot(low(coef.T), image[...], (1, 0))
    cut = out_a.shape[0]

    def give(value):
        out_a[...] = value[:cut, :].astype(out_a.dtype)
        out_b[...] = value[cut:, :].astype(out_b.dtype)

    @pl.when(flags[0] == 0)
    def _():
        mate = jnp.concatenate([mate_a[...], mate_b[...]], axis=0)
        _, mate_coef = pair(mate, text[:rows, :], mate_ids[...], ids[...], params)
        give(total + dot(low(mate_coef.T), mate, (1, 0)))

    @pl.when(flags[0] == 1)
    def _():
        give(total)

    image_sum[...] = dot(low(coef), text[:rows, :], (1, 0))


def relay_kernel(flags, token, text, far, out_a, out_b):
    cut = out_a.shape[0]

    def fill(source):
        out_a[...] = source[:cut, :]
        out_b[...] = source[cut:, :]

    pl.when(flags[0] == 0)(lambda: fill(text))
    pl.when(flags[0] == 1)(lambda: fill(far))


def far_kernel(flags, params, ids, mate_ids, image, mate_a, mate_b, far, image_in, loss_in, late, image_sum, loss):
    rows = image.shape[0]
    far_ids = ids_of(far, rows, rows)
    more, coef = pair(image[...], far[:rows, :], ids[...], far_ids, params)
    loss[...] = loss_in[...] + more
    image_sum[...] = image_in[...] + dot(low(coef), far[:rows, :], (1, 0))
    part = dot(low(coef.T), image[...], (1, 0))

    @pl.when(flags[0] == 0)
    def _():
        late[...] = part

    @pl.when(flags[0] == 1)
    def _():
        mate = jnp.concatenate([mate_a[...], mate_b[...]], axis=0)
        _, mate_coef = pair(mate, far[:rows, :], mate_ids[...], far_ids, params)
        late[...] = part + dot(low(mate_coef.T), mate, (1, 0))


def near_kernel(params, ids, image, near_a, near_b, image_in, loss_in, image_grad, loss):
    rows = image.shape[0]
    rest = rows - near_a.shape[0]
    near = jnp.concatenate([near_a[...], near_b[:rest, :]], axis=0)
    more, coef = pair(image[...], near, ids[...], ids_of(near_b, rest, rows), params)
    loss[...] = (loss_in[...] + more) * (1.0 / ((SHIFTS + 1) * rows))
    image_grad[...] = (image_in[...] + dot(low(coef), near, (1, 0))).astype(image_grad.dtype)


def call(kernel, name, outs, scalars, *operands):
    return pl.pallas_call(
        kernel,
        out_shape=[jax.ShapeDtypeStruct(s, d) for s, d in outs],
        in_specs=[SMEM] * len(scalars) + [VMEM] * len(operands),
        out_specs=[VMEM] * len(outs),
        compiler_params=pltpu.CompilerParams(vmem_limit_bytes=16 * 1024 * 1024),
        cost_estimate=pl.CostEstimate(flops=0, bytes_accessed=0, transcendentals=0),
        name=name,
    )(*scalars, *operands)


def add_part(name, start, chunks, arrived, late, *before):
    return pl.pallas_call(
        functools.partial(add_kernel, start, chunks),
        out_shape=jax.ShapeDtypeStruct(late.shape, late.dtype),
        in_specs=[VMEM, VMEM] + [HBM] * len(before),
        out_specs=HBM,
        scratch_shapes=[pltpu.VMEM(arrived.shape, late.dtype), pltpu.SemaphoreType.DMA((chunks,))],
        input_output_aliases={2: 0} if before else {},
        compiler_params=pltpu.CompilerParams(vmem_limit_bytes=16 * 1024 * 1024),
        cost_estimate=pl.CostEstimate(flops=0, bytes_accessed=0, transcendentals=0),
        name=name,
    )(arrived, late, *before)


def body(image_emb, text_emb, text_accum, pair_ids, log_scale, bias):
    count = lax.axis_size(AXES)
    rows, width = image_emb.shape
    half = rows // 2
    f32, bf16 = jnp.float32, jnp.bfloat16
    flags = (lax.axis_index("group") % 2).astype(jnp.int32).reshape(1)
    params = jnp.concatenate([log_scale, bias])
    ids = pair_ids.reshape(1, rows)

    skip = [(i, (i + 2) % count) for i in range(count)]
    swap = [(i, i ^ 1) for i in range(count)]

    def ahead(value):
        return lax.ppermute(value, AXES, skip)

    def across(value):
        return lax.ppermute(value, AXES, swap)

    text = pl.pallas_call(
        cast_kernel,
        out_shape=jax.ShapeDtypeStruct((rows + PAD, width), bf16),
        in_specs=[HBM, HBM],
        out_specs=VMEM,
        scratch_shapes=[
            pltpu.VMEM((rows, width), f32),
            pltpu.VMEM((1, rows), jnp.int32),
            pltpu.SemaphoreType.DMA((CHUNKS,)),
            pltpu.SemaphoreType.DMA,
        ],
        compiler_params=pltpu.CompilerParams(vmem_limit_bytes=16 * 1024 * 1024),
        cost_estimate=pl.CostEstimate(flops=0, bytes_accessed=0, transcendentals=0),
        name="cast",
    )(*(pltpu.with_memory_space_constraint(value, pltpu.HBM) for value in (ids, text_emb)))
    far = ahead(text)

    image, text = lax.optimization_barrier((image_emb, text))
    image_emb = image
    mate_a, mate_b = across(image[:half]), across(image[half:])
    mate_ids = across(ids)

    cut = rows - rows // 4
    out_a, out_b, image_sum, loss = call(
        own_kernel, "own", [((cut, width), bf16), ((rows - cut, width), bf16), ((rows, width), f32), ((1, rows), f32)],
        (flags, params), ids, mate_ids, image_emb, mate_a, mate_b, text, text_accum,
    )
    arrived_a, arrived_b = ahead(out_a), ahead(out_b)

    passed_a, passed_b = call(
        relay_kernel, "relay", [((half, width), bf16), ((rows + PAD - half, width), bf16)],
        (flags,), loss, text, far,
    )
    near_a, near_b = across(passed_a), across(passed_b)
    late, image_sum, loss = call(
        far_kernel, "far", [((rows, width), f32), ((rows, width), f32), ((1, rows), f32)],
        (flags, params), ids, mate_ids, image_emb, mate_a, mate_b, far, image_sum, loss,
    )
    image_grad, loss = call(
        near_kernel, "near", [((rows, width), bf16), ((1, rows), f32)],
        (params,), ids, image_emb, near_a, near_b, image_sum, loss,
    )
    late, image_grad = lax.optimization_barrier((late, image_grad))
    text_grad = add_part("add_a", 0, CHUNKS, arrived_a, late)
    text_grad = add_part("add_b", cut, 2, arrived_b, late, text_grad)
    return (loss.reshape(rows), image_grad, text_grad)


def solution(mesh):
    in_specs = (P(AXES, None), P(AXES, None), P(AXES, None), P(AXES), P(), P())
    out_specs = (P(AXES), P(AXES, None), P(AXES, None))
    return jax.shard_map(body, mesh=mesh, in_specs=in_specs, out_specs=out_specs, check_vma=False)
```

```python
import functools

import jax
import jax.numpy as jnp
from jax import lax
from jax.experimental import pallas as pl
from jax.experimental.pallas import tpu as pltpu
from jax.sharding import PartitionSpec as P

SHIFTS = 2
AXES = ("dp", "group")
PAD = 8
CHUNKS = 4
VMEM = pl.BlockSpec(memory_space=pltpu.VMEM)
SMEM = pl.BlockSpec(memory_space=pltpu.SMEM)
HBM = pl.BlockSpec(memory_space=pltpu.HBM)


def dot(a, b, contract):
    return lax.dot_general(a, b, ((contract[:1], contract[1:]), ((), ())), preferred_element_type=jnp.float32)


def ids_of(text, at, rows):
    parts = text[at:, :rows].astype(jnp.float32).astype(jnp.int32)
    return parts[0:1] + parts[1:2] * 256 + parts[2:3] * 65536 + parts[3:4] * 16777216


def pair(images, texts, image_ids, text_ids, params):
    raw = dot(images, texts, (1, 1))
    rows = raw.shape[0]
    scale = jnp.exp(jnp.full((1, rows), params[0], jnp.float32))
    logits = scale * raw + params[1]
    same = jnp.broadcast_to(image_ids, (rows, rows)).T == text_ids
    margin = jnp.where(same, -logits, logits)
    tail = jnp.exp(-jnp.abs(margin))
    loss = jnp.maximum(margin, 0.0) + jnp.log1p(tail)
    sigmoid = jnp.where(margin >= 0, 1.0, tail) / (1.0 + tail)
    coef = jnp.where(same, -sigmoid, sigmoid) * scale
    return jnp.sum(loss.T, axis=0, keepdims=True), coef


def low(coef):
    return coef.astype(jnp.bfloat16)


def cast_kernel(ids, text, out, staged, ids_in, sems, ids_sem):
    rows, width = text.shape
    step = rows // CHUNKS
    ids_copy = pltpu.make_async_copy(ids, ids_in, ids_sem)
    copies = [
        pltpu.make_async_copy(text.at[pl.ds(k * step, step)], staged.at[pl.ds(k * step, step)], sems.at[k])
        for k in range(CHUNKS)
    ]
    for copy in copies:
        copy.start()
    ids_copy.start()
    out[rows:, :] = jnp.zeros((PAD, width), out.dtype)
    for k, copy in enumerate(copies):
        copy.wait()
        out[k * step:(k + 1) * step, :] = staged[k * step:(k + 1) * step, :].astype(out.dtype)
    ids_copy.wait()
    row = lax.broadcasted_iota(jnp.int32, (PAD, rows), 0)
    spread = jnp.broadcast_to(ids_in[...], (PAD, rows))
    parts = jnp.zeros((PAD, rows), jnp.int32)
    for k in range(4):
        parts = jnp.where(row == k, (spread >> (8 * k)) & 255, parts)
    out[rows:, :rows] = parts.astype(jnp.float32).astype(out.dtype)


def add_kernel(start, chunks, count, late, *refs):
    arrived, (out, staged, sems) = refs[:count], refs[-3:]
    step = staged.shape[0] // chunks
    copies = []
    for k in range(chunks):
        here, there = pl.ds(k * step, step), pl.ds(start + k * step, step)
        staged[here, :] = sum((part[here, :].astype(staged.dtype) for part in arrived), late[there, :])
        copies.append(pltpu.make_async_copy(staged.at[here], out.at[there], sems.at[k]))
        copies[-1].start()
    for copy in copies:
        copy.wait()


def own_kernel(flags, params, ids, mate_ids, image, mate_a, mate_b, text, accum, out_a, out_b, image_sum, loss):
    rows = image.shape[0]
    own_loss, coef = pair(image[...], text[:rows, :], ids[...], ids[...], params)
    loss[...] = own_loss
    total = accum[...] + dot(low(coef.T), image[...], (1, 0))
    cut = out_a.shape[0]

    def give(value):
        out_a[...] = value[:cut, :].astype(out_a.dtype)
        out_b[...] = value[cut:, :].astype(out_b.dtype)

    @pl.when(flags[0] == 0)
    def _():
        mate = jnp.concatenate([mate_a[...], mate_b[...]], axis=0)
        _, mate_coef = pair(mate, text[:rows, :], mate_ids[...], ids[...], params)
        give(total + dot(low(mate_coef.T), mate, (1, 0)))

    @pl.when(flags[0] == 1)
    def _():
        give(total)

    image_sum[...] = dot(low(coef), text[:rows, :], (1, 0))


def relay_kernel(flags, token, text, far, out_a, out_b):
    cut = out_a.shape[0]

    def fill(source):
        out_a[...] = source[:cut, :]
        out_b[...] = source[cut:, :]

    pl.when(flags[0] == 0)(lambda: fill(text))
    pl.when(flags[0] == 1)(lambda: fill(far))


def far_kernel(flags, params, ids, mate_ids, image, mate_a, mate_b, far, image_in, loss_in, late, image_sum, loss):
    rows = image.shape[0]
    far_ids = ids_of(far, rows, rows)
    more, coef = pair(image[...], far[:rows, :], ids[...], far_ids, params)
    loss[...] = loss_in[...] + more
    image_sum[...] = image_in[...] + dot(low(coef), far[:rows, :], (1, 0))
    part = dot(low(coef.T), image[...], (1, 0))

    @pl.when(flags[0] == 0)
    def _():
        late[...] = part

    @pl.when(flags[0] == 1)
    def _():
        mate = jnp.concatenate([mate_a[...], mate_b[...]], axis=0)
        _, mate_coef = pair(mate, far[:rows, :], mate_ids[...], far_ids, params)
        late[...] = part + dot(low(mate_coef.T), mate, (1, 0))


def near_kernel(params, ids, image, near_a, near_b, image_in, loss_in, image_grad, loss):
    rows = image.shape[0]
    rest = rows - near_a.shape[0]
    near = jnp.concatenate([near_a[...], near_b[:rest, :]], axis=0)
    more, coef = pair(image[...], near, ids[...], ids_of(near_b, rest, rows), params)
    loss[...] = (loss_in[...] + more) * (1.0 / ((SHIFTS + 1) * rows))
    image_grad[...] = (image_in[...] + dot(low(coef), near, (1, 0))).astype(image_grad.dtype)


def call(kernel, name, outs, scalars, *operands):
    return pl.pallas_call(
        kernel,
        out_shape=[jax.ShapeDtypeStruct(s, d) for s, d in outs],
        in_specs=[SMEM] * len(scalars) + [VMEM] * len(operands),
        out_specs=[VMEM] * len(outs),
        compiler_params=pltpu.CompilerParams(vmem_limit_bytes=16 * 1024 * 1024),
        cost_estimate=pl.CostEstimate(flops=0, bytes_accessed=0, transcendentals=0),
        name=name,
    )(*scalars, *operands)


def add_part(name, start, chunks, late, arrived, *before):
    return pl.pallas_call(
        functools.partial(add_kernel, start, chunks, len(arrived)),
        out_shape=jax.ShapeDtypeStruct(late.shape, late.dtype),
        in_specs=[VMEM] * (1 + len(arrived)) + [HBM] * len(before),
        out_specs=HBM,
        scratch_shapes=[pltpu.VMEM(arrived[0].shape, late.dtype), pltpu.SemaphoreType.DMA((chunks,))],
        input_output_aliases={1 + len(arrived): 0} if before else {},
        compiler_params=pltpu.CompilerParams(vmem_limit_bytes=16 * 1024 * 1024),
        cost_estimate=pl.CostEstimate(flops=0, bytes_accessed=0, transcendentals=0),
        name=name,
    )(late, *arrived, *before)


def body(image_emb, text_emb, text_accum, pair_ids, log_scale, bias):
    count = lax.axis_size(AXES)
    rows, width = image_emb.shape
    half = rows // 2
    f32, bf16 = jnp.float32, jnp.bfloat16
    flags = (lax.axis_index("group") % 2).astype(jnp.int32).reshape(1)
    params = jnp.concatenate([log_scale, bias])
    ids = pair_ids.reshape(1, rows)

    skip = [(i, (i + 2) % count) for i in range(count)]
    swap = [(i, i ^ 1) for i in range(count)]

    def ahead(value):
        return lax.ppermute(value, AXES, skip)

    def across(value):
        return lax.ppermute(value, AXES, swap)

    text = pl.pallas_call(
        cast_kernel,
        out_shape=jax.ShapeDtypeStruct((rows + PAD, width), bf16),
        in_specs=[HBM, HBM],
        out_specs=VMEM,
        scratch_shapes=[
            pltpu.VMEM((rows, width), f32),
            pltpu.VMEM((1, rows), jnp.int32),
            pltpu.SemaphoreType.DMA((CHUNKS,)),
            pltpu.SemaphoreType.DMA,
        ],
        compiler_params=pltpu.CompilerParams(vmem_limit_bytes=16 * 1024 * 1024),
        cost_estimate=pl.CostEstimate(flops=0, bytes_accessed=0, transcendentals=0),
        name="cast",
    )(*(pltpu.with_memory_space_constraint(value, pltpu.HBM) for value in (ids, text_emb)))
    far = ahead(text)

    image, text = lax.optimization_barrier((image_emb, text))
    image_emb = image
    mate_a, mate_b = across(image[:half]), across(image[half:])
    mate_ids = across(ids)

    cut = rows - rows * 3 // 16
    out_a, out_b, image_sum, loss = call(
        own_kernel, "own", [((cut, width), bf16), ((rows - cut, width), bf16), ((rows, width), f32), ((1, rows), f32)],
        (flags, params), ids, mate_ids, image_emb, mate_a, mate_b, text, text_accum,
    )
    turn = count - 4
    arrived_a = ahead(out_a)
    to_turn = lax.ppermute(out_b, AXES, [(count - 2, turn), (count - 1, turn + 1)])
    turned = lax.ppermute(to_turn, AXES, [(turn, 0), (turn + 1, 1)])
    arrived_b = lax.ppermute(out_b, AXES, skip[:-2])

    passed_a, passed_b = call(
        relay_kernel, "relay", [((half, width), bf16), ((rows + PAD - half, width), bf16)],
        (flags,), lax.optimization_barrier((loss, to_turn))[0], text, far,
    )
    near_a, near_b = across(passed_a), across(passed_b)
    late, image_sum, loss = call(
        far_kernel, "far", [((rows, width), f32), ((rows, width), f32), ((1, rows), f32)],
        (flags, params), ids, mate_ids, image_emb, mate_a, mate_b, far, image_sum, loss,
    )
    image_grad, loss = call(
        near_kernel, "near", [((rows, width), bf16), ((1, rows), f32)],
        (params,), ids, image_emb, near_a, near_b, image_sum, loss,
    )
    late, image_grad = lax.optimization_barrier((late, image_grad))
    text_grad = add_part("add_a", 0, 2, late, (arrived_a,))
    text_grad = add_part("add_b", cut, 1, late, (arrived_b, turned), text_grad)
    return (loss.reshape(rows), image_grad, text_grad)


def solution(mesh):
    in_specs = (P(AXES, None), P(AXES, None), P(AXES, None), P(AXES), P(), P())
    out_specs = (P(AXES), P(AXES, None), P(AXES, None))
    return jax.shard_map(body, mesh=mesh, in_specs=in_specs, out_specs=out_specs, check_vma=False)
```

```python
import functools

import jax
import jax.numpy as jnp
from jax import lax
from jax.experimental import pallas as pl
from jax.experimental.pallas import tpu as pltpu
from jax.sharding import PartitionSpec as P

SHIFTS = 2
AXES = ("dp", "group")
PAD = 8
CHUNKS = 4
VMEM = pl.BlockSpec(memory_space=pltpu.VMEM)
SMEM = pl.BlockSpec(memory_space=pltpu.SMEM)
HBM = pl.BlockSpec(memory_space=pltpu.HBM)


def dot(a, b, contract):
    return lax.dot_general(a, b, ((contract[:1], contract[1:]), ((), ())), preferred_element_type=jnp.float32)


def ids_of(text, at, rows):
    parts = text[at:, :rows].astype(jnp.float32).astype(jnp.int32)
    return parts[0:1] + parts[1:2] * 256 + parts[2:3] * 65536 + parts[3:4] * 16777216


def pair(images, texts, image_ids, text_ids, params):
    raw = dot(images, texts, (1, 1))
    rows = raw.shape[0]
    scale = jnp.exp(jnp.full((1, rows), params[0], jnp.float32))
    logits = scale * raw + params[1]
    same = jnp.broadcast_to(image_ids, (rows, rows)).T == text_ids
    margin = jnp.where(same, -logits, logits)
    tail = jnp.exp(-jnp.abs(margin))
    loss = jnp.maximum(margin, 0.0) + jnp.log1p(tail)
    sigmoid = jnp.where(margin >= 0, 1.0, tail) / (1.0 + tail)
    coef = jnp.where(same, -sigmoid, sigmoid) * scale
    return jnp.sum(loss.T, axis=0, keepdims=True), coef


def low(coef):
    return coef.astype(jnp.bfloat16)


def cast_kernel(ids, text, out, staged, ids_in, sems, ids_sem):
    rows, width = text.shape
    step = rows // CHUNKS
    ids_copy = pltpu.make_async_copy(ids, ids_in, ids_sem)
    copies = [
        pltpu.make_async_copy(text.at[pl.ds(k * step, step)], staged.at[pl.ds(k * step, step)], sems.at[k])
        for k in range(CHUNKS)
    ]
    for copy in copies:
        copy.start()
    ids_copy.start()
    out[rows:, :] = jnp.zeros((PAD, width), out.dtype)
    for k, copy in enumerate(copies):
        copy.wait()
        out[k * step:(k + 1) * step, :] = staged[k * step:(k + 1) * step, :].astype(out.dtype)
    ids_copy.wait()
    row = lax.broadcasted_iota(jnp.int32, (PAD, rows), 0)
    spread = jnp.broadcast_to(ids_in[...], (PAD, rows))
    parts = jnp.zeros((PAD, rows), jnp.int32)
    for k in range(4):
        parts = jnp.where(row == k, (spread >> (8 * k)) & 255, parts)
    out[rows:, :rows] = parts.astype(jnp.float32).astype(out.dtype)


def add_kernel(start, chunks, count, late, *refs):
    arrived, (out, staged, sems) = refs[:count], refs[-3:]
    step = staged.shape[0] // chunks
    copies = []
    for k in range(chunks):
        here, there = pl.ds(k * step, step), pl.ds(start + k * step, step)
        staged[here, :] = sum((part[here, :].astype(staged.dtype) for part in arrived), late[there, :])
        copies.append(pltpu.make_async_copy(staged.at[here], out.at[there], sems.at[k]))
        copies[-1].start()
    for copy in copies:
        copy.wait()


def own_kernel(flags, params, ids, mate_ids, image, mate_a, mate_b, text, accum, out_a, out_b, image_sum, loss):
    rows = image.shape[0]
    own_loss, coef = pair(image[...], text[:rows, :], ids[...], ids[...], params)
    loss[...] = own_loss
    total = accum[...] + dot(low(coef.T), image[...], (1, 0))
    cut = out_a.shape[0]

    def give(value):
        out_a[...] = value[:cut, :].astype(out_a.dtype)
        out_b[...] = value[cut:, :].astype(out_b.dtype)

    @pl.when(flags[0] == 0)
    def _():
        mate = jnp.concatenate([mate_a[...], mate_b[...]], axis=0)
        _, mate_coef = pair(mate, text[:rows, :], mate_ids[...], ids[...], params)
        give(total + dot(low(mate_coef.T), mate, (1, 0)))

    @pl.when(flags[0] == 1)
    def _():
        give(total)

    image_sum[...] = dot(low(coef), text[:rows, :], (1, 0))


def relay_kernel(flags, token, text, far, out_a, out_b):
    cut = out_a.shape[0]

    def fill(source):
        out_a[...] = source[:cut, :]
        out_b[...] = source[cut:, :]

    pl.when(flags[0] == 0)(lambda: fill(text))
    pl.when(flags[0] == 1)(lambda: fill(far))


def far_kernel(flags, params, ids, mate_ids, image, mate_a, mate_b, far, image_in, loss_in, late, image_sum, loss):
    rows = image.shape[0]
    far_ids = ids_of(far, rows, rows)
    more, coef = pair(image[...], far[:rows, :], ids[...], far_ids, params)
    loss[...] = loss_in[...] + more
    image_sum[...] = image_in[...] + dot(low(coef), far[:rows, :], (1, 0))
    part = dot(low(coef.T), image[...], (1, 0))

    @pl.when(flags[0] == 0)
    def _():
        late[...] = part

    @pl.when(flags[0] == 1)
    def _():
        mate = jnp.concatenate([mate_a[...], mate_b[...]], axis=0)
        _, mate_coef = pair(mate, far[:rows, :], mate_ids[...], far_ids, params)
        late[...] = part + dot(low(mate_coef.T), mate, (1, 0))


def near_kernel(params, ids, image, near_a, near_b, image_in, loss_in, image_grad, loss):
    rows = image.shape[0]
    rest = rows - near_a.shape[0]
    near = jnp.concatenate([near_a[...], near_b[:rest, :]], axis=0)
    more, coef = pair(image[...], near, ids[...], ids_of(near_b, rest, rows), params)
    loss[...] = (loss_in[...] + more) * (1.0 / ((SHIFTS + 1) * rows))
    image_grad[...] = (image_in[...] + dot(low(coef), near, (1, 0))).astype(image_grad.dtype)


def call(kernel, name, outs, scalars, *operands):
    return pl.pallas_call(
        kernel,
        out_shape=[jax.ShapeDtypeStruct(s, d) for s, d in outs],
        in_specs=[SMEM] * len(scalars) + [VMEM] * len(operands),
        out_specs=[VMEM] * len(outs),
        compiler_params=pltpu.CompilerParams(vmem_limit_bytes=16 * 1024 * 1024),
        cost_estimate=pl.CostEstimate(flops=0, bytes_accessed=0, transcendentals=0),
        name=name,
    )(*scalars, *operands)


def add_part(name, start, chunks, late, arrived, *before):
    return pl.pallas_call(
        functools.partial(add_kernel, start, chunks, len(arrived)),
        out_shape=jax.ShapeDtypeStruct(late.shape, late.dtype),
        in_specs=[VMEM] * (1 + len(arrived)) + [HBM] * len(before),
        out_specs=HBM,
        scratch_shapes=[pltpu.VMEM(arrived[0].shape, late.dtype), pltpu.SemaphoreType.DMA((chunks,))],
        input_output_aliases={1 + len(arrived): 0} if before else {},
        compiler_params=pltpu.CompilerParams(vmem_limit_bytes=16 * 1024 * 1024),
        cost_estimate=pl.CostEstimate(flops=0, bytes_accessed=0, transcendentals=0),
        name=name,
    )(late, *arrived, *before)


def body(image_emb, text_emb, text_accum, pair_ids, log_scale, bias):
    count = lax.axis_size(AXES)
    rows, width = image_emb.shape
    half = rows // 2
    f32, bf16 = jnp.float32, jnp.bfloat16
    flags = (lax.axis_index("group") % 2).astype(jnp.int32).reshape(1)
    params = jnp.concatenate([log_scale, bias])
    ids = pair_ids.reshape(1, rows)

    skip = [(i, (i + 2) % count) for i in range(count)]
    swap = [(i, i ^ 1) for i in range(count)]

    def ahead(value):
        return lax.ppermute(value, AXES, skip)

    def across(value):
        return lax.ppermute(value, AXES, swap)

    text = pl.pallas_call(
        cast_kernel,
        out_shape=jax.ShapeDtypeStruct((rows + PAD, width), bf16),
        in_specs=[HBM, HBM],
        out_specs=VMEM,
        scratch_shapes=[
            pltpu.VMEM((rows, width), f32),
            pltpu.VMEM((1, rows), jnp.int32),
            pltpu.SemaphoreType.DMA((CHUNKS,)),
            pltpu.SemaphoreType.DMA,
        ],
        compiler_params=pltpu.CompilerParams(vmem_limit_bytes=16 * 1024 * 1024),
        cost_estimate=pl.CostEstimate(flops=0, bytes_accessed=0, transcendentals=0),
        name="cast",
    )(*(pltpu.with_memory_space_constraint(value, pltpu.HBM) for value in (ids, text_emb)))
    far = ahead(text)

    image, text = lax.optimization_barrier((image_emb, text))
    image_emb = image
    mate_a, mate_b = across(image[:half]), across(image[half:])
    mate_ids = across(ids)

    cut = rows - rows * 3 // 8
    out_a, out_b, image_sum, loss = call(
        own_kernel, "own", [((cut, width), bf16), ((rows - cut, width), bf16), ((rows, width), f32), ((1, rows), f32)],
        (flags, params), ids, mate_ids, image_emb, mate_a, mate_b, text, text_accum,
    )
    turn = count - 4
    arrived_a = ahead(out_a)
    to_turn = lax.ppermute(out_b, AXES, [(count - 2, turn)])
    turned = lax.ppermute(to_turn, AXES, [(turn, 0)])
    arrived_b = lax.ppermute(out_b, AXES, skip[:-2] + skip[-1:])

    passed_a, passed_b = call(
        relay_kernel, "relay", [((half, width), bf16), ((rows + PAD - half, width), bf16)],
        (flags,), lax.optimization_barrier((loss, to_turn))[0], text, far,
    )
    near_a, near_b = across(passed_a), across(passed_b)
    late, image_sum, loss = call(
        far_kernel, "far", [((rows, width), f32), ((rows, width), f32), ((1, rows), f32)],
        (flags, params), ids, mate_ids, image_emb, mate_a, mate_b, far, image_sum, loss,
    )
    image_grad, loss = call(
        near_kernel, "near", [((rows, width), bf16), ((1, rows), f32)],
        (params,), ids, image_emb, near_a, near_b, image_sum, loss,
    )
    late, image_grad = lax.optimization_barrier((late, image_grad))
    text_grad = add_part("add_a", 0, 2, late, (arrived_a,))
    text_grad = add_part("add_b", cut, 1, late, (arrived_b, turned), text_grad)
    return (loss.reshape(rows), image_grad, text_grad)


def solution(mesh):
    in_specs = (P(AXES, None), P(AXES, None), P(AXES, None), P(AXES), P(), P())
    out_specs = (P(AXES), P(AXES, None), P(AXES, None))
    return jax.shard_map(body, mesh=mesh, in_specs=in_specs, out_specs=out_specs, check_vma=False)
```

```python
import functools

import jax
import jax.numpy as jnp
from jax import lax
from jax.experimental import pallas as pl
from jax.experimental.pallas import tpu as pltpu
from jax.sharding import PartitionSpec as P

SHIFTS = 2
AXES = ("dp", "group")
PAD = 8
CHUNKS = 4
VMEM = pl.BlockSpec(memory_space=pltpu.VMEM)
SMEM = pl.BlockSpec(memory_space=pltpu.SMEM)
HBM = pl.BlockSpec(memory_space=pltpu.HBM)


def dot(a, b, contract):
    return lax.dot_general(a, b, ((contract[:1], contract[1:]), ((), ())), preferred_element_type=jnp.float32)


def ids_of(text, at, rows):
    parts = text[at:, :rows].astype(jnp.float32).astype(jnp.int32)
    return parts[0:1] + parts[1:2] * 256 + parts[2:3] * 65536 + parts[3:4] * 16777216


def pair(images, texts, image_ids, text_ids, params):
    raw = dot(images, texts, (1, 1))
    rows = raw.shape[0]
    scale = jnp.exp(jnp.full((1, rows), params[0], jnp.float32))
    logits = scale * raw + params[1]
    same = jnp.broadcast_to(image_ids, (rows, rows)).T == text_ids
    margin = jnp.where(same, -logits, logits)
    tail = jnp.exp(-jnp.abs(margin))
    loss = jnp.maximum(margin, 0.0) + jnp.log1p(tail)
    sigmoid = jnp.where(margin >= 0, 1.0, tail) / (1.0 + tail)
    coef = jnp.where(same, -sigmoid, sigmoid) * scale
    return jnp.sum(loss.T, axis=0, keepdims=True), coef


def low(coef):
    return coef.astype(jnp.bfloat16)


def cast_kernel(ids, text, out, staged, ids_in, sems, ids_sem):
    rows, width = text.shape
    step = rows // CHUNKS
    ids_copy = pltpu.make_async_copy(ids, ids_in, ids_sem)
    copies = [
        pltpu.make_async_copy(text.at[pl.ds(k * step, step)], staged.at[pl.ds(k * step, step)], sems.at[k])
        for k in range(CHUNKS)
    ]
    for copy in copies:
        copy.start()
    ids_copy.start()
    out[rows:, :] = jnp.zeros((PAD, width), out.dtype)
    for k, copy in enumerate(copies):
        copy.wait()
        out[k * step:(k + 1) * step, :] = staged[k * step:(k + 1) * step, :].astype(out.dtype)
    ids_copy.wait()
    row = lax.broadcasted_iota(jnp.int32, (PAD, rows), 0)
    spread = jnp.broadcast_to(ids_in[...], (PAD, rows))
    parts = jnp.zeros((PAD, rows), jnp.int32)
    for k in range(4):
        parts = jnp.where(row == k, (spread >> (8 * k)) & 255, parts)
    out[rows:, :rows] = parts.astype(jnp.float32).astype(out.dtype)


def add_kernel(start, chunks, late, arrived, *refs):
    flag_turned, (out, staged, sems) = refs[:2], refs[-3:]
    step = staged.shape[0] // chunks
    copies = []
    for k in range(chunks):
        here, there = pl.ds(k * step, step), pl.ds(start + k * step, step)
        staged[here, :] = arrived[here, :].astype(staged.dtype) + late[there, :]
        if start:
            flag, turned = flag_turned

            @pl.when(flag[0] == 1)
            def _():
                part = turned[pl.ds(staged.shape[0] + k * step, step), :]
                staged[here, :] = part.astype(staged.dtype) + late[there, :]

        copies.append(pltpu.make_async_copy(staged.at[here], out.at[there], sems.at[k]))
        copies[-1].start()
    for copy in copies:
        copy.wait()


def own_kernel(flags, params, ids, mate_ids, image, mate_a, mate_b, text, accum, out_a, out_b, image_sum, loss):
    rows = image.shape[0]
    own_loss, coef = pair(image[...], text[:rows, :], ids[...], ids[...], params)
    loss[...] = own_loss
    total = accum[...] + dot(low(coef.T), image[...], (1, 0))
    cut = out_a.shape[0]

    def give(value):
        out_a[...] = value[:cut, :].astype(out_a.dtype)
        out_b[...] = value[cut:, :].astype(out_b.dtype)

    @pl.when(flags[0] == 0)
    def _():
        mate = jnp.concatenate([mate_a[...], mate_b[...]], axis=0)
        _, mate_coef = pair(mate, text[:rows, :], mate_ids[...], ids[...], params)
        give(total + dot(low(mate_coef.T), mate, (1, 0)))

    @pl.when(flags[0] == 1)
    def _():
        give(total)

    image_sum[...] = dot(low(coef), text[:rows, :], (1, 0))


def relay_kernel(flags, token, text, far, out_a, out_b):
    cut = out_a.shape[0]

    def fill(source):
        out_a[...] = source[:cut, :]
        out_b[...] = source[cut:, :]

    pl.when(flags[0] == 0)(lambda: fill(text))
    pl.when(flags[0] == 1)(lambda: fill(far))


def far_kernel(flags, params, ids, mate_ids, image, mate_a, mate_b, far, image_in, loss_in, late, image_sum, loss):
    rows = image.shape[0]
    far_ids = ids_of(far, rows, rows)
    more, coef = pair(image[...], far[:rows, :], ids[...], far_ids, params)
    loss[...] = loss_in[...] + more
    image_sum[...] = image_in[...] + dot(low(coef), far[:rows, :], (1, 0))
    part = dot(low(coef.T), image[...], (1, 0))

    @pl.when(flags[0] == 0)
    def _():
        late[...] = part

    @pl.when(flags[0] == 1)
    def _():
        mate = jnp.concatenate([mate_a[...], mate_b[...]], axis=0)
        _, mate_coef = pair(mate, far[:rows, :], mate_ids[...], far_ids, params)
        late[...] = part + dot(low(mate_coef.T), mate, (1, 0))


def near_kernel(params, ids, image, near_a, near_b, image_in, loss_in, image_grad, loss):
    rows = image.shape[0]
    rest = rows - near_a.shape[0]
    near = jnp.concatenate([near_a[...], near_b[:rest, :]], axis=0)
    more, coef = pair(image[...], near, ids[...], ids_of(near_b, rest, rows), params)
    loss[...] = (loss_in[...] + more) * (1.0 / ((SHIFTS + 1) * rows))
    image_grad[...] = (image_in[...] + dot(low(coef), near, (1, 0))).astype(image_grad.dtype)


def call(kernel, name, outs, scalars, *operands):
    return pl.pallas_call(
        kernel,
        out_shape=[jax.ShapeDtypeStruct(s, d) for s, d in outs],
        in_specs=[SMEM] * len(scalars) + [VMEM] * len(operands),
        out_specs=[VMEM] * len(outs),
        compiler_params=pltpu.CompilerParams(vmem_limit_bytes=16 * 1024 * 1024),
        cost_estimate=pl.CostEstimate(flops=0, bytes_accessed=0, transcendentals=0),
        name=name,
    )(*scalars, *operands)


def add_part(name, start, chunks, late, arrived, *more):
    return pl.pallas_call(
        functools.partial(add_kernel, start, chunks),
        out_shape=jax.ShapeDtypeStruct(late.shape, late.dtype),
        in_specs=[VMEM, VMEM] + ([SMEM, VMEM, HBM] if more else []),
        out_specs=HBM,
        scratch_shapes=[pltpu.VMEM(arrived.shape, late.dtype), pltpu.SemaphoreType.DMA((chunks,))],
        input_output_aliases={4: 0} if more else {},
        compiler_params=pltpu.CompilerParams(vmem_limit_bytes=16 * 1024 * 1024),
        cost_estimate=pl.CostEstimate(flops=0, bytes_accessed=0, transcendentals=0),
        name=name,
    )(late, arrived, *more)


def body(image_emb, text_emb, text_accum, pair_ids, log_scale, bias):
    count = lax.axis_size(AXES)
    rows, width = image_emb.shape
    half = rows // 2
    f32, bf16 = jnp.float32, jnp.bfloat16
    flags = (lax.axis_index("group") % 2).astype(jnp.int32).reshape(1)
    params = jnp.concatenate([log_scale, bias])
    ids = pair_ids.reshape(1, rows)

    skip = [(i, (i + 2) % count) for i in range(count)]
    swap = [(i, i ^ 1) for i in range(count)]

    def ahead(value):
        return lax.ppermute(value, AXES, skip)

    def across(value):
        return lax.ppermute(value, AXES, swap)

    text = pl.pallas_call(
        cast_kernel,
        out_shape=jax.ShapeDtypeStruct((rows + PAD, width), bf16),
        in_specs=[HBM, HBM],
        out_specs=VMEM,
        scratch_shapes=[
            pltpu.VMEM((rows, width), f32),
            pltpu.VMEM((1, rows), jnp.int32),
            pltpu.SemaphoreType.DMA((CHUNKS,)),
            pltpu.SemaphoreType.DMA,
        ],
        compiler_params=pltpu.CompilerParams(vmem_limit_bytes=16 * 1024 * 1024),
        cost_estimate=pl.CostEstimate(flops=0, bytes_accessed=0, transcendentals=0),
        name="cast",
    )(*(pltpu.with_memory_space_constraint(value, pltpu.HBM) for value in (ids, text_emb)))
    far = ahead(text)

    image, text = lax.optimization_barrier((image_emb, text))
    image_emb = image
    mate_a, mate_b = across(image[:half]), across(image[half:])
    mate_ids = across(ids)

    cut = rows - rows * 3 // 16
    out_a, out_b, image_sum, loss = call(
        own_kernel, "own", [((cut, width), bf16), ((rows - cut, width), bf16), ((rows, width), f32), ((1, rows), f32)],
        (flags, params), ids, mate_ids, image_emb, mate_a, mate_b, text, text_accum,
    )
    turn = count - 4
    arrived_a = ahead(out_a)
    pairs = [[i, i + 1] for i in range(0, count, 2)]
    first_legs = pairs[:-2] + [[turn, count - 2], [turn + 1, count - 1]]
    second_legs = pairs[1:-2] + [[0, turn], [1, turn + 1], [count - 2, count - 1]]
    to_turn = lax.all_gather(out_b, AXES, axis_index_groups=first_legs)[1]
    turned = lax.all_gather(to_turn, AXES, axis_index_groups=second_legs, tiled=True)
    at_start = (lax.axis_index(AXES) < 2).astype(jnp.int32).reshape(1)
    arrived_b = lax.ppermute(out_b, AXES, skip[:-2])

    passed_a, passed_b = call(
        relay_kernel, "relay", [((half, width), bf16), ((rows + PAD - half, width), bf16)],
        (flags,), to_turn, text, far,
    )
    near_a, near_b = across(passed_a), across(passed_b)
    late, image_sum, loss = call(
        far_kernel, "far", [((rows, width), f32), ((rows, width), f32), ((1, rows), f32)],
        (flags, params), ids, mate_ids, image_emb, mate_a, mate_b, far, image_sum, loss,
    )
    image_grad, loss = call(
        near_kernel, "near", [((rows, width), bf16), ((1, rows), f32)],
        (params,), ids, image_emb, near_a, near_b, image_sum, loss,
    )
    late, image_grad = lax.optimization_barrier((late, image_grad))
    text_grad = add_part("add_a", 0, 2, late, arrived_a)
    text_grad = add_part("add_b", cut, 1, late, arrived_b, at_start, turned, text_grad)
    return (loss.reshape(rows), image_grad, text_grad)


def solution(mesh):
    in_specs = (P(AXES, None), P(AXES, None), P(AXES, None), P(AXES), P(), P())
    out_specs = (P(AXES), P(AXES, None), P(AXES, None))
    return jax.shard_map(body, mesh=mesh, in_specs=in_specs, out_specs=out_specs, check_vma=False)
```

```python
import functools

import jax
import jax.numpy as jnp
from jax import lax
from jax.experimental import pallas as pl
from jax.experimental.pallas import tpu as pltpu
from jax.sharding import PartitionSpec as P

SHIFTS = 2
AXES = ("dp", "group")
CHUNKS = 4
VMEM = pl.BlockSpec(memory_space=pltpu.VMEM)
SMEM = pl.BlockSpec(memory_space=pltpu.SMEM)
HBM = pl.BlockSpec(memory_space=pltpu.HBM)


def dot(a, b, contract):
    return lax.dot_general(a, b, ((contract[:1], contract[1:]), ((), ())), preferred_element_type=jnp.float32)


def pair(images, texts, image_ids, text_ids, params):
    raw = dot(images, texts, (1, 1))
    rows = raw.shape[0]
    scale = jnp.exp(jnp.full((1, rows), params[0], jnp.float32))
    logits = scale * raw + params[1]
    same = jnp.broadcast_to(image_ids, (rows, rows)).T == text_ids
    margin = jnp.where(same, -logits, logits)
    tail = jnp.exp(-jnp.abs(margin))
    loss = jnp.maximum(margin, 0.0) + jnp.log1p(tail)
    sigmoid = jnp.where(margin >= 0, 1.0, tail) / (1.0 + tail)
    coef = jnp.where(same, -sigmoid, sigmoid) * scale
    return jnp.sum(loss.T, axis=0, keepdims=True), coef


def low(coef):
    return coef.astype(jnp.bfloat16)


def cast_kernel(text, out, staged, sems):
    step = text.shape[0] // CHUNKS
    parts = [pl.ds(k * step, step) for k in range(CHUNKS)]
    copies = [pltpu.make_async_copy(text.at[part], staged.at[part], sems.at[k]) for k, part in enumerate(parts)]
    for copy in copies:
        copy.start()
    for part, copy in zip(parts, copies):
        copy.wait()
        out[part, :] = staged[part, :].astype(out.dtype)


def add_kernel(start, chunks, arrived, late, *refs):
    out, staged, sems = refs[-3:]
    step = arrived.shape[0] // chunks
    copies = []
    for k in range(chunks):
        here, there = pl.ds(k * step, step), pl.ds(start + k * step, step)
        staged[here, :] = arrived[here, :].astype(staged.dtype) + late[there, :]
        copies.append(pltpu.make_async_copy(staged.at[here], out.at[there], sems.at[k]))
        copies[-1].start()
    for copy in copies:
        copy.wait()


def own_kernel(flags, params, ids, mate_ids, image, mate_a, mate_b, text, accum, out_a, out_b, image_sum, loss):
    own_loss, coef = pair(image[...], text[...], ids[...], ids[...], params)
    loss[...] = own_loss
    total = accum[...] + dot(low(coef.T), image[...], (1, 0))
    cut = out_a.shape[0]

    def give(value):
        out_a[...] = value[:cut, :].astype(out_a.dtype)
        out_b[...] = value[cut:, :].astype(out_b.dtype)

    @pl.when(flags[0] == 0)
    def _():
        mate = jnp.concatenate([mate_a[...], mate_b[...]], axis=0)
        _, mate_coef = pair(mate, text[...], mate_ids[...], ids[...], params)
        give(total + dot(low(mate_coef.T), mate, (1, 0)))

    @pl.when(flags[0] == 1)
    def _():
        give(total)

    image_sum[...] = dot(low(coef), text[...], (1, 0))


def relay_kernel(flags, token, text, far, out_a, out_b):
    cut = out_a.shape[0]

    def fill(source):
        out_a[...] = source[:cut, :]
        out_b[...] = source[cut:, :]

    pl.when(flags[0] == 0)(lambda: fill(text))
    pl.when(flags[0] == 1)(lambda: fill(far))


def far_kernel(flags, params, ids, mate_ids, far_ids, image, mate_a, mate_b, far, image_in, loss_in,
               late, image_sum, loss):
    more, coef = pair(image[...], far[...], ids[...], far_ids[...], params)
    loss[...] = loss_in[...] + more
    image_sum[...] = image_in[...] + dot(low(coef), far[...], (1, 0))
    part = dot(low(coef.T), image[...], (1, 0))

    @pl.when(flags[0] == 0)
    def _():
        late[...] = part

    @pl.when(flags[0] == 1)
    def _():
        mate = jnp.concatenate([mate_a[...], mate_b[...]], axis=0)
        _, mate_coef = pair(mate, far[...], mate_ids[...], far_ids[...], params)
        late[...] = part + dot(low(mate_coef.T), mate, (1, 0))


def near_kernel(params, ids, near_ids, image, near_a, near_b, image_in, loss_in, image_grad, loss):
    near = jnp.concatenate([near_a[...], near_b[...]], axis=0)
    more, coef = pair(image[...], near, ids[...], near_ids[...], params)
    loss[...] = (loss_in[...] + more) * (1.0 / ((SHIFTS + 1) * image.shape[0]))
    image_grad[...] = (image_in[...] + dot(low(coef), near, (1, 0))).astype(image_grad.dtype)


def call(kernel, name, outs, scalars, *operands):
    return pl.pallas_call(
        kernel,
        out_shape=[jax.ShapeDtypeStruct(s, d) for s, d in outs],
        in_specs=[SMEM] * len(scalars) + [VMEM] * len(operands),
        out_specs=[VMEM] * len(outs),
        compiler_params=pltpu.CompilerParams(vmem_limit_bytes=16 * 1024 * 1024),
        cost_estimate=pl.CostEstimate(flops=0, bytes_accessed=0, transcendentals=0),
        name=name,
    )(*scalars, *operands)


def add_part(name, start, chunks, arrived, late, *before):
    return pl.pallas_call(
        functools.partial(add_kernel, start, chunks),
        out_shape=jax.ShapeDtypeStruct(late.shape, late.dtype),
        in_specs=[VMEM, VMEM] + [HBM] * len(before),
        out_specs=HBM,
        scratch_shapes=[pltpu.VMEM(arrived.shape, late.dtype), pltpu.SemaphoreType.DMA((chunks,))],
        input_output_aliases={2: 0} if before else {},
        compiler_params=pltpu.CompilerParams(vmem_limit_bytes=16 * 1024 * 1024),
        cost_estimate=pl.CostEstimate(flops=0, bytes_accessed=0, transcendentals=0),
        name=name,
    )(arrived, late, *before)


def body(image_emb, text_emb, text_accum, pair_ids, log_scale, bias):
    count = lax.axis_size(AXES)
    rows, width = image_emb.shape
    half = rows // 2
    f32, bf16 = jnp.float32, jnp.bfloat16
    flags = (lax.axis_index("group") % 2).astype(jnp.int32).reshape(1)
    params = jnp.concatenate([log_scale, bias])
    ids = pair_ids.reshape(1, rows)

    skip = [(i, (i + 2) % count) for i in range(count)]
    swap = [(i, i ^ 1) for i in range(count)]

    def ahead(value):
        return lax.ppermute(value, AXES, skip)

    def across(value):
        return lax.ppermute(value, AXES, swap)

    text = pl.pallas_call(
        cast_kernel,
        out_shape=jax.ShapeDtypeStruct((rows, width), bf16),
        in_specs=[HBM],
        out_specs=VMEM,
        scratch_shapes=[pltpu.VMEM((rows, width), f32), pltpu.SemaphoreType.DMA((CHUNKS,))],
        compiler_params=pltpu.CompilerParams(vmem_limit_bytes=16 * 1024 * 1024),
        cost_estimate=pl.CostEstimate(flops=0, bytes_accessed=0, transcendentals=0),
        name="cast",
    )(pltpu.with_memory_space_constraint(text_emb, pltpu.HBM))
    far = ahead(text)

    image, text = lax.optimization_barrier((image_emb, text))
    image_emb = image
    mate_a, mate_b = across(image[:half]), across(image[half:])
    mate_ids = across(ids)
    both_ids = ahead(jnp.concatenate([ids, mate_ids]))

    cut = rows - rows // 8
    out_a, out_b, image_sum, loss = call(
        own_kernel, "own", [((cut, width), bf16), ((rows - cut, width), bf16), ((rows, width), f32), ((1, rows), f32)],
        (flags, params), ids, mate_ids, image_emb, mate_a, mate_b, text, text_accum,
    )
    arrived_a, arrived_b = ahead(out_a), ahead(out_b)

    far_ids, near_ids = both_ids[:1], jnp.where(flags[0] == 0, both_ids[1:], mate_ids)
    passed_a, passed_b = call(
        relay_kernel, "relay", [((cut - 16, width), bf16), ((rows - cut + 16, width), bf16)],
        (flags,), far_ids, text, far,
    )
    near_a, near_b = across(passed_a), across(passed_b)
    late, image_sum, loss = call(
        far_kernel, "far", [((rows, width), f32), ((rows, width), f32), ((1, rows), f32)],
        (flags, params), ids, mate_ids, far_ids, image_emb, mate_a, mate_b, far, image_sum, loss,
    )
    image_grad, loss = call(
        near_kernel, "near", [((rows, width), bf16), ((1, rows), f32)],
        (params,), ids, near_ids, image_emb, near_a, near_b, image_sum, loss,
    )
    late, image_grad = lax.optimization_barrier((late, image_grad))
    text_grad = add_part("add_a", 0, CHUNKS, arrived_a, late)
    text_grad = add_part("add_b", cut, 1, arrived_b, late, text_grad)
    return (loss.reshape(rows), image_grad, text_grad)


def solution(mesh):
    in_specs = (P(AXES, None), P(AXES, None), P(AXES, None), P(AXES), P(), P())
    out_specs = (P(AXES), P(AXES, None), P(AXES, None))
    return jax.shard_map(body, mesh=mesh, in_specs=in_specs, out_specs=out_specs, check_vma=False)
```

```python
import functools

import jax
import jax.numpy as jnp
from jax import lax
from jax.experimental import pallas as pl
from jax.experimental.pallas import tpu as pltpu
from jax.sharding import PartitionSpec as P

SHIFTS = 2
AXES = ("dp", "group")
CHUNKS = 4
VMEM = pl.BlockSpec(memory_space=pltpu.VMEM)
SMEM = pl.BlockSpec(memory_space=pltpu.SMEM)
ANY = pl.BlockSpec(memory_space=pl.ANY)
HBM = pl.BlockSpec(memory_space=pltpu.HBM)


def dot(a, b, contract):
    return lax.dot_general(a, b, ((contract[:1], contract[1:]), ((), ())), preferred_element_type=jnp.float32)


def pair(images, texts, image_ids, text_ids, params):
    raw = dot(images, texts, (1, 1))
    rows = raw.shape[0]
    scale = jnp.exp(jnp.full((1, rows), params[0], jnp.float32))
    logits = scale * raw + params[1]
    same = jnp.broadcast_to(image_ids, (rows, rows)).T == text_ids
    margin = jnp.where(same, -logits, logits)
    tail = jnp.exp(-jnp.abs(margin))
    loss = jnp.maximum(margin, 0.0) + jnp.log1p(tail)
    sigmoid = jnp.where(margin >= 0, 1.0, tail) / (1.0 + tail)
    coef = jnp.where(same, -sigmoid, sigmoid) * scale
    return jnp.sum(loss.T, axis=0, keepdims=True), coef


def low(coef):
    return coef.astype(jnp.bfloat16)


def cast_kernel(text, out, staged, sems):
    step = text.shape[0] // CHUNKS
    parts = [pl.ds(k * step, step) for k in range(CHUNKS)]
    copies = [pltpu.make_async_copy(text.at[part], staged.at[part], sems.at[k]) for k, part in enumerate(parts)]
    for copy in copies:
        copy.start()
    for part, copy in zip(parts, copies):
        copy.wait()
        out[part, :] = staged[part, :].astype(out.dtype)


def load_kernel(text, image, out, half_a, half_b, sems):
    half = half_a.shape[0]
    copies = [
        pltpu.make_async_copy(image.at[pl.ds(0, half)], half_a, sems.at[0]),
        pltpu.make_async_copy(image.at[pl.ds(half, half)], half_b, sems.at[1]),
        pltpu.make_async_copy(image, out, sems.at[2]),
    ]
    for copy in copies:
        copy.start()
    for copy in copies:
        copy.wait()


def add_kernel(start, chunks, arrived, late, *refs):
    out, staged, sems = refs[-3:]
    step = arrived.shape[0] // chunks
    copies = []
    for k in range(chunks):
        here, there = pl.ds(k * step, step), pl.ds(start + k * step, step)
        staged[here, :] = arrived[here, :].astype(staged.dtype) + late[there, :]
        copies.append(pltpu.make_async_copy(staged.at[here], out.at[there], sems.at[k]))
        copies[-1].start()
    for copy in copies:
        copy.wait()


def own_kernel(flags, params, ids, mate_ids, image, mate_a, mate_b, text, accum_in, out_a, out_b, image_sum, loss,
               accum, sem):
    copy = pltpu.make_async_copy(accum_in, accum, sem)
    copy.start()
    own_loss, coef = pair(image[...], text[...], ids[...], ids[...], params)
    loss[...] = own_loss
    part = dot(low(coef.T), image[...], (1, 0))
    copy.wait()
    total = accum[...] + part
    cut = out_a.shape[0]

    def give(value):
        out_a[...] = value[:cut, :].astype(out_a.dtype)
        out_b[...] = value[cut:, :].astype(out_b.dtype)

    @pl.when(flags[0] == 0)
    def _():
        mate = jnp.concatenate([mate_a[...], mate_b[...]], axis=0)
        _, mate_coef = pair(mate, text[...], mate_ids[...], ids[...], params)
        give(total + dot(low(mate_coef.T), mate, (1, 0)))

    @pl.when(flags[0] == 1)
    def _():
        give(total)

    image_sum[...] = dot(low(coef), text[...], (1, 0))


def relay_kernel(flags, token, text, far, out_a, out_b):
    cut = out_a.shape[0]

    def fill(source):
        out_a[...] = source[:cut, :]
        out_b[...] = source[cut:, :]

    pl.when(flags[0] == 0)(lambda: fill(text))
    pl.when(flags[0] == 1)(lambda: fill(far))


def far_kernel(flags, params, ids, mate_ids, both_ids, image, mate_a, mate_b, far, image_in, loss_in,
               late, image_sum, loss):
    more, coef = pair(image[...], far[...], ids[...], both_ids[:1, :], params)
    loss[...] = loss_in[...] + more
    image_sum[...] = image_in[...] + dot(low(coef), far[...], (1, 0))
    part = dot(low(coef.T), image[...], (1, 0))

    @pl.when(flags[0] == 0)
    def _():
        late[...] = part

    @pl.when(flags[0] == 1)
    def _():
        mate = jnp.concatenate([mate_a[...], mate_b[...]], axis=0)
        _, mate_coef = pair(mate, far[...], mate_ids[...], both_ids[:1, :], params)
        late[...] = part + dot(low(mate_coef.T), mate, (1, 0))


def near_kernel(flags, params, ids, mate_ids, both_ids, image, near_a, near_b, image_in, loss_in, image_grad, loss):
    near_ids = jnp.where(flags[0] == 0, both_ids[1:, :], mate_ids[...])
    near = jnp.concatenate([near_a[...], near_b[...]], axis=0)
    more, coef = pair(image[...], near, ids[...], near_ids, params)
    loss[...] = (loss_in[...] + more) * (1.0 / ((SHIFTS + 1) * image.shape[0]))
    image_grad[...] = (image_in[...] + dot(low(coef), near, (1, 0))).astype(image_grad.dtype)


def call(kernel, name, outs, scalars, *operands, flops=0):
    return pl.pallas_call(
        kernel,
        out_shape=[jax.ShapeDtypeStruct(s, d) for s, d in outs],
        in_specs=[SMEM] * len(scalars) + [VMEM] * len(operands),
        out_specs=[VMEM] * len(outs),
        compiler_params=pltpu.CompilerParams(vmem_limit_bytes=16 * 1024 * 1024),
        cost_estimate=pl.CostEstimate(flops=flops, bytes_accessed=0, transcendentals=0),
        name=name,
    )(*scalars, *operands)


def add_part(name, start, chunks, arrived, late, *before):
    return pl.pallas_call(
        functools.partial(add_kernel, start, chunks),
        out_shape=jax.ShapeDtypeStruct(late.shape, late.dtype),
        in_specs=[VMEM, VMEM] + [HBM] * len(before),
        out_specs=HBM,
        scratch_shapes=[pltpu.VMEM(arrived.shape, late.dtype), pltpu.SemaphoreType.DMA((chunks,))],
        input_output_aliases={2: 0} if before else {},
        compiler_params=pltpu.CompilerParams(vmem_limit_bytes=16 * 1024 * 1024),
        cost_estimate=pl.CostEstimate(flops=0, bytes_accessed=0, transcendentals=0),
        name=name,
    )(arrived, late, *before)


def body(image_emb, text_emb, text_accum, pair_ids, log_scale, bias):
    count = lax.axis_size(AXES)
    rows, width = image_emb.shape
    half = rows // 2
    f32, bf16 = jnp.float32, jnp.bfloat16
    flags = (lax.axis_index("group") % 2).astype(jnp.int32).reshape(1)
    params = jnp.concatenate([log_scale, bias])
    ids = pair_ids.reshape(1, rows)

    skip = [(i, (i + 2) % count) for i in range(count)]
    swap = [(i, i ^ 1) for i in range(count)]

    def ahead(value):
        return lax.ppermute(value, AXES, skip)

    def across(value):
        return lax.ppermute(value, AXES, swap)

    text = pl.pallas_call(
        cast_kernel,
        out_shape=jax.ShapeDtypeStruct((rows, width), bf16),
        in_specs=[HBM],
        out_specs=VMEM,
        scratch_shapes=[pltpu.VMEM((rows, width), f32), pltpu.SemaphoreType.DMA((CHUNKS,))],
        compiler_params=pltpu.CompilerParams(vmem_limit_bytes=16 * 1024 * 1024),
        cost_estimate=pl.CostEstimate(flops=0, bytes_accessed=0, transcendentals=0),
        name="cast",
    )(pltpu.with_memory_space_constraint(text_emb, pltpu.HBM))
    far = ahead(text)

    image, half_a, half_b = pl.pallas_call(
        load_kernel,
        out_shape=[jax.ShapeDtypeStruct((n, width), bf16) for n in (rows, half, rows - half)],
        in_specs=[ANY, HBM],
        out_specs=[VMEM] * 3,
        scratch_shapes=[pltpu.SemaphoreType.DMA((3,))],
        compiler_params=pltpu.CompilerParams(vmem_limit_bytes=16 * 1024 * 1024),
        cost_estimate=pl.CostEstimate(flops=0, bytes_accessed=0, transcendentals=0),
        name="load",
    )(text, pltpu.with_memory_space_constraint(image_emb, pltpu.HBM))
    mate_a, mate_b = across(half_a), across(half_b)
    mate_ids = across(ids)
    both_ids = ahead(jnp.concatenate([ids, mate_ids]))

    cut = rows - rows * 3 // 16
    out_a, out_b, image_sum, loss = pl.pallas_call(
        own_kernel,
        out_shape=[
            jax.ShapeDtypeStruct((cut, width), bf16),
            jax.ShapeDtypeStruct((rows - cut, width), bf16),
            jax.ShapeDtypeStruct((rows, width), f32),
            jax.ShapeDtypeStruct((1, rows), f32),
        ],
        in_specs=[SMEM] * 2 + [VMEM] * 6 + [HBM],
        out_specs=[VMEM] * 4,
        scratch_shapes=[pltpu.VMEM((rows, width), f32), pltpu.SemaphoreType.DMA],
        compiler_params=pltpu.CompilerParams(vmem_limit_bytes=16 * 1024 * 1024),
        cost_estimate=pl.CostEstimate(flops=0, bytes_accessed=0, transcendentals=0),
        name="own",
    )(flags, params, ids, mate_ids, image, mate_a, mate_b, text,
      pltpu.with_memory_space_constraint(text_accum, pltpu.HBM))
    arrived_a, arrived_b = ahead(out_a), ahead(out_b)

    passed_a, passed_b = call(
        relay_kernel, "relay", [((cut - 16, width), bf16), ((rows - cut + 16, width), bf16)],
        (flags,), both_ids, text, far, flops=1 << 30,
    )
    near_a, near_b = across(passed_a), across(passed_b)
    late, image_sum, loss = call(
        far_kernel, "far", [((rows, width), f32), ((rows, width), f32), ((1, rows), f32)],
        (flags, params), ids, mate_ids, both_ids, image, mate_a, mate_b, far, image_sum, loss,
    )
    image_grad, loss = call(
        near_kernel, "near", [((rows, width), bf16), ((1, rows), f32)],
        (flags, params), ids, mate_ids, both_ids, image, near_a, near_b, image_sum, loss,
    )
    late, image_grad = lax.optimization_barrier((late, image_grad))
    text_grad = add_part("add_a", 0, 2, arrived_a, late)
    text_grad = add_part("add_b", cut, 1, arrived_b, late, text_grad)
    return (loss.reshape(rows), image_grad, text_grad)


def solution(mesh):
    in_specs = (P(AXES, None), P(AXES, None), P(AXES, None), P(AXES), P(), P())
    out_specs = (P(AXES), P(AXES, None), P(AXES, None))
    return jax.shard_map(body, mesh=mesh, in_specs=in_specs, out_specs=out_specs, check_vma=False)
```

```python
import functools

import jax
import jax.numpy as jnp
from jax import lax
from jax.experimental import pallas as pl
from jax.experimental.pallas import tpu as pltpu
from jax.sharding import PartitionSpec as P

SHIFTS = 2
AXES = ("dp", "group")
STEP = 16
VMEM = pl.BlockSpec(memory_space=pltpu.VMEM)
SMEM = pl.BlockSpec(memory_space=pltpu.SMEM)
ANY = pl.BlockSpec(memory_space=pl.ANY)
HBM = pl.BlockSpec(memory_space=pltpu.HBM)


def dot(a, b, contract):
    return lax.dot_general(a, b, ((contract[:1], contract[1:]), ((), ())), preferred_element_type=jnp.float32)


def pair(images, texts, image_ids, text_ids, params):
    raw = dot(images, texts, (1, 1))
    rows = raw.shape[0]
    scale = jnp.exp(jnp.full((1, rows), params[0], jnp.float32))
    logits = scale * raw + params[1]
    same = jnp.broadcast_to(image_ids, (rows, rows)).T == text_ids
    margin = jnp.where(same, -logits, logits)
    tail = jnp.exp(-jnp.abs(margin))
    loss = jnp.maximum(margin, 0.0) + jnp.log1p(tail)
    sigmoid = jnp.where(margin >= 0, 1.0, tail) / (1.0 + tail)
    coef = jnp.where(same, -sigmoid, sigmoid) * scale
    return jnp.sum(loss.T, axis=0, keepdims=True), coef


def whole(a, b):
    return jnp.concatenate([a[...], b[...]], axis=0)


def low(coef):
    return coef.astype(jnp.bfloat16)


def cast_kernel(text, out):
    out[...] = text[...].astype(out.dtype)


def load_kernel(text, image, out_a, out_b, sems):
    half = out_a.shape[0]
    copies = [
        pltpu.make_async_copy(image.at[pl.ds(0, half)], out_a, sems.at[0]),
        pltpu.make_async_copy(image.at[pl.ds(half, half)], out_b, sems.at[1]),
    ]
    for copy in copies:
        copy.start()
    for copy in copies:
        copy.wait()


def add_kernel(start, chunks, arrived, late, *refs):
    out, staged, sems = refs[-3:]
    step = arrived.shape[0] // chunks
    copies = []
    for k in range(chunks):
        here, there = pl.ds(k * step, step), pl.ds(start + k * step, step)
        staged[here, :] = arrived[here, :].astype(staged.dtype) + late[there, :]
        copies.append(pltpu.make_async_copy(staged.at[here], out.at[there], sems.at[k]))
        copies[-1].start()
    for copy in copies:
        copy.wait()


def own_kernel(flags, params, ids, mate_ids, image_a, image_b, mate_a, mate_b, text, accum_in, out_a, out_b, image_sum, loss,
               accum, sem):
    copy = pltpu.make_async_copy(accum_in, accum, sem)
    copy.start()
    image = whole(image_a, image_b)
    own_loss, coef = pair(image, text[...], ids[...], ids[...], params)
    loss[...] = own_loss
    copy.wait()
    total = accum[...] + dot(low(coef.T), image, (1, 0))
    cut = out_a.shape[0]

    def give(value):
        out_a[...] = value[:cut, :].astype(out_a.dtype)
        out_b[...] = value[cut:, :].astype(out_b.dtype)

    @pl.when(flags[0] == 0)
    def _():
        mate = whole(mate_a, mate_b)
        _, mate_coef = pair(mate, text[...], mate_ids[...], ids[...], params)
        give(total + dot(low(mate_coef.T), mate, (1, 0)))

    @pl.when(flags[0] == 1)
    def _():
        give(total)

    image_sum[...] = dot(low(coef), text[...], (1, 0))


def relay_kernel(flags, token, text, far, out_a, out_b):
    cut = out_a.shape[0]

    def fill(source):
        out_a[...] = source[:cut, :]
        out_b[...] = source[cut:, :]

    pl.when(flags[0] == 0)(lambda: fill(text))
    pl.when(flags[0] == 1)(lambda: fill(far))


def far_kernel(flags, params, ids, mate_ids, both_ids, image_a, image_b, mate_a, mate_b, far, image_in,
               loss_in, late, image_sum, loss):
    image = whole(image_a, image_b)
    more, coef = pair(image, far[...], ids[...], both_ids[:1, :], params)
    loss[...] = loss_in[...] + more
    image_sum[...] = image_in[...] + dot(low(coef), far[...], (1, 0))
    part = dot(low(coef.T), image, (1, 0))

    @pl.when(flags[0] == 0)
    def _():
        late[...] = part

    @pl.when(flags[0] == 1)
    def _():
        mate = whole(mate_a, mate_b)
        _, mate_coef = pair(mate, far[...], mate_ids[...], both_ids[:1, :], params)
        late[...] = part + dot(low(mate_coef.T), mate, (1, 0))


def near_kernel(flags, params, ids, mate_ids, both_ids, image_a, image_b, near_a, near_b, image_in, loss_in,
                image_grad, loss):
    image = whole(image_a, image_b)
    near_ids = jnp.where(flags[0] == 0, both_ids[1:, :], mate_ids[...])
    near = whole(near_a, near_b)
    more, coef = pair(image, near, ids[...], near_ids, params)
    loss[...] = (loss_in[...] + more) * (1.0 / ((SHIFTS + 1) * image.shape[0]))
    image_grad[...] = (image_in[...] + dot(low(coef), near, (1, 0))).astype(image_grad.dtype)


def call(kernel, name, outs, scalars, *operands, flops=0):
    return pl.pallas_call(
        kernel,
        out_shape=[jax.ShapeDtypeStruct(s, d) for s, d in outs],
        in_specs=[SMEM] * len(scalars) + [VMEM] * len(operands),
        out_specs=[VMEM] * len(outs),
        compiler_params=pltpu.CompilerParams(vmem_limit_bytes=16 * 1024 * 1024),
        cost_estimate=pl.CostEstimate(flops=flops, bytes_accessed=0, transcendentals=0),
        name=name,
    )(*scalars, *operands)


def add_part(name, start, chunks, arrived, late, *before):
    return pl.pallas_call(
        functools.partial(add_kernel, start, chunks),
        out_shape=jax.ShapeDtypeStruct(late.shape, late.dtype),
        in_specs=[VMEM, VMEM] + [HBM] * len(before),
        out_specs=HBM,
        scratch_shapes=[pltpu.VMEM(arrived.shape, late.dtype), pltpu.SemaphoreType.DMA((chunks,))],
        input_output_aliases={2: 0} if before else {},
        compiler_params=pltpu.CompilerParams(vmem_limit_bytes=16 * 1024 * 1024),
        cost_estimate=pl.CostEstimate(flops=0, bytes_accessed=0, transcendentals=0),
        name=name,
    )(arrived, late, *before)


def body(image_emb, text_emb, text_accum, pair_ids, log_scale, bias):
    count = lax.axis_size(AXES)
    rows, width = image_emb.shape
    half = rows // 2
    f32, bf16 = jnp.float32, jnp.bfloat16
    flags = (lax.axis_index("group") % 2).astype(jnp.int32).reshape(1)
    params = jnp.concatenate([log_scale, bias])
    ids = pair_ids.reshape(1, rows)

    skip = [(i, (i + 2) % count) for i in range(count)]
    swap = [(i, i ^ 1) for i in range(count)]

    def ahead(value):
        return lax.ppermute(value, AXES, skip)

    def across(value):
        return lax.ppermute(value, AXES, swap)

    (text,) = call(cast_kernel, "cast", [((rows, width), bf16)], (), text_emb)
    far = ahead(text)

    image_a, image_b = pl.pallas_call(
        load_kernel,
        out_shape=[jax.ShapeDtypeStruct((n, width), bf16) for n in (half, rows - half)],
        in_specs=[ANY, HBM],
        out_specs=[VMEM] * 2,
        scratch_shapes=[pltpu.SemaphoreType.DMA((2,))],
        compiler_params=pltpu.CompilerParams(vmem_limit_bytes=16 * 1024 * 1024),
        cost_estimate=pl.CostEstimate(flops=0, bytes_accessed=0, transcendentals=0),
        name="load",
    )(text, pltpu.with_memory_space_constraint(image_emb, pltpu.HBM))
    mate_a, mate_b = across(image_a), across(image_b)
    mate_ids = across(ids)
    both_ids = ahead(jnp.concatenate([ids, mate_ids]))

    cut = rows - rows * 3 // 16
    out_a, out_b, image_sum, loss = pl.pallas_call(
        own_kernel,
        out_shape=[
            jax.ShapeDtypeStruct((cut, width), bf16),
            jax.ShapeDtypeStruct((rows - cut, width), bf16),
            jax.ShapeDtypeStruct((rows, width), f32),
            jax.ShapeDtypeStruct((1, rows), f32),
        ],
        in_specs=[SMEM] * 2 + [VMEM] * 7 + [HBM],
        out_specs=[VMEM] * 4,
        scratch_shapes=[pltpu.VMEM((rows, width), f32), pltpu.SemaphoreType.DMA],
        compiler_params=pltpu.CompilerParams(vmem_limit_bytes=16 * 1024 * 1024),
        cost_estimate=pl.CostEstimate(flops=0, bytes_accessed=0, transcendentals=0),
        name="own",
    )(flags, params, ids, mate_ids, image_a, image_b, mate_a, mate_b, text,
      pltpu.with_memory_space_constraint(text_accum, pltpu.HBM))
    arrived_a, arrived_b = ahead(out_a), ahead(out_b)

    passed_a, passed_b = call(
        relay_kernel, "relay", [((cut - 16, width), bf16), ((rows - cut + 16, width), bf16)],
        (flags,), both_ids, text, far, flops=1 << 30,
    )
    near_a, near_b = across(passed_a), across(passed_b)
    late, image_sum, loss = call(
        far_kernel, "far", [((rows, width), f32), ((rows, width), f32), ((1, rows), f32)],
        (flags, params), ids, mate_ids, both_ids, image_a, image_b, mate_a, mate_b, far, image_sum,
        loss,
    )
    image_grad, loss = call(
        near_kernel, "near", [((rows, width), bf16), ((1, rows), f32)],
        (flags, params), ids, mate_ids, both_ids, image_a, image_b, near_a, near_b, image_sum, loss,
    )
    late, image_grad = lax.optimization_barrier((late, image_grad))
    text_grad = add_part("add_a", 0, cut // STEP, arrived_a, late)
    text_grad = add_part("add_b", cut, (rows - cut) // STEP, arrived_b, late, text_grad)
    return (loss.reshape(rows), image_grad, text_grad)


def solution(mesh):
    in_specs = (P(AXES, None), P(AXES, None), P(AXES, None), P(AXES), P(), P())
    out_specs = (P(AXES), P(AXES, None), P(AXES, None))
    return jax.shard_map(body, mesh=mesh, in_specs=in_specs, out_specs=out_specs, check_vma=False)
```

```python
import functools

import jax
import jax.numpy as jnp
from jax import lax
from jax.experimental import pallas as pl
from jax.experimental.pallas import tpu as pltpu
from jax.sharding import PartitionSpec as P

SHIFTS = 2
AXES = ("dp", "group")
STEP = 16
VMEM = pl.BlockSpec(memory_space=pltpu.VMEM)
SMEM = pl.BlockSpec(memory_space=pltpu.SMEM)
ANY = pl.BlockSpec(memory_space=pl.ANY)
HBM = pl.BlockSpec(memory_space=pltpu.HBM)


def dot(a, b, contract):
    return lax.dot_general(a, b, ((contract[:1], contract[1:]), ((), ())), preferred_element_type=jnp.float32)


def pair(images, texts, image_ids, text_ids, params):
    raw = dot(images, texts, (1, 1))
    rows = raw.shape[0]
    scale = jnp.exp(jnp.full((1, rows), params[0], jnp.float32))
    logits = scale * raw + params[1]
    same = jnp.broadcast_to(image_ids, (rows, rows)).T == text_ids
    margin = jnp.where(same, -logits, logits)
    tail = jnp.exp(-jnp.abs(margin))
    loss = jnp.maximum(margin, 0.0) + jnp.log1p(tail)
    sigmoid = jnp.where(margin >= 0, 1.0, tail) / (1.0 + tail)
    coef = jnp.where(same, -sigmoid, sigmoid) * scale
    return jnp.sum(loss.T, axis=0, keepdims=True), coef


def whole(a, b):
    return jnp.concatenate([a[...], b[...]], axis=0)


def low(coef):
    return coef.astype(jnp.bfloat16)


def fetch(image, out_a, out_b, sems):
    half = out_a.shape[0]
    copies = [
        pltpu.make_async_copy(image.at[pl.ds(0, half)], out_a, sems.at[0]),
        pltpu.make_async_copy(image.at[pl.ds(half, half)], out_b, sems.at[1]),
    ]
    for copy in copies:
        copy.start()
    for copy in copies:
        copy.wait()


def cast_kernel(flags, text, image, out, image_a, image_b, sems):
    out[...] = text[...].astype(out.dtype)

    @pl.when(flags[0] == 1)
    def _():
        fetch(image, image_a, image_b, sems)


def load_kernel(flags, early_a, early_b, image, image_a, image_b, sems):
    @pl.when(flags[0] == 0)
    def _():
        fetch(image, image_a, image_b, sems)

    @pl.when(flags[0] == 1)
    def _():
        image_a[...] = early_a[...]
        image_b[...] = early_b[...]


def add_kernel(start, chunks, arrived, late, *refs):
    out, staged, sems = refs[-3:]
    step = arrived.shape[0] // chunks
    copies = []
    for k in range(chunks):
        here, there = pl.ds(k * step, step), pl.ds(start + k * step, step)
        staged[here, :] = arrived[here, :].astype(staged.dtype) + late[there, :]
        copies.append(pltpu.make_async_copy(staged.at[here], out.at[there], sems.at[k]))
        copies[-1].start()
    for copy in copies:
        copy.wait()


def own_kernel(flags, params, ids, mate_ids, image_a, image_b, mate_a, mate_b, text, accum_in, out_a, out_b, image_sum, loss,
               accum, sem):
    copy = pltpu.make_async_copy(accum_in, accum, sem)
    copy.start()
    image = whole(image_a, image_b)
    own_loss, coef = pair(image, text[...], ids[...], ids[...], params)
    loss[...] = own_loss
    copy.wait()
    total = accum[...] + dot(low(coef.T), image, (1, 0))
    cut = out_a.shape[0]

    def give(value):
        out_a[...] = value[:cut, :].astype(out_a.dtype)
        out_b[...] = value[cut:, :].astype(out_b.dtype)

    @pl.when(flags[0] == 0)
    def _():
        mate = whole(mate_a, mate_b)
        _, mate_coef = pair(mate, text[...], mate_ids[...], ids[...], params)
        give(total + dot(low(mate_coef.T), mate, (1, 0)))

    @pl.when(flags[0] == 1)
    def _():
        give(total)

    image_sum[...] = dot(low(coef), text[...], (1, 0))


def relay_kernel(flags, token, text, far, out_a, out_b):
    cut = out_a.shape[0]

    def fill(source):
        out_a[...] = source[:cut, :]
        out_b[...] = source[cut:, :]

    pl.when(flags[0] == 0)(lambda: fill(text))
    pl.when(flags[0] == 1)(lambda: fill(far))


def far_kernel(flags, params, ids, mate_ids, both_ids, image_a, image_b, mate_a, mate_b, far, image_in,
               loss_in, late, image_sum, loss):
    image = whole(image_a, image_b)
    more, coef = pair(image, far[...], ids[...], both_ids[:1, :], params)
    loss[...] = loss_in[...] + more
    image_sum[...] = image_in[...] + dot(low(coef), far[...], (1, 0))
    part = dot(low(coef.T), image, (1, 0))

    @pl.when(flags[0] == 0)
    def _():
        late[...] = part

    @pl.when(flags[0] == 1)
    def _():
        mate = whole(mate_a, mate_b)
        _, mate_coef = pair(mate, far[...], mate_ids[...], both_ids[:1, :], params)
        late[...] = part + dot(low(mate_coef.T), mate, (1, 0))


def near_kernel(flags, params, ids, mate_ids, both_ids, image_a, image_b, near_a, near_b, image_in, loss_in,
                image_grad, loss):
    image = whole(image_a, image_b)
    near_ids = jnp.where(flags[0] == 0, both_ids[1:, :], mate_ids[...])
    near = whole(near_a, near_b)
    more, coef = pair(image, near, ids[...], near_ids, params)
    loss[...] = (loss_in[...] + more) * (1.0 / ((SHIFTS + 1) * image.shape[0]))
    image_grad[...] = (image_in[...] + dot(low(coef), near, (1, 0))).astype(image_grad.dtype)


def call(kernel, name, outs, scalars, *operands, flops=0):
    return pl.pallas_call(
        kernel,
        out_shape=[jax.ShapeDtypeStruct(s, d) for s, d in outs],
        in_specs=[SMEM] * len(scalars) + [VMEM] * len(operands),
        out_specs=[VMEM] * len(outs),
        compiler_params=pltpu.CompilerParams(vmem_limit_bytes=16 * 1024 * 1024),
        cost_estimate=pl.CostEstimate(flops=flops, bytes_accessed=0, transcendentals=0),
        name=name,
    )(*scalars, *operands)


def add_part(name, start, chunks, arrived, late, *before):
    return pl.pallas_call(
        functools.partial(add_kernel, start, chunks),
        out_shape=jax.ShapeDtypeStruct(late.shape, late.dtype),
        in_specs=[VMEM, VMEM] + [HBM] * len(before),
        out_specs=HBM,
        scratch_shapes=[pltpu.VMEM(arrived.shape, late.dtype), pltpu.SemaphoreType.DMA((chunks,))],
        input_output_aliases={2: 0} if before else {},
        compiler_params=pltpu.CompilerParams(vmem_limit_bytes=16 * 1024 * 1024),
        cost_estimate=pl.CostEstimate(flops=0, bytes_accessed=0, transcendentals=0),
        name=name,
    )(arrived, late, *before)


def body(image_emb, text_emb, text_accum, pair_ids, log_scale, bias):
    count = lax.axis_size(AXES)
    rows, width = image_emb.shape
    half = rows // 2
    f32, bf16 = jnp.float32, jnp.bfloat16
    flags = (lax.axis_index("group") % 2).astype(jnp.int32).reshape(1)
    params = jnp.concatenate([log_scale, bias])
    ids = pair_ids.reshape(1, rows)

    skip = [(i, (i + 2) % count) for i in range(count)]
    swap = [(i, i ^ 1) for i in range(count)]

    def ahead(value):
        return lax.ppermute(value, AXES, skip)

    def across(value):
        return lax.ppermute(value, AXES, swap)

    fixed_image = pltpu.with_memory_space_constraint(image_emb, pltpu.HBM)
    halves = [jax.ShapeDtypeStruct((n, width), bf16) for n in (half, rows - half)]
    text, early_a, early_b = pl.pallas_call(
        cast_kernel,
        out_shape=[jax.ShapeDtypeStruct((rows, width), bf16)] + halves,
        in_specs=[SMEM, VMEM, HBM],
        out_specs=[VMEM] * 3,
        scratch_shapes=[pltpu.SemaphoreType.DMA((2,))],
        compiler_params=pltpu.CompilerParams(vmem_limit_bytes=16 * 1024 * 1024),
        cost_estimate=pl.CostEstimate(flops=0, bytes_accessed=0, transcendentals=0),
        name="cast",
    )(flags, text_emb, fixed_image)
    far = ahead(text)

    image_a, image_b = pl.pallas_call(
        load_kernel,
        out_shape=halves,
        in_specs=[SMEM, VMEM, VMEM, HBM],
        out_specs=[VMEM] * 2,
        scratch_shapes=[pltpu.SemaphoreType.DMA((2,))],
        compiler_params=pltpu.CompilerParams(vmem_limit_bytes=16 * 1024 * 1024),
        cost_estimate=pl.CostEstimate(flops=0, bytes_accessed=0, transcendentals=0),
        name="load",
    )(flags, early_a, early_b, fixed_image)
    mate_a, mate_b = across(image_a), across(image_b)
    mate_ids = across(ids)
    both_ids = ahead(jnp.concatenate([ids, mate_ids]))

    cut = rows - rows * 3 // 16
    out_a, out_b, image_sum, loss = pl.pallas_call(
        own_kernel,
        out_shape=[
            jax.ShapeDtypeStruct((cut, width), bf16),
            jax.ShapeDtypeStruct((rows - cut, width), bf16),
            jax.ShapeDtypeStruct((rows, width), f32),
            jax.ShapeDtypeStruct((1, rows), f32),
        ],
        in_specs=[SMEM] * 2 + [VMEM] * 7 + [HBM],
        out_specs=[VMEM] * 4,
        scratch_shapes=[pltpu.VMEM((rows, width), f32), pltpu.SemaphoreType.DMA],
        compiler_params=pltpu.CompilerParams(vmem_limit_bytes=16 * 1024 * 1024),
        cost_estimate=pl.CostEstimate(flops=0, bytes_accessed=0, transcendentals=0),
        name="own",
    )(flags, params, ids, mate_ids, image_a, image_b, mate_a, mate_b, text,
      pltpu.with_memory_space_constraint(text_accum, pltpu.HBM))
    arrived_a, arrived_b = ahead(out_a), ahead(out_b)

    passed_a, passed_b = call(
        relay_kernel, "relay", [((cut - 16, width), bf16), ((rows - cut + 16, width), bf16)],
        (flags,), both_ids, text, far, flops=1 << 30,
    )
    near_a, near_b = across(passed_a), across(passed_b)
    late, image_sum, loss = call(
        far_kernel, "far", [((rows, width), f32), ((rows, width), f32), ((1, rows), f32)],
        (flags, params), ids, mate_ids, both_ids, image_a, image_b, mate_a, mate_b, far, image_sum,
        loss,
    )
    image_grad, loss = call(
        near_kernel, "near", [((rows, width), bf16), ((1, rows), f32)],
        (flags, params), ids, mate_ids, both_ids, image_a, image_b, near_a, near_b, image_sum, loss,
    )
    late, image_grad = lax.optimization_barrier((late, image_grad))
    text_grad = add_part("add_a", 0, cut // STEP, arrived_a, late)
    text_grad = add_part("add_b", cut, (rows - cut) // STEP, arrived_b, late, text_grad)
    return (loss.reshape(rows), image_grad, text_grad)


def solution(mesh):
    in_specs = (P(AXES, None), P(AXES, None), P(AXES, None), P(AXES), P(), P())
    out_specs = (P(AXES), P(AXES, None), P(AXES, None))
    return jax.shard_map(body, mesh=mesh, in_specs=in_specs, out_specs=out_specs, check_vma=False)
```

```python
import functools

import jax
import jax.numpy as jnp
from jax import lax
from jax.experimental import pallas as pl
from jax.experimental.pallas import tpu as pltpu
from jax.sharding import PartitionSpec as P

SHIFTS = 2
AXES = ("dp", "group")
STEP = 16
VMEM = pl.BlockSpec(memory_space=pltpu.VMEM)
SMEM = pl.BlockSpec(memory_space=pltpu.SMEM)
ANY = pl.BlockSpec(memory_space=pl.ANY)
HBM = pl.BlockSpec(memory_space=pltpu.HBM)


def dot(a, b, contract):
    return lax.dot_general(a, b, ((contract[:1], contract[1:]), ((), ())), preferred_element_type=jnp.float32)


def pair(images, texts, image_ids, text_ids, params):
    raw = dot(images, texts, (1, 1))
    rows = raw.shape[0]
    scale = jnp.exp(jnp.full((1, rows), params[0], jnp.float32))
    logits = scale * raw + params[1]
    same = jnp.broadcast_to(image_ids, (rows, rows)).T == text_ids
    margin = jnp.where(same, -logits, logits)
    tail = jnp.exp(-jnp.abs(margin))
    loss = jnp.maximum(margin, 0.0) + jnp.log1p(tail)
    sigmoid = jnp.where(margin >= 0, 1.0, tail) / (1.0 + tail)
    coef = jnp.where(same, -sigmoid, sigmoid) * scale
    return jnp.sum(loss.T, axis=0, keepdims=True), coef


def whole(a, b):
    return jnp.concatenate([a[...], b[...]], axis=0)


def low(coef):
    return coef.astype(jnp.bfloat16)


def cast_kernel(text, out):
    out[...] = text[...].astype(out.dtype)


def load_kernel(text, image, out_a, out_b, sems):
    half = out_a.shape[0]
    copies = [
        pltpu.make_async_copy(image.at[pl.ds(0, half)], out_a, sems.at[0]),
        pltpu.make_async_copy(image.at[pl.ds(half, half)], out_b, sems.at[1]),
    ]
    for copy in copies:
        copy.start()
    for copy in copies:
        copy.wait()


def add_kernel(start, chunks, count, late, *refs):
    arrived, (out, staged, sems) = refs[:count], refs[-3:]
    step = staged.shape[0] // chunks
    copies = []
    for k in range(chunks):
        here, there = pl.ds(k * step, step), pl.ds(start + k * step, step)
        staged[here, :] = sum((part[here, :].astype(staged.dtype) for part in arrived), late[there, :])
        copies.append(pltpu.make_async_copy(staged.at[here], out.at[there], sems.at[k]))
        copies[-1].start()
    for copy in copies:
        copy.wait()


def own_kernel(flags, params, ids, mate_ids, image_a, image_b, mate_a, mate_b, text, accum_in, out_a, out_b, image_sum, loss,
               accum, sem):
    copy = pltpu.make_async_copy(accum_in, accum, sem)
    copy.start()
    image = whole(image_a, image_b)
    own_loss, coef = pair(image, text[...], ids[...], ids[...], params)
    loss[...] = own_loss
    copy.wait()
    total = accum[...] + dot(low(coef.T), image, (1, 0))
    cut = out_a.shape[0]

    def give(value):
        out_a[...] = value[:cut, :].astype(out_a.dtype)
        out_b[...] = value[cut:, :].astype(out_b.dtype)

    @pl.when(flags[0] == 0)
    def _():
        mate = whole(mate_a, mate_b)
        _, mate_coef = pair(mate, text[...], mate_ids[...], ids[...], params)
        give(total + dot(low(mate_coef.T), mate, (1, 0)))

    @pl.when(flags[0] == 1)
    def _():
        give(total)

    image_sum[...] = dot(low(coef), text[...], (1, 0))


def ids_kernel(token, both_ids, out):
    out[...] = both_ids[...]


def relay_kernel(flags, token, leg, text, far, out_a, out_b):
    cut = out_a.shape[0]

    def fill(source):
        out_a[...] = source[:cut, :]
        out_b[...] = source[cut:, :]

    pl.when(flags[0] == 0)(lambda: fill(text))
    pl.when(flags[0] == 1)(lambda: fill(far))


def far_kernel(flags, params, ids, mate_ids, both_ids, image_a, image_b, mate_a, mate_b, far, image_in,
               loss_in, late, image_sum, loss):
    image = whole(image_a, image_b)
    more, coef = pair(image, far[...], ids[...], both_ids[:1, :], params)
    loss[...] = loss_in[...] + more
    image_sum[...] = image_in[...] + dot(low(coef), far[...], (1, 0))
    part = dot(low(coef.T), image, (1, 0))

    @pl.when(flags[0] == 0)
    def _():
        late[...] = part

    @pl.when(flags[0] == 1)
    def _():
        mate = whole(mate_a, mate_b)
        _, mate_coef = pair(mate, far[...], mate_ids[...], both_ids[:1, :], params)
        late[...] = part + dot(low(mate_coef.T), mate, (1, 0))


def near_kernel(flags, params, ids, mate_ids, both_ids, image_a, image_b, near_a, near_b, image_in, loss_in,
                image_grad, loss):
    image = whole(image_a, image_b)
    near_ids = jnp.where(flags[0] == 0, both_ids[1:, :], mate_ids[...])
    near = whole(near_a, near_b)
    more, coef = pair(image, near, ids[...], near_ids, params)
    loss[...] = (loss_in[...] + more) * (1.0 / ((SHIFTS + 1) * image.shape[0]))
    image_grad[...] = (image_in[...] + dot(low(coef), near, (1, 0))).astype(image_grad.dtype)


def call(kernel, name, outs, scalars, *operands, flops=0):
    return pl.pallas_call(
        kernel,
        out_shape=[jax.ShapeDtypeStruct(s, d) for s, d in outs],
        in_specs=[SMEM] * len(scalars) + [VMEM] * len(operands),
        out_specs=[VMEM] * len(outs),
        compiler_params=pltpu.CompilerParams(vmem_limit_bytes=16 * 1024 * 1024),
        cost_estimate=pl.CostEstimate(flops=flops, bytes_accessed=0, transcendentals=0),
        name=name,
    )(*scalars, *operands)


def add_part(name, start, chunks, late, arrived, *before):
    return pl.pallas_call(
        functools.partial(add_kernel, start, chunks, len(arrived)),
        out_shape=jax.ShapeDtypeStruct(late.shape, late.dtype),
        in_specs=[VMEM] * (1 + len(arrived)) + [HBM] * len(before),
        out_specs=HBM,
        scratch_shapes=[pltpu.VMEM(arrived[0].shape, late.dtype), pltpu.SemaphoreType.DMA((chunks,))],
        input_output_aliases={1 + len(arrived): 0} if before else {},
        compiler_params=pltpu.CompilerParams(vmem_limit_bytes=16 * 1024 * 1024),
        cost_estimate=pl.CostEstimate(flops=0, bytes_accessed=0, transcendentals=0),
        name=name,
    )(late, *arrived, *before)


def body(image_emb, text_emb, text_accum, pair_ids, log_scale, bias):
    count = lax.axis_size(AXES)
    rows, width = image_emb.shape
    half = rows // 2
    f32, bf16 = jnp.float32, jnp.bfloat16
    flags = (lax.axis_index("group") % 2).astype(jnp.int32).reshape(1)
    params = jnp.concatenate([log_scale, bias])
    ids = pair_ids.reshape(1, rows)

    skip = [(i, (i + 2) % count) for i in range(count)]
    swap = [(i, i ^ 1) for i in range(count)]

    def ahead(value):
        return lax.ppermute(value, AXES, skip)

    def across(value):
        return lax.ppermute(value, AXES, swap)

    (text,) = call(cast_kernel, "cast", [((rows, width), bf16)], (), text_emb)
    far = ahead(text)

    image_a, image_b = pl.pallas_call(
        load_kernel,
        out_shape=[jax.ShapeDtypeStruct((n, width), bf16) for n in (half, rows - half)],
        in_specs=[ANY, HBM],
        out_specs=[VMEM] * 2,
        scratch_shapes=[pltpu.SemaphoreType.DMA((2,))],
        compiler_params=pltpu.CompilerParams(vmem_limit_bytes=16 * 1024 * 1024),
        cost_estimate=pl.CostEstimate(flops=0, bytes_accessed=0, transcendentals=0),
        name="load",
    )(text, pltpu.with_memory_space_constraint(image_emb, pltpu.HBM))
    mate_a, mate_b = across(image_a), across(image_b)
    mate_ids = across(ids)
    both_ids = ahead(jnp.concatenate([ids, mate_ids]))

    cut = rows - rows // 4
    out_a, out_b, image_sum, loss = pl.pallas_call(
        own_kernel,
        out_shape=[
            jax.ShapeDtypeStruct((cut, width), bf16),
            jax.ShapeDtypeStruct((rows - cut, width), bf16),
            jax.ShapeDtypeStruct((rows, width), f32),
            jax.ShapeDtypeStruct((1, rows), f32),
        ],
        in_specs=[SMEM] * 2 + [VMEM] * 7 + [HBM],
        out_specs=[VMEM] * 4,
        scratch_shapes=[pltpu.VMEM((rows, width), f32), pltpu.SemaphoreType.DMA],
        compiler_params=pltpu.CompilerParams(vmem_limit_bytes=16 * 1024 * 1024),
        cost_estimate=pl.CostEstimate(flops=0, bytes_accessed=0, transcendentals=0),
        name="own",
    )(flags, params, ids, mate_ids, image_a, image_b, mate_a, mate_b, text,
      pltpu.with_memory_space_constraint(text_accum, pltpu.HBM))
    turn = lax.axis_size("group")
    to_turn = lax.ppermute(out_b, AXES, [(count - 2, turn)])
    turned = lax.ppermute(to_turn, AXES, [(turn, 0)])
    arrived_a = ahead(out_a)
    arrived_b = lax.ppermute(out_b, AXES, skip[:-2] + skip[-1:])

    (both_ids,) = call(ids_kernel, "ids", [((2, rows), jnp.int32)], (), loss, both_ids, flops=2 << 30)
    passed_a, passed_b = call(
        relay_kernel, "relay", [((cut - 16, width), bf16), ((rows - cut + 16, width), bf16)],
        (flags,), both_ids, to_turn, text, far, flops=1 << 30,
    )
    near_a, near_b = across(passed_a), across(passed_b)
    late, image_sum, loss = call(
        far_kernel, "far", [((rows, width), f32), ((rows, width), f32), ((1, rows), f32)],
        (flags, params), ids, mate_ids, both_ids, image_a, image_b, mate_a, mate_b, far, image_sum,
        loss,
    )
    image_grad, loss = call(
        near_kernel, "near", [((rows, width), bf16), ((1, rows), f32)],
        (flags, params), ids, mate_ids, both_ids, image_a, image_b, near_a, near_b, image_sum, loss,
    )
    late, image_grad = lax.optimization_barrier((late, image_grad))
    text_grad = add_part("add_a", 0, cut // STEP, late, (arrived_a,))
    text_grad = add_part("add_b", cut, (rows - cut) // STEP, late, (arrived_b, turned), text_grad)
    return (loss.reshape(rows), image_grad, text_grad)


def solution(mesh):
    in_specs = (P(AXES, None), P(AXES, None), P(AXES, None), P(AXES), P(), P())
    out_specs = (P(AXES), P(AXES, None), P(AXES, None))
    return jax.shard_map(body, mesh=mesh, in_specs=in_specs, out_specs=out_specs, check_vma=False)
```

```python
import functools

import jax
import jax.numpy as jnp
from jax import lax
from jax.experimental import pallas as pl
from jax.experimental.pallas import tpu as pltpu
from jax.sharding import PartitionSpec as P

SHIFTS = 2
AXES = ("dp", "group")
STEP = 16
PIECES = 4
VMEM = pl.BlockSpec(memory_space=pltpu.VMEM)
SMEM = pl.BlockSpec(memory_space=pltpu.SMEM)
ANY = pl.BlockSpec(memory_space=pl.ANY)
HBM = pl.BlockSpec(memory_space=pltpu.HBM)


def dot(a, b, contract):
    return lax.dot_general(a, b, ((contract[:1], contract[1:]), ((), ())), preferred_element_type=jnp.float32)


def pair(images, texts, image_ids, text_ids, params):
    raw = dot(images, texts, (1, 1))
    rows = raw.shape[0]
    scale = jnp.exp(jnp.full((1, rows), params[0], jnp.float32))
    logits = scale * raw + params[1]
    same = jnp.broadcast_to(image_ids, (rows, rows)).T == text_ids
    margin = jnp.where(same, -logits, logits)
    tail = jnp.exp(-jnp.abs(margin))
    loss = jnp.maximum(margin, 0.0) + jnp.log1p(tail)
    sigmoid = jnp.where(margin >= 0, 1.0, tail) / (1.0 + tail)
    coef = jnp.where(same, -sigmoid, sigmoid) * scale
    return jnp.sum(loss.T, axis=0, keepdims=True), coef


def whole(*parts):
    return jnp.concatenate([part[...] for part in parts], axis=0)


def low(coef):
    return coef.astype(jnp.bfloat16)


def cast_kernel(text, out):
    out[...] = text[...].astype(out.dtype)


def load_kernel(text, image, out_a, out_b, sems):
    half = out_a.shape[0]
    copies = [
        pltpu.make_async_copy(image.at[pl.ds(0, half)], out_a, sems.at[0]),
        pltpu.make_async_copy(image.at[pl.ds(half, half)], out_b, sems.at[1]),
    ]
    for copy in copies:
        copy.start()
    for copy in copies:
        copy.wait()


def add_kernel(start, chunks, count, late, *refs):
    arrived, (out, staged, sems) = refs[:count], refs[-3:]
    step = staged.shape[0] // chunks
    copies = []
    for k in range(chunks):
        here, there = pl.ds(k * step, step), pl.ds(start + k * step, step)
        staged[here, :] = sum((part[here, :].astype(staged.dtype) for part in arrived), late[there, :])
        copies.append(pltpu.make_async_copy(staged.at[here], out.at[there], sems.at[k]))
        copies[-1].start()
    for copy in copies:
        copy.wait()


def own_kernel(flags, params, ids, mate_ids, image_a, image_b, mate_a, mate_b, text, accum_in, out_a, out_b, image_sum, loss,
               accum, sem):
    copy = pltpu.make_async_copy(accum_in, accum, sem)
    copy.start()
    image = whole(image_a, image_b)
    own_loss, coef = pair(image, text[...], ids[...], ids[...], params)
    loss[...] = own_loss
    copy.wait()
    total = accum[...] + dot(low(coef.T), image, (1, 0))
    cut = out_a.shape[0]

    def give(value):
        out_a[...] = value[:cut, :].astype(out_a.dtype)
        out_b[...] = value[cut:, :].astype(out_b.dtype)

    @pl.when(flags[0] == 0)
    def _():
        mate = whole(mate_a, mate_b)
        _, mate_coef = pair(mate, text[...], mate_ids[...], ids[...], params)
        give(total + dot(low(mate_coef.T), mate, (1, 0)))

    @pl.when(flags[0] == 1)
    def _():
        give(total)

    image_sum[...] = dot(low(coef), text[...], (1, 0))


def ids_kernel(token, both_ids, out):
    out[...] = both_ids[...]


def relay_kernel(flags, token, text, far, *outs):
    step = outs[0].shape[0]

    def fill(source):
        for k, out in enumerate(outs):
            out[...] = source[k * step:(k + 1) * step, :]

    pl.when(flags[0] == 0)(lambda: fill(text))
    pl.when(flags[0] == 1)(lambda: fill(far))


def far_kernel(flags, params, ids, mate_ids, both_ids, image_a, image_b, mate_a, mate_b, far, image_in,
               loss_in, late, image_sum, loss):
    image = whole(image_a, image_b)
    more, coef = pair(image, far[...], ids[...], both_ids[:1, :], params)
    loss[...] = loss_in[...] + more
    image_sum[...] = image_in[...] + dot(low(coef), far[...], (1, 0))
    part = dot(low(coef.T), image, (1, 0))

    @pl.when(flags[0] == 0)
    def _():
        late[...] = part

    @pl.when(flags[0] == 1)
    def _():
        mate = whole(mate_a, mate_b)
        _, mate_coef = pair(mate, far[...], mate_ids[...], both_ids[:1, :], params)
        late[...] = part + dot(low(mate_coef.T), mate, (1, 0))


def near_kernel(flags, params, ids, mate_ids, both_ids, image_a, image_b, image_in, loss_in, *refs):
    image_grad, loss = refs[PIECES:]
    image = whole(image_a, image_b)
    near_ids = jnp.where(flags[0] == 0, both_ids[1:, :], mate_ids[...])
    near = whole(*refs[:PIECES])
    more, coef = pair(image, near, ids[...], near_ids, params)
    loss[...] = (loss_in[...] + more) * (1.0 / ((SHIFTS + 1) * image.shape[0]))
    image_grad[...] = (image_in[...] + dot(low(coef), near, (1, 0))).astype(image_grad.dtype)


def call(kernel, name, outs, scalars, *operands, flops=0):
    return pl.pallas_call(
        kernel,
        out_shape=[jax.ShapeDtypeStruct(s, d) for s, d in outs],
        in_specs=[SMEM] * len(scalars) + [VMEM] * len(operands),
        out_specs=[VMEM] * len(outs),
        compiler_params=pltpu.CompilerParams(vmem_limit_bytes=16 * 1024 * 1024),
        cost_estimate=pl.CostEstimate(flops=flops, bytes_accessed=0, transcendentals=0),
        name=name,
    )(*scalars, *operands)


def add_part(name, start, chunks, late, arrived, *before):
    return pl.pallas_call(
        functools.partial(add_kernel, start, chunks, len(arrived)),
        out_shape=jax.ShapeDtypeStruct(late.shape, late.dtype),
        in_specs=[VMEM] * (1 + len(arrived)) + [HBM] * len(before),
        out_specs=HBM,
        scratch_shapes=[pltpu.VMEM(arrived[0].shape, late.dtype), pltpu.SemaphoreType.DMA((chunks,))],
        input_output_aliases={1 + len(arrived): 0} if before else {},
        compiler_params=pltpu.CompilerParams(vmem_limit_bytes=16 * 1024 * 1024),
        cost_estimate=pl.CostEstimate(flops=0, bytes_accessed=0, transcendentals=0),
        name=name,
    )(late, *arrived, *before)


def body(image_emb, text_emb, text_accum, pair_ids, log_scale, bias):
    count = lax.axis_size(AXES)
    rows, width = image_emb.shape
    half = rows // 2
    f32, bf16 = jnp.float32, jnp.bfloat16
    flags = (lax.axis_index("group") % 2).astype(jnp.int32).reshape(1)
    params = jnp.concatenate([log_scale, bias])
    ids = pair_ids.reshape(1, rows)

    skip = [(i, (i + 2) % count) for i in range(count)]
    swap = [(i, i ^ 1) for i in range(count)]

    def ahead(value):
        return lax.ppermute(value, AXES, skip)

    def across(value):
        return lax.ppermute(value, AXES, swap)

    (text,) = call(cast_kernel, "cast", [((rows, width), bf16)], (), text_emb)
    far = ahead(text)

    image_a, image_b = pl.pallas_call(
        load_kernel,
        out_shape=[jax.ShapeDtypeStruct((n, width), bf16) for n in (half, rows - half)],
        in_specs=[ANY, HBM],
        out_specs=[VMEM] * 2,
        scratch_shapes=[pltpu.SemaphoreType.DMA((2,))],
        compiler_params=pltpu.CompilerParams(vmem_limit_bytes=16 * 1024 * 1024),
        cost_estimate=pl.CostEstimate(flops=0, bytes_accessed=0, transcendentals=0),
        name="load",
    )(text, pltpu.with_memory_space_constraint(image_emb, pltpu.HBM))
    mate_a, mate_b = across(image_a), across(image_b)
    mate_ids = across(ids)
    both_ids = ahead(jnp.concatenate([ids, mate_ids]))

    cut = rows - rows * 3 // 8
    out_a, out_b, image_sum, loss = pl.pallas_call(
        own_kernel,
        out_shape=[
            jax.ShapeDtypeStruct((cut, width), bf16),
            jax.ShapeDtypeStruct((rows - cut, width), bf16),
            jax.ShapeDtypeStruct((rows, width), f32),
            jax.ShapeDtypeStruct((1, rows), f32),
        ],
        in_specs=[SMEM] * 2 + [VMEM] * 7 + [HBM],
        out_specs=[VMEM] * 4,
        scratch_shapes=[pltpu.VMEM((rows, width), f32), pltpu.SemaphoreType.DMA],
        compiler_params=pltpu.CompilerParams(vmem_limit_bytes=16 * 1024 * 1024),
        cost_estimate=pl.CostEstimate(flops=0, bytes_accessed=0, transcendentals=0),
        name="own",
    )(flags, params, ids, mate_ids, image_a, image_b, mate_a, mate_b, text,
      pltpu.with_memory_space_constraint(text_accum, pltpu.HBM))
    turn = lax.axis_size("group")
    to_turn = lax.ppermute(out_b, AXES, [(count - 2, turn)])
    turned = lax.ppermute(to_turn, AXES, [(turn, 0)])
    arrived_a = ahead(out_a)
    arrived_b = lax.ppermute(out_b, AXES, skip[:-2] + skip[-1:])

    (both_ids,) = call(ids_kernel, "ids", [((2, rows), jnp.int32)], (), loss, both_ids, flops=2 << 30)
    passed = call(
        relay_kernel, "relay", [((rows // PIECES, width), bf16)] * PIECES,
        (flags,), both_ids, text, far, flops=1 << 30,
    )
    near = [across(piece) for piece in passed]
    late, image_sum, loss = call(
        far_kernel, "far", [((rows, width), f32), ((rows, width), f32), ((1, rows), f32)],
        (flags, params), ids, mate_ids, both_ids, image_a, image_b, mate_a, mate_b, far, image_sum,
        loss,
    )
    image_grad, loss = call(
        near_kernel, "near", [((rows, width), bf16), ((1, rows), f32)],
        (flags, params), ids, mate_ids, both_ids, image_a, image_b, image_sum, loss, *near,
    )
    late, image_grad = lax.optimization_barrier((late, image_grad))
    text_grad = add_part("add_b", cut, (rows - cut) // STEP, late, (arrived_b, turned))
    text_grad = add_part("add_a", 0, cut // STEP, late, (arrived_a,), text_grad)
    return (loss.reshape(rows), image_grad, text_grad)


def solution(mesh):
    in_specs = (P(AXES, None), P(AXES, None), P(AXES, None), P(AXES), P(), P())
    out_specs = (P(AXES), P(AXES, None), P(AXES, None))
    return jax.shard_map(body, mesh=mesh, in_specs=in_specs, out_specs=out_specs, check_vma=False)
```

```python
import jax
import jax.numpy as jnp
from jax import lax
from jax.experimental import pallas as pl
from jax.experimental.pallas import tpu as pltpu
from jax.sharding import PartitionSpec as P

SHIFTS = 2
AXES = ("dp", "group")
STEP = 16
VMEM = pl.BlockSpec(memory_space=pltpu.VMEM)
SMEM = pl.BlockSpec(memory_space=pltpu.SMEM)
ANY = pl.BlockSpec(memory_space=pl.ANY)
HBM = pl.BlockSpec(memory_space=pltpu.HBM)


def dot(a, b, contract):
    return lax.dot_general(a, b, ((contract[:1], contract[1:]), ((), ())), preferred_element_type=jnp.float32)


def pair(images, texts, image_ids, text_ids, params):
    raw = dot(images, texts, (1, 1))
    rows = raw.shape[0]
    scale = jnp.exp(jnp.full((1, rows), params[0], jnp.float32))
    logits = scale * raw + params[1]
    same = jnp.broadcast_to(image_ids, (rows, rows)).T == text_ids
    margin = jnp.where(same, -logits, logits)
    tail = jnp.exp(-jnp.abs(margin))
    loss = jnp.maximum(margin, 0.0) + jnp.log1p(tail)
    sigmoid = jnp.where(margin >= 0, 1.0, tail) / (1.0 + tail)
    coef = jnp.where(same, -sigmoid, sigmoid) * scale
    return jnp.sum(loss.T, axis=0, keepdims=True), coef


def whole(a, b):
    return jnp.concatenate([a[...], b[...]], axis=0)


def low(coef):
    return coef.astype(jnp.bfloat16)


def cast_kernel(text, out):
    out[...] = text[...].astype(out.dtype)


def load_kernel(text, image, out_a, out_b, sems):
    half = out_a.shape[0]
    copies = [
        pltpu.make_async_copy(image.at[pl.ds(0, half)], out_a, sems.at[0]),
        pltpu.make_async_copy(image.at[pl.ds(half, half)], out_b, sems.at[1]),
    ]
    for copy in copies:
        copy.start()
    for copy in copies:
        copy.wait()


def add_kernel(first, second, turned, late, out, staged, sems):
    cut = first.shape[0]
    copies = []
    for k in range(out.shape[0] // STEP):
        rows = pl.ds(k * STEP, STEP)
        if k * STEP < cut:
            arrived = first[rows, :].astype(staged.dtype)
        else:
            part = pl.ds(k * STEP - cut, STEP)
            arrived = second[part, :].astype(staged.dtype) + turned[part, :].astype(staged.dtype)
        staged[rows, :] = arrived + late[rows, :]
        copies.append(pltpu.make_async_copy(staged.at[rows], out.at[rows], sems.at[k]))
        copies[-1].start()
    for copy in copies:
        copy.wait()


def own_kernel(flags, params, ids, mate_ids, image_a, image_b, mate_a, mate_b, text, accum_in, out_a, out_b, image_sum, loss,
               accum, sem):
    copy = pltpu.make_async_copy(accum_in, accum, sem)
    copy.start()
    image = whole(image_a, image_b)
    own_loss, coef = pair(image, text[...], ids[...], ids[...], params)
    loss[...] = own_loss
    copy.wait()
    total = accum[...] + dot(low(coef.T), image, (1, 0))
    cut = out_a.shape[0]

    def give(value):
        out_a[...] = value[:cut, :].astype(out_a.dtype)
        out_b[...] = value[cut:, :].astype(out_b.dtype)

    @pl.when(flags[0] == 0)
    def _():
        mate = whole(mate_a, mate_b)
        _, mate_coef = pair(mate, text[...], mate_ids[...], ids[...], params)
        give(total + dot(low(mate_coef.T), mate, (1, 0)))

    @pl.when(flags[0] == 1)
    def _():
        give(total)

    image_sum[...] = dot(low(coef), text[...], (1, 0))


def ids_kernel(token, both_ids, out):
    out[...] = both_ids[...]


def relay_kernel(flags, token, leg, text, far, out_a, out_b):
    cut = out_a.shape[0]

    def fill(source):
        out_a[...] = source[:cut, :]
        out_b[...] = source[cut:, :]

    pl.when(flags[0] == 0)(lambda: fill(text))
    pl.when(flags[0] == 1)(lambda: fill(far))


def far_kernel(flags, params, ids, mate_ids, both_ids, image_a, image_b, mate_a, mate_b, far, image_in,
               loss_in, late, image_sum, loss):
    image = whole(image_a, image_b)
    more, coef = pair(image, far[...], ids[...], both_ids[:1, :], params)
    loss[...] = loss_in[...] + more
    image_sum[...] = image_in[...] + dot(low(coef), far[...], (1, 0))
    part = dot(low(coef.T), image, (1, 0))

    @pl.when(flags[0] == 0)
    def _():
        late[...] = part

    @pl.when(flags[0] == 1)
    def _():
        mate = whole(mate_a, mate_b)
        _, mate_coef = pair(mate, far[...], mate_ids[...], both_ids[:1, :], params)
        late[...] = part + dot(low(mate_coef.T), mate, (1, 0))


def near_kernel(flags, params, ids, mate_ids, both_ids, image_a, image_b, near_a, near_b, image_in, loss_in,
                image_grad, loss):
    image = whole(image_a, image_b)
    near_ids = jnp.where(flags[0] == 0, both_ids[1:, :], mate_ids[...])
    near = whole(near_a, near_b)
    more, coef = pair(image, near, ids[...], near_ids, params)
    loss[...] = (loss_in[...] + more) * (1.0 / ((SHIFTS + 1) * image.shape[0]))
    image_grad[...] = (image_in[...] + dot(low(coef), near, (1, 0))).astype(image_grad.dtype)


def call(kernel, name, outs, scalars, *operands, flops=0):
    return pl.pallas_call(
        kernel,
        out_shape=[jax.ShapeDtypeStruct(s, d) for s, d in outs],
        in_specs=[SMEM] * len(scalars) + [VMEM] * len(operands),
        out_specs=[VMEM] * len(outs),
        compiler_params=pltpu.CompilerParams(vmem_limit_bytes=16 * 1024 * 1024),
        cost_estimate=pl.CostEstimate(flops=flops, bytes_accessed=0, transcendentals=0),
        name=name,
    )(*scalars, *operands)


def body(image_emb, text_emb, text_accum, pair_ids, log_scale, bias):
    count = lax.axis_size(AXES)
    rows, width = image_emb.shape
    half = rows // 2
    f32, bf16 = jnp.float32, jnp.bfloat16
    flags = (lax.axis_index("group") % 2).astype(jnp.int32).reshape(1)
    params = jnp.concatenate([log_scale, bias])
    ids = pair_ids.reshape(1, rows)

    skip = [(i, (i + 2) % count) for i in range(count)]
    swap = [(i, i ^ 1) for i in range(count)]

    def ahead(value):
        return lax.ppermute(value, AXES, skip)

    def across(value):
        return lax.ppermute(value, AXES, swap)

    (text,) = call(cast_kernel, "cast", [((rows, width), bf16)], (), text_emb)
    far = ahead(text)

    image_a, image_b = pl.pallas_call(
        load_kernel,
        out_shape=[jax.ShapeDtypeStruct((n, width), bf16) for n in (half, rows - half)],
        in_specs=[ANY, HBM],
        out_specs=[VMEM] * 2,
        scratch_shapes=[pltpu.SemaphoreType.DMA((2,))],
        compiler_params=pltpu.CompilerParams(vmem_limit_bytes=16 * 1024 * 1024),
        cost_estimate=pl.CostEstimate(flops=0, bytes_accessed=0, transcendentals=0),
        name="load",
    )(text, pltpu.with_memory_space_constraint(image_emb, pltpu.HBM))
    mate_a, mate_b = across(image_a), across(image_b)
    mate_ids = across(ids)
    both_ids = ahead(jnp.concatenate([ids, mate_ids]))

    cut = rows - rows * 3 // 16
    out_a, out_b, image_sum, loss = pl.pallas_call(
        own_kernel,
        out_shape=[
            jax.ShapeDtypeStruct((cut, width), bf16),
            jax.ShapeDtypeStruct((rows - cut, width), bf16),
            jax.ShapeDtypeStruct((rows, width), f32),
            jax.ShapeDtypeStruct((1, rows), f32),
        ],
        in_specs=[SMEM] * 2 + [VMEM] * 7 + [HBM],
        out_specs=[VMEM] * 4,
        scratch_shapes=[pltpu.VMEM((rows, width), f32), pltpu.SemaphoreType.DMA],
        compiler_params=pltpu.CompilerParams(vmem_limit_bytes=16 * 1024 * 1024),
        cost_estimate=pl.CostEstimate(flops=0, bytes_accessed=0, transcendentals=0),
        name="own",
    )(flags, params, ids, mate_ids, image_a, image_b, mate_a, mate_b, text,
      pltpu.with_memory_space_constraint(text_accum, pltpu.HBM))
    turn = lax.axis_size("group")
    to_turn = lax.ppermute(out_b, AXES, [(count - 2, turn)])
    turned = lax.ppermute(to_turn, AXES, [(turn, 0)])
    arrived_a = ahead(out_a)
    arrived_b = lax.ppermute(out_b, AXES, skip[:-2] + skip[-1:])

    (both_ids,) = call(ids_kernel, "ids", [((2, rows), jnp.int32)], (), loss, both_ids, flops=2 << 30)
    passed_a, passed_b = call(
        relay_kernel, "relay", [((cut - 16, width), bf16), ((rows - cut + 16, width), bf16)],
        (flags,), both_ids, to_turn, text, far, flops=1 << 30,
    )
    near_a, near_b = across(passed_a), across(passed_b)
    late, image_sum, loss = call(
        far_kernel, "far", [((rows, width), f32), ((rows, width), f32), ((1, rows), f32)],
        (flags, params), ids, mate_ids, both_ids, image_a, image_b, mate_a, mate_b, far, image_sum,
        loss,
    )
    image_grad, loss = call(
        near_kernel, "near", [((rows, width), bf16), ((1, rows), f32)],
        (flags, params), ids, mate_ids, both_ids, image_a, image_b, near_a, near_b, image_sum, loss,
    )
    late, image_grad = lax.optimization_barrier((late, image_grad))
    text_grad = pl.pallas_call(
        add_kernel,
        out_shape=jax.ShapeDtypeStruct((rows, width), f32),
        in_specs=[VMEM] * 4,
        out_specs=HBM,
        scratch_shapes=[pltpu.VMEM((rows, width), f32), pltpu.SemaphoreType.DMA((rows // STEP,))],
        compiler_params=pltpu.CompilerParams(vmem_limit_bytes=16 * 1024 * 1024),
        cost_estimate=pl.CostEstimate(flops=0, bytes_accessed=0, transcendentals=0),
        name="add",
    )(arrived_a, arrived_b, turned, late)
    return (loss.reshape(rows), image_grad, text_grad)


def solution(mesh):
    in_specs = (P(AXES, None), P(AXES, None), P(AXES, None), P(AXES), P(), P())
    out_specs = (P(AXES), P(AXES, None), P(AXES, None))
    return jax.shard_map(body, mesh=mesh, in_specs=in_specs, out_specs=out_specs, check_vma=False)
```

```python
import functools

import jax
import jax.numpy as jnp
from jax import lax
from jax.experimental import pallas as pl
from jax.experimental.pallas import tpu as pltpu
from jax.sharding import PartitionSpec as P

SHIFTS = 2
AXES = ("dp", "group")
STEP = 16
VMEM = pl.BlockSpec(memory_space=pltpu.VMEM)
SMEM = pl.BlockSpec(memory_space=pltpu.SMEM)
ANY = pl.BlockSpec(memory_space=pl.ANY)
HBM = pl.BlockSpec(memory_space=pltpu.HBM)


def dot(a, b, contract):
    return lax.dot_general(a, b, ((contract[:1], contract[1:]), ((), ())), preferred_element_type=jnp.float32)


def pair(images, texts, image_ids, text_ids, params):
    raw = dot(images, texts, (1, 1))
    rows = raw.shape[0]
    scale = jnp.exp(jnp.full((1, rows), params[0], jnp.float32))
    logits = scale * raw + params[1]
    same = jnp.broadcast_to(image_ids, (rows, rows)).T == text_ids
    margin = jnp.where(same, -logits, logits)
    tail = jnp.exp(-jnp.abs(margin))
    loss = jnp.maximum(margin, 0.0) + jnp.log1p(tail)
    sigmoid = jnp.where(margin >= 0, 1.0, tail) / (1.0 + tail)
    coef = jnp.where(same, -sigmoid, sigmoid) * scale
    return jnp.sum(loss.T, axis=0, keepdims=True), coef


def whole(a, b):
    return jnp.concatenate([a[...], b[...]], axis=0)


def low(coef):
    return coef.astype(jnp.bfloat16)


def cast_kernel(text, out):
    out[...] = text[...].astype(out.dtype)


def load_kernel(text, image, out_a, out_b, sems):
    half = out_a.shape[0]
    copies = [
        pltpu.make_async_copy(image.at[pl.ds(0, half)], out_a, sems.at[0]),
        pltpu.make_async_copy(image.at[pl.ds(half, half)], out_b, sems.at[1]),
    ]
    for copy in copies:
        copy.start()
    for copy in copies:
        copy.wait()


def add_kernel(start, chunks, arrived, late, *refs):
    out, staged, sems = refs[-3:]
    step = arrived.shape[0] // chunks
    copies = []
    for k in range(chunks):
        here, there = pl.ds(k * step, step), pl.ds(start + k * step, step)
        staged[here, :] = arrived[here, :].astype(staged.dtype) + late[there, :]
        copies.append(pltpu.make_async_copy(staged.at[here], out.at[there], sems.at[k]))
        copies[-1].start()
    for copy in copies:
        copy.wait()


def own_kernel(flags, params, ids, mate_ids, image_a, image_b, mate_a, mate_b, text, accum_in, out_a, out_b, image_sum, loss,
               accum, sem):
    copy = pltpu.make_async_copy(accum_in, accum, sem)
    copy.start()
    image = whole(image_a, image_b)
    own_loss, coef = pair(image, text[...], ids[...], ids[...], params)
    loss[...] = own_loss
    copy.wait()
    total = accum[...] + dot(low(coef.T), image, (1, 0))
    cut = out_a.shape[0]

    def give(value):
        out_a[...] = value[:cut, :].astype(out_a.dtype)
        out_b[...] = value[cut:, :].astype(out_b.dtype)

    @pl.when(flags[0] == 0)
    def _():
        mate = whole(mate_a, mate_b)
        _, mate_coef = pair(mate, text[...], mate_ids[...], ids[...], params)
        give(total + dot(low(mate_coef.T), mate, (1, 0)))

    @pl.when(flags[0] == 1)
    def _():
        give(total)

    image_sum[...] = dot(low(coef), text[...], (1, 0))


def ids_kernel(token, both_ids, out):
    out[...] = both_ids[...]


def relay_kernel(flags, token, before, text, far, out_a, out_b):
    cut = out_a.shape[0]

    def fill(source):
        out_a[...] = source[:cut, :]
        out_b[...] = source[cut:, :]

    pl.when(flags[0] == 0)(lambda: fill(text))
    pl.when(flags[0] == 1)(lambda: fill(far))


def far_kernel(flags, params, ids, mate_ids, both_ids, image_a, image_b, mate_a, mate_b, far, image_in,
               loss_in, late, image_sum, loss):
    image = whole(image_a, image_b)
    more, coef = pair(image, far[...], ids[...], both_ids[:1, :], params)
    loss[...] = loss_in[...] + more
    image_sum[...] = image_in[...] + dot(low(coef), far[...], (1, 0))
    part = dot(low(coef.T), image, (1, 0))

    @pl.when(flags[0] == 0)
    def _():
        late[...] = part

    @pl.when(flags[0] == 1)
    def _():
        mate = whole(mate_a, mate_b)
        _, mate_coef = pair(mate, far[...], mate_ids[...], both_ids[:1, :], params)
        late[...] = part + dot(low(mate_coef.T), mate, (1, 0))


def near_kernel(flags, params, ids, mate_ids, both_ids, image_a, image_b, near_a, near_b, image_in, loss_in,
                image_grad, loss):
    image = whole(image_a, image_b)
    near_ids = jnp.where(flags[0] == 0, both_ids[1:, :], mate_ids[...])
    near = whole(near_a, near_b)
    more, coef = pair(image, near, ids[...], near_ids, params)
    loss[...] = (loss_in[...] + more) * (1.0 / ((SHIFTS + 1) * image.shape[0]))
    image_grad[...] = (image_in[...] + dot(low(coef), near, (1, 0))).astype(image_grad.dtype)


def call(kernel, name, outs, scalars, *operands, flops=0):
    return pl.pallas_call(
        kernel,
        out_shape=[jax.ShapeDtypeStruct(s, d) for s, d in outs],
        in_specs=[SMEM] * len(scalars) + [VMEM] * len(operands),
        out_specs=[VMEM] * len(outs),
        compiler_params=pltpu.CompilerParams(vmem_limit_bytes=16 * 1024 * 1024),
        cost_estimate=pl.CostEstimate(flops=flops, bytes_accessed=0, transcendentals=0),
        name=name,
    )(*scalars, *operands)


def add_part(name, start, chunks, arrived, late, *before):
    return pl.pallas_call(
        functools.partial(add_kernel, start, chunks),
        out_shape=jax.ShapeDtypeStruct(late.shape, late.dtype),
        in_specs=[VMEM, VMEM] + [HBM] * len(before),
        out_specs=HBM,
        scratch_shapes=[pltpu.VMEM(arrived.shape, late.dtype), pltpu.SemaphoreType.DMA((chunks,))],
        input_output_aliases={2: 0} if before else {},
        compiler_params=pltpu.CompilerParams(vmem_limit_bytes=16 * 1024 * 1024),
        cost_estimate=pl.CostEstimate(flops=0, bytes_accessed=0, transcendentals=0),
        name=name,
    )(arrived, late, *before)


def body(image_emb, text_emb, text_accum, pair_ids, log_scale, bias):
    count = lax.axis_size(AXES)
    rows, width = image_emb.shape
    half = rows // 2
    f32, bf16 = jnp.float32, jnp.bfloat16
    flags = (lax.axis_index("group") % 2).astype(jnp.int32).reshape(1)
    params = jnp.concatenate([log_scale, bias])
    ids = pair_ids.reshape(1, rows)

    skip = [(i, (i + 2) % count) for i in range(count)]
    swap = [(i, i ^ 1) for i in range(count)]

    def ahead(value):
        return lax.ppermute(value, AXES, skip)

    def across(value):
        return lax.ppermute(value, AXES, swap)

    (text,) = call(cast_kernel, "cast", [((rows, width), bf16)], (), text_emb)
    far = ahead(text)

    image_a, image_b = pl.pallas_call(
        load_kernel,
        out_shape=[jax.ShapeDtypeStruct((n, width), bf16) for n in (half, rows - half)],
        in_specs=[ANY, HBM],
        out_specs=[VMEM] * 2,
        scratch_shapes=[pltpu.SemaphoreType.DMA((2,))],
        compiler_params=pltpu.CompilerParams(vmem_limit_bytes=16 * 1024 * 1024),
        cost_estimate=pl.CostEstimate(flops=0, bytes_accessed=0, transcendentals=0),
        name="load",
    )(text, pltpu.with_memory_space_constraint(image_emb, pltpu.HBM))
    mate_a, mate_b = across(image_a), across(image_b)
    mate_ids = across(ids)
    both_ids = ahead(jnp.concatenate([ids, mate_ids]))

    cut = rows - rows * 3 // 16
    out_a, out_b, image_sum, loss = pl.pallas_call(
        own_kernel,
        out_shape=[
            jax.ShapeDtypeStruct((cut, width), bf16),
            jax.ShapeDtypeStruct((rows - cut, width), bf16),
            jax.ShapeDtypeStruct((rows, width), f32),
            jax.ShapeDtypeStruct((1, rows), f32),
        ],
        in_specs=[SMEM] * 2 + [VMEM] * 7 + [HBM],
        out_specs=[VMEM] * 4,
        scratch_shapes=[pltpu.VMEM((rows, width), f32), pltpu.SemaphoreType.DMA],
        compiler_params=pltpu.CompilerParams(vmem_limit_bytes=16 * 1024 * 1024),
        cost_estimate=pl.CostEstimate(flops=0, bytes_accessed=0, transcendentals=0),
        name="own",
    )(flags, params, ids, mate_ids, image_a, image_b, mate_a, mate_b, text,
      pltpu.with_memory_space_constraint(text_accum, pltpu.HBM))
    crossed = [(i, target ^ 1) for i, target in skip]
    arrived_a = ahead(out_a)
    mate_rows = across(out_b)
    arrived_b = lax.ppermute(mate_rows, AXES, crossed)

    (both_ids,) = call(ids_kernel, "ids", [((2, rows), jnp.int32)], (), loss, both_ids, flops=2 << 30)
    passed_a, passed_b = call(
        relay_kernel, "relay", [((cut - 16, width), bf16), ((rows - cut + 16, width), bf16)],
        (flags,), both_ids, mate_rows, text, far, flops=1 << 30,
    )
    near_a, near_b = across(passed_a), across(passed_b)
    late, image_sum, loss = call(
        far_kernel, "far", [((rows, width), f32), ((rows, width), f32), ((1, rows), f32)],
        (flags, params), ids, mate_ids, both_ids, image_a, image_b, mate_a, mate_b, far, image_sum,
        loss,
    )
    image_grad, loss = call(
        near_kernel, "near", [((rows, width), bf16), ((1, rows), f32)],
        (flags, params), ids, mate_ids, both_ids, image_a, image_b, near_a, near_b, image_sum, loss,
    )
    late, image_grad = lax.optimization_barrier((late, image_grad))
    text_grad = add_part("add_a", 0, cut // STEP, arrived_a, late)
    text_grad = add_part("add_b", cut, (rows - cut) // STEP, arrived_b, late, text_grad)
    return (loss.reshape(rows), image_grad, text_grad)


def solution(mesh):
    in_specs = (P(AXES, None), P(AXES, None), P(AXES, None), P(AXES), P(), P())
    out_specs = (P(AXES), P(AXES, None), P(AXES, None))
    return jax.shard_map(body, mesh=mesh, in_specs=in_specs, out_specs=out_specs, check_vma=False)
```

```python
import functools

import jax
import jax.numpy as jnp
from jax import lax
from jax.experimental import pallas as pl
from jax.experimental.pallas import tpu as pltpu
from jax.sharding import PartitionSpec as P

SHIFTS = 2
AXES = ("dp", "group")
STEP = 16
PIECES = 4
VMEM = pl.BlockSpec(memory_space=pltpu.VMEM)
SMEM = pl.BlockSpec(memory_space=pltpu.SMEM)
ANY = pl.BlockSpec(memory_space=pl.ANY)
HBM = pl.BlockSpec(memory_space=pltpu.HBM)


def dot(a, b, contract):
    return lax.dot_general(a, b, ((contract[:1], contract[1:]), ((), ())), preferred_element_type=jnp.float32)


def pair(images, texts, image_ids, text_ids, params):
    raw = dot(images, texts, (1, 1))
    rows = raw.shape[0]
    scale = jnp.exp(jnp.full((1, rows), params[0], jnp.float32))
    logits = scale * raw + params[1]
    same = jnp.broadcast_to(image_ids, (rows, rows)).T == text_ids
    margin = jnp.where(same, -logits, logits)
    tail = jnp.exp(-jnp.abs(margin))
    loss = jnp.maximum(margin, 0.0) + jnp.log1p(tail)
    sigmoid = jnp.where(margin >= 0, 1.0, tail) / (1.0 + tail)
    coef = jnp.where(same, -sigmoid, sigmoid) * scale
    return jnp.sum(loss.T, axis=0, keepdims=True), coef


def whole(*parts):
    return jnp.concatenate([part[...] for part in parts], axis=0)


def low(coef):
    return coef.astype(jnp.bfloat16)


def cast_kernel(text, out, staged, sem):
    copy = pltpu.make_async_copy(text.at[pl.ds(0, out.shape[0])], staged, sem)
    copy.start()
    copy.wait()
    out[...] = staged[...].astype(out.dtype)


def load_kernel(before, text, image, out, *refs):
    images, (staged, sems) = refs[:-2], refs[-2:]
    step, rest = images[0].shape[0], out.shape[0]
    copies = [pltpu.make_async_copy(text.at[pl.ds(text.shape[0] - rest, rest)], staged, sems.at[PIECES])]
    for k, piece in enumerate(images):
        copies.append(pltpu.make_async_copy(image.at[pl.ds(k * step, step)], piece, sems.at[k]))
    for copy in copies:
        copy.start()
    copies[0].wait()
    out[...] = staged[...].astype(out.dtype)
    for copy in copies[1:]:
        copy.wait()


def add_kernel(start, chunks, arrived, late, *refs):
    out, staged, sems = refs[-3:]
    step = arrived.shape[0] // chunks
    copies = []
    for k in range(chunks):
        here, there = pl.ds(k * step, step), pl.ds(start + k * step, step)
        staged[here, :] = arrived[here, :].astype(staged.dtype) + late[there, :]
        copies.append(pltpu.make_async_copy(staged.at[here], out.at[there], sems.at[k]))
        copies[-1].start()
    for copy in copies:
        copy.wait()


def own_kernel(flags, params, ids, mate_ids, text_a, text_b, accum_in, *refs):
    images, mates = refs[:PIECES], refs[PIECES:2 * PIECES]
    out_a, out_b, image_sum, loss, accum, sem = refs[2 * PIECES:]
    copy = pltpu.make_async_copy(accum_in, accum, sem)
    copy.start()
    image, text = whole(*images), whole(text_a, text_b)
    own_loss, coef = pair(image, text, ids[...], ids[...], params)
    loss[...] = own_loss
    copy.wait()
    total = accum[...] + dot(low(coef.T), image, (1, 0))
    cut = out_a.shape[0]

    def give(value):
        out_a[...] = value[:cut, :].astype(out_a.dtype)
        out_b[...] = value[cut:, :].astype(out_b.dtype)

    @pl.when(flags[0] == 0)
    def _():
        mate = whole(*mates)
        _, mate_coef = pair(mate, text, mate_ids[...], ids[...], params)
        give(total + dot(low(mate_coef.T), mate, (1, 0)))

    @pl.when(flags[0] == 1)
    def _():
        give(total)

    image_sum[...] = dot(low(coef), text, (1, 0))


def ids_kernel(token, both_ids, out):
    out[...] = both_ids[...]


def relay_kernel(flags, token, before, text_a, text_b, far_a, far_b, out_a, out_b):
    cut, top = out_a.shape[0], text_a.shape[0]

    def fill(upper, lower):
        out_a[:top, :] = upper[...]
        out_a[top:, :] = lower[:cut - top, :]
        out_b[...] = lower[cut - top:, :]

    pl.when(flags[0] == 0)(lambda: fill(text_a, text_b))
    pl.when(flags[0] == 1)(lambda: fill(far_a, far_b))


def far_kernel(flags, params, ids, mate_ids, both_ids, far_a, far_b, image_in, loss_in, *refs):
    images, mates = refs[:PIECES], refs[PIECES:2 * PIECES]
    late, image_sum, loss = refs[2 * PIECES:]
    image, far = whole(*images), whole(far_a, far_b)
    more, coef = pair(image, far, ids[...], both_ids[:1, :], params)
    loss[...] = loss_in[...] + more
    image_sum[...] = image_in[...] + dot(low(coef), far, (1, 0))
    part = dot(low(coef.T), image, (1, 0))

    @pl.when(flags[0] == 0)
    def _():
        late[...] = part

    @pl.when(flags[0] == 1)
    def _():
        mate = whole(*mates)
        _, mate_coef = pair(mate, far, mate_ids[...], both_ids[:1, :], params)
        late[...] = part + dot(low(mate_coef.T), mate, (1, 0))


def near_kernel(flags, params, ids, mate_ids, both_ids, near_a, near_b, image_in, loss_in, *refs):
    image_grad, loss = refs[PIECES:]
    image = whole(*refs[:PIECES])
    near_ids = jnp.where(flags[0] == 0, both_ids[1:, :], mate_ids[...])
    near = whole(near_a, near_b)
    more, coef = pair(image, near, ids[...], near_ids, params)
    loss[...] = (loss_in[...] + more) * (1.0 / ((SHIFTS + 1) * image.shape[0]))
    image_grad[...] = (image_in[...] + dot(low(coef), near, (1, 0))).astype(image_grad.dtype)


def call(kernel, name, outs, scalars, *operands, flops=0):
    return pl.pallas_call(
        kernel,
        out_shape=[jax.ShapeDtypeStruct(s, d) for s, d in outs],
        in_specs=[SMEM] * len(scalars) + [VMEM] * len(operands),
        out_specs=[VMEM] * len(outs),
        compiler_params=pltpu.CompilerParams(vmem_limit_bytes=16 * 1024 * 1024),
        cost_estimate=pl.CostEstimate(flops=flops, bytes_accessed=0, transcendentals=0),
        name=name,
    )(*scalars, *operands)


def add_part(name, start, chunks, arrived, late, *before):
    return pl.pallas_call(
        functools.partial(add_kernel, start, chunks),
        out_shape=jax.ShapeDtypeStruct(late.shape, late.dtype),
        in_specs=[VMEM, VMEM] + [HBM] * len(before),
        out_specs=HBM,
        scratch_shapes=[pltpu.VMEM(arrived.shape, late.dtype), pltpu.SemaphoreType.DMA((chunks,))],
        input_output_aliases={2: 0} if before else {},
        compiler_params=pltpu.CompilerParams(vmem_limit_bytes=16 * 1024 * 1024),
        cost_estimate=pl.CostEstimate(flops=0, bytes_accessed=0, transcendentals=0),
        name=name,
    )(arrived, late, *before)


def body(image_emb, text_emb, text_accum, pair_ids, log_scale, bias):
    count = lax.axis_size(AXES)
    rows, width = image_emb.shape
    f32, bf16 = jnp.float32, jnp.bfloat16
    flags = (lax.axis_index("group") % 2).astype(jnp.int32).reshape(1)
    params = jnp.concatenate([log_scale, bias])
    ids = pair_ids.reshape(1, rows)

    skip = [(i, (i + 2) % count) for i in range(count)]
    swap = [(i, i ^ 1) for i in range(count)]

    def ahead(value):
        return lax.ppermute(value, AXES, skip)

    def across(value):
        return lax.ppermute(value, AXES, swap)

    top = rows * 176 // 256
    fixed_text = pltpu.with_memory_space_constraint(text_emb, pltpu.HBM)
    text_a = pl.pallas_call(
        cast_kernel,
        out_shape=jax.ShapeDtypeStruct((top, width), bf16),
        in_specs=[HBM],
        out_specs=VMEM,
        scratch_shapes=[pltpu.VMEM((top, width), f32), pltpu.SemaphoreType.DMA],
        compiler_params=pltpu.CompilerParams(vmem_limit_bytes=16 * 1024 * 1024),
        cost_estimate=pl.CostEstimate(flops=0, bytes_accessed=0, transcendentals=0),
        name="cast",
    )(fixed_text)
    text_b, *images = pl.pallas_call(
        load_kernel,
        out_shape=[
            jax.ShapeDtypeStruct((rows - top, width), bf16),
            *[jax.ShapeDtypeStruct((rows // PIECES, width), bf16)] * PIECES,
        ],
        in_specs=[ANY, HBM, HBM],
        out_specs=[VMEM] * (1 + PIECES),
        scratch_shapes=[pltpu.VMEM((rows - top, width), f32), pltpu.SemaphoreType.DMA((PIECES + 1,))],
        compiler_params=pltpu.CompilerParams(vmem_limit_bytes=16 * 1024 * 1024),
        cost_estimate=pl.CostEstimate(flops=0, bytes_accessed=0, transcendentals=0),
        name="load",
    )(text_a, fixed_text, pltpu.with_memory_space_constraint(image_emb, pltpu.HBM))
    far_a, far_b = ahead(text_a), ahead(text_b)
    mates = [across(piece) for piece in images]
    mate_ids = across(ids)
    both_ids = ahead(jnp.concatenate([ids, mate_ids]))

    cut = rows - rows * 3 // 16
    out_a, out_b, image_sum, loss = pl.pallas_call(
        own_kernel,
        out_shape=[
            jax.ShapeDtypeStruct((cut, width), bf16),
            jax.ShapeDtypeStruct((rows - cut, width), bf16),
            jax.ShapeDtypeStruct((rows, width), f32),
            jax.ShapeDtypeStruct((1, rows), f32),
        ],
        in_specs=[SMEM] * 2 + [VMEM] * 4 + [HBM] + [VMEM] * 2 * PIECES,
        out_specs=[VMEM] * 4,
        scratch_shapes=[pltpu.VMEM((rows, width), f32), pltpu.SemaphoreType.DMA],
        compiler_params=pltpu.CompilerParams(vmem_limit_bytes=16 * 1024 * 1024),
        cost_estimate=pl.CostEstimate(flops=0, bytes_accessed=0, transcendentals=0),
        name="own",
    )(flags, params, ids, mate_ids, text_a, text_b, pltpu.with_memory_space_constraint(text_accum, pltpu.HBM),
      *images, *mates)
    crossed = [(i, target ^ 1) for i, target in skip]
    arrived_a = ahead(out_a)
    mate_rows = across(out_b)
    arrived_b = lax.ppermute(mate_rows, AXES, crossed)

    (both_ids,) = call(ids_kernel, "ids", [((2, rows), jnp.int32)], (), loss, both_ids, flops=1300000000)
    passed_a, passed_b = call(
        relay_kernel, "relay", [((cut - 16, width), bf16), ((rows - cut + 16, width), bf16)],
        (flags,), both_ids, mate_rows, text_a, text_b, far_a, far_b, flops=1 << 30,
    )
    near_a, near_b = across(passed_a), across(passed_b)
    late, image_sum, loss = call(
        far_kernel, "far", [((rows, width), f32), ((rows, width), f32), ((1, rows), f32)],
        (flags, params), ids, mate_ids, both_ids, far_a, far_b, image_sum, loss, *images, *mates,
    )
    image_grad, loss = call(
        near_kernel, "near", [((rows, width), bf16), ((1, rows), f32)],
        (flags, params), ids, mate_ids, both_ids, near_a, near_b, image_sum, loss, *images,
    )
    late, image_grad = lax.optimization_barrier((late, image_grad))
    text_grad = add_part("add_a", 0, cut // STEP, arrived_a, late)
    text_grad = add_part("add_b", cut, (rows - cut) // STEP, arrived_b, late, text_grad)
    return (loss.reshape(rows), image_grad, text_grad)


def solution(mesh):
    in_specs = (P(AXES, None), P(AXES, None), P(AXES, None), P(AXES), P(), P())
    out_specs = (P(AXES), P(AXES, None), P(AXES, None))
    return jax.shard_map(body, mesh=mesh, in_specs=in_specs, out_specs=out_specs, check_vma=False)
```

```python
import functools

import jax
import jax.numpy as jnp
from jax import lax
from jax.experimental import pallas as pl
from jax.experimental.pallas import tpu as pltpu
from jax.sharding import PartitionSpec as P

SHIFTS = 2
AXES = ("dp", "group")
STEP = 16
PIECES = 4
VMEM = pl.BlockSpec(memory_space=pltpu.VMEM)
SMEM = pl.BlockSpec(memory_space=pltpu.SMEM)
ANY = pl.BlockSpec(memory_space=pl.ANY)
HBM = pl.BlockSpec(memory_space=pltpu.HBM)


def dot(a, b, contract):
    return lax.dot_general(a, b, ((contract[:1], contract[1:]), ((), ())), preferred_element_type=jnp.float32)


def pair(images, texts, image_ids, text_ids, params):
    raw = dot(images, texts, (1, 1))
    rows = raw.shape[0]
    scale = jnp.exp(jnp.full((1, rows), params[0], jnp.float32))
    logits = scale * raw + params[1]
    same = jnp.broadcast_to(image_ids, (rows, rows)).T == text_ids
    margin = jnp.where(same, -logits, logits)
    tail = jnp.exp(-jnp.abs(margin))
    loss = jnp.maximum(margin, 0.0) + jnp.log1p(tail)
    sigmoid = jnp.where(margin >= 0, 1.0, tail) / (1.0 + tail)
    coef = jnp.where(same, -sigmoid, sigmoid) * scale
    return jnp.sum(loss.T, axis=0, keepdims=True), coef


def whole(*parts):
    return jnp.concatenate([part[...] for part in parts], axis=0)


def low(coef):
    return coef.astype(jnp.bfloat16)


def cast_kernel(text, out, staged, sem):
    copy = pltpu.make_async_copy(text.at[pl.ds(0, out.shape[0])], staged, sem)
    copy.start()
    copy.wait()
    out[...] = staged[...].astype(out.dtype)


def load_kernel(before, text, image, out, *refs):
    images, (staged, sems) = refs[:-2], refs[-2:]
    step, rest = images[0].shape[0], out.shape[0]
    copies = [pltpu.make_async_copy(text.at[pl.ds(text.shape[0] - rest, rest)], staged, sems.at[PIECES])]
    for k, piece in enumerate(images):
        copies.append(pltpu.make_async_copy(image.at[pl.ds(k * step, step)], piece, sems.at[k]))
    for copy in copies:
        copy.start()
    copies[0].wait()
    out[...] = staged[...].astype(out.dtype)
    for copy in copies[1:]:
        copy.wait()


def add_kernel(start, chunks, arrived, late, *refs):
    out, staged, sems = refs[-3:]
    step = arrived.shape[0] // chunks
    copies = []
    for k in range(chunks):
        here, there = pl.ds(k * step, step), pl.ds(start + k * step, step)
        staged[here, :] = arrived[here, :].astype(staged.dtype) + late[there, :]
        copies.append(pltpu.make_async_copy(staged.at[here], out.at[there], sems.at[k]))
        copies[-1].start()
    for copy in copies:
        copy.wait()


def own_kernel(flags, params, ids, mate_ids, text_a, text_b, accum_in, *refs):
    images, mates = refs[:PIECES], refs[PIECES:2 * PIECES]
    out_a, out_b, image_sum, loss, accum, sem = refs[2 * PIECES:]
    copy = pltpu.make_async_copy(accum_in, accum, sem)
    copy.start()
    image, text = whole(*images), whole(text_a, text_b)
    own_loss, coef = pair(image, text, ids[...], ids[...], params)
    loss[...] = own_loss
    image_sum[...] = dot(low(coef), text, (1, 0))
    cut = out_a.shape[0]

    def give(value):
        out_a[...] = value[:cut, :].astype(out_a.dtype)
        out_b[...] = value[cut:, :].astype(out_b.dtype)

    @pl.when(flags[0] == 0)
    def _():
        mate = whole(*mates)
        _, mate_coef = pair(mate, text, mate_ids[...], ids[...], params)
        copy.wait()
        give(accum[...] + dot(low(coef.T), image, (1, 0)) + dot(low(mate_coef.T), mate, (1, 0)))

    @pl.when(flags[0] == 1)
    def _():
        copy.wait()
        give(accum[...] + dot(low(coef.T), image, (1, 0)))


def ids_kernel(token, both_ids, out):
    out[...] = both_ids[...]


def relay_kernel(flags, token, before, text_a, text_b, far_a, far_b, out_a, out_b):
    cut, top = out_a.shape[0], text_a.shape[0]

    def fill(upper, lower):
        out_a[:top, :] = upper[...]
        out_a[top:, :] = lower[:cut - top, :]
        out_b[...] = lower[cut - top:, :]

    pl.when(flags[0] == 0)(lambda: fill(text_a, text_b))
    pl.when(flags[0] == 1)(lambda: fill(far_a, far_b))


def far_kernel(flags, params, ids, mate_ids, both_ids, far_a, far_b, image_in, loss_in, *refs):
    images, mates = refs[:PIECES], refs[PIECES:2 * PIECES]
    late, image_sum, loss = refs[2 * PIECES:]
    image, far = whole(*images), whole(far_a, far_b)
    more, coef = pair(image, far, ids[...], both_ids[:1, :], params)
    loss[...] = loss_in[...] + more
    image_sum[...] = image_in[...] + dot(low(coef), far, (1, 0))
    part = dot(low(coef.T), image, (1, 0))

    @pl.when(flags[0] == 0)
    def _():
        late[...] = part

    @pl.when(flags[0] == 1)
    def _():
        mate = whole(*mates)
        _, mate_coef = pair(mate, far, mate_ids[...], both_ids[:1, :], params)
        late[...] = part + dot(low(mate_coef.T), mate, (1, 0))


def near_kernel(flags, params, ids, mate_ids, both_ids, near_a, near_b, image_in, loss_in, *refs):
    image_grad, loss = refs[PIECES:]
    image = whole(*refs[:PIECES])
    near_ids = jnp.where(flags[0] == 0, both_ids[1:, :], mate_ids[...])
    near = whole(near_a, near_b)
    more, coef = pair(image, near, ids[...], near_ids, params)
    loss[...] = (loss_in[...] + more) * (1.0 / ((SHIFTS + 1) * image.shape[0]))
    image_grad[...] = (image_in[...] + dot(low(coef), near, (1, 0))).astype(image_grad.dtype)


def call(kernel, name, outs, scalars, *operands, flops=0):
    return pl.pallas_call(
        kernel,
        out_shape=[jax.ShapeDtypeStruct(s, d) for s, d in outs],
        in_specs=[SMEM] * len(scalars) + [VMEM] * len(operands),
        out_specs=[VMEM] * len(outs),
        compiler_params=pltpu.CompilerParams(vmem_limit_bytes=16 * 1024 * 1024),
        cost_estimate=pl.CostEstimate(flops=flops, bytes_accessed=0, transcendentals=0),
        name=name,
    )(*scalars, *operands)


def add_part(name, start, chunks, arrived, late, *before):
    return pl.pallas_call(
        functools.partial(add_kernel, start, chunks),
        out_shape=jax.ShapeDtypeStruct(late.shape, late.dtype),
        in_specs=[VMEM, VMEM] + [HBM] * len(before),
        out_specs=HBM,
        scratch_shapes=[pltpu.VMEM(arrived.shape, late.dtype), pltpu.SemaphoreType.DMA((chunks,))],
        input_output_aliases={2: 0} if before else {},
        compiler_params=pltpu.CompilerParams(vmem_limit_bytes=16 * 1024 * 1024),
        cost_estimate=pl.CostEstimate(flops=0, bytes_accessed=0, transcendentals=0),
        name=name,
    )(arrived, late, *before)


def body(image_emb, text_emb, text_accum, pair_ids, log_scale, bias):
    count = lax.axis_size(AXES)
    rows, width = image_emb.shape
    f32, bf16 = jnp.float32, jnp.bfloat16
    flags = (lax.axis_index("group") % 2).astype(jnp.int32).reshape(1)
    params = jnp.concatenate([log_scale, bias])
    ids = pair_ids.reshape(1, rows)

    skip = [(i, (i + 2) % count) for i in range(count)]
    swap = [(i, i ^ 1) for i in range(count)]

    def ahead(value):
        return lax.ppermute(value, AXES, skip)

    def across(value):
        return lax.ppermute(value, AXES, swap)

    top = rows * 176 // 256
    fixed_text = pltpu.with_memory_space_constraint(text_emb, pltpu.HBM)
    text_a = pl.pallas_call(
        cast_kernel,
        out_shape=jax.ShapeDtypeStruct((top, width), bf16),
        in_specs=[HBM],
        out_specs=VMEM,
        scratch_shapes=[pltpu.VMEM((top, width), f32), pltpu.SemaphoreType.DMA],
        compiler_params=pltpu.CompilerParams(vmem_limit_bytes=16 * 1024 * 1024),
        cost_estimate=pl.CostEstimate(flops=0, bytes_accessed=0, transcendentals=0),
        name="cast",
    )(fixed_text)
    text_b, *images = pl.pallas_call(
        load_kernel,
        out_shape=[
            jax.ShapeDtypeStruct((rows - top, width), bf16),
            *[jax.ShapeDtypeStruct((rows // PIECES, width), bf16)] * PIECES,
        ],
        in_specs=[ANY, HBM, HBM],
        out_specs=[VMEM] * (1 + PIECES),
        scratch_shapes=[pltpu.VMEM((rows - top, width), f32), pltpu.SemaphoreType.DMA((PIECES + 1,))],
        compiler_params=pltpu.CompilerParams(vmem_limit_bytes=16 * 1024 * 1024),
        cost_estimate=pl.CostEstimate(flops=0, bytes_accessed=0, transcendentals=0),
        name="load",
    )(text_a, fixed_text, pltpu.with_memory_space_constraint(image_emb, pltpu.HBM))
    far_a, far_b = ahead(text_a), ahead(text_b)
    mates = [across(piece) for piece in images]
    mate_ids = across(ids)
    both_ids = ahead(jnp.concatenate([ids, mate_ids]))

    cut = rows - rows * 3 // 16
    out_a, out_b, image_sum, loss = pl.pallas_call(
        own_kernel,
        out_shape=[
            jax.ShapeDtypeStruct((cut, width), bf16),
            jax.ShapeDtypeStruct((rows - cut, width), bf16),
            jax.ShapeDtypeStruct((rows, width), f32),
            jax.ShapeDtypeStruct((1, rows), f32),
        ],
        in_specs=[SMEM] * 2 + [VMEM] * 4 + [HBM] + [VMEM] * 2 * PIECES,
        out_specs=[VMEM] * 4,
        scratch_shapes=[pltpu.VMEM((rows, width), f32), pltpu.SemaphoreType.DMA],
        compiler_params=pltpu.CompilerParams(vmem_limit_bytes=16 * 1024 * 1024),
        cost_estimate=pl.CostEstimate(flops=0, bytes_accessed=0, transcendentals=0),
        name="own",
    )(flags, params, ids, mate_ids, text_a, text_b, pltpu.with_memory_space_constraint(text_accum, pltpu.HBM),
      *images, *mates)
    crossed = [(i, target ^ 1) for i, target in skip]
    arrived_a = ahead(out_a)
    mate_rows = across(out_b)
    arrived_b = lax.ppermute(mate_rows, AXES, crossed)

    (both_ids,) = call(ids_kernel, "ids", [((2, rows), jnp.int32)], (), loss, both_ids, flops=1300000000)
    passed_a, passed_b = call(
        relay_kernel, "relay", [((cut - 16, width), bf16), ((rows - cut + 16, width), bf16)],
        (flags,), both_ids, mate_rows, text_a, text_b, far_a, far_b, flops=1 << 30,
    )
    near_a, near_b = across(passed_a), across(passed_b)
    late, image_sum, loss = call(
        far_kernel, "far", [((rows, width), f32), ((rows, width), f32), ((1, rows), f32)],
        (flags, params), ids, mate_ids, both_ids, far_a, far_b, image_sum, loss, *images, *mates,
    )
    image_grad, loss = call(
        near_kernel, "near", [((rows, width), bf16), ((1, rows), f32)],
        (flags, params), ids, mate_ids, both_ids, near_a, near_b, image_sum, loss, *images,
    )
    late, image_grad = lax.optimization_barrier((late, image_grad))
    text_grad = add_part("add_a", 0, cut // STEP, arrived_a, late)
    text_grad = add_part("add_b", cut, (rows - cut) // STEP, arrived_b, late, text_grad)
    return (loss.reshape(rows), image_grad, text_grad)


def solution(mesh):
    in_specs = (P(AXES, None), P(AXES, None), P(AXES, None), P(AXES), P(), P())
    out_specs = (P(AXES), P(AXES, None), P(AXES, None))
    return jax.shard_map(body, mesh=mesh, in_specs=in_specs, out_specs=out_specs, check_vma=False)
```

```python
import functools

import jax
import jax.numpy as jnp
from jax import lax
from jax.experimental import pallas as pl
from jax.experimental.pallas import tpu as pltpu
from jax.sharding import PartitionSpec as P

SHIFTS = 2
AXES = ("dp", "group")
STEP = 16
VMEM = pl.BlockSpec(memory_space=pltpu.VMEM)
SMEM = pl.BlockSpec(memory_space=pltpu.SMEM)
ANY = pl.BlockSpec(memory_space=pl.ANY)
HBM = pl.BlockSpec(memory_space=pltpu.HBM)


def dot(a, b, contract):
    return lax.dot_general(a, b, ((contract[:1], contract[1:]), ((), ())), preferred_element_type=jnp.float32)


def pair(images, texts, image_ids, text_ids, params):
    raw = dot(images, texts, (1, 1))
    rows = raw.shape[0]
    scale = jnp.exp(jnp.full((1, rows), params[0], jnp.float32))
    logits = scale * raw + params[1]
    same = jnp.broadcast_to(image_ids, (rows, rows)).T == text_ids
    margin = jnp.where(same, -logits, logits)
    tail = jnp.exp(-jnp.abs(margin))
    loss = jnp.maximum(margin, 0.0) + jnp.log1p(tail)
    sigmoid = jnp.where(margin >= 0, 1.0, tail) / (1.0 + tail)
    coef = jnp.where(same, -sigmoid, sigmoid) * scale
    return jnp.sum(loss.T, axis=0, keepdims=True), coef


def whole(a, b):
    return jnp.concatenate([a[...], b[...]], axis=0)


def low(coef):
    return coef.astype(jnp.bfloat16)


def cast_kernel(text, out):
    out[...] = text[...].astype(out.dtype)


def load_kernel(text, image, out_a, out_b, sems):
    half = out_a.shape[0]
    copies = [
        pltpu.make_async_copy(image.at[pl.ds(0, half)], out_a, sems.at[0]),
        pltpu.make_async_copy(image.at[pl.ds(half, half)], out_b, sems.at[1]),
    ]
    for copy in copies:
        copy.start()
    for copy in copies:
        copy.wait()


def add_kernel(start, chunks, arrived, late, *refs):
    out, staged, sems = refs[-3:]
    step = arrived.shape[0] // chunks
    copies = []
    for k in range(chunks):
        here, there = pl.ds(k * step, step), pl.ds(start + k * step, step)
        staged[here, :] = arrived[here, :].astype(staged.dtype) + late[there, :]
        copies.append(pltpu.make_async_copy(staged.at[here], out.at[there], sems.at[k]))
        copies[-1].start()
    for copy in copies:
        copy.wait()


def own_kernel(flags, params, ids, mate_ids, image_a, image_b, mate_a, mate_b, text, accum_in, out_a, out_b, image_sum, loss,
               accum, sem):
    copy = pltpu.make_async_copy(accum_in, accum, sem)
    copy.start()
    image = whole(image_a, image_b)
    own_loss, coef = pair(image, text[...], ids[...], ids[...], params)
    loss[...] = own_loss
    image_sum[...] = dot(low(coef), text[...], (1, 0))
    cut = out_a.shape[0]

    def give(value):
        out_a[...] = value[:cut, :].astype(out_a.dtype)
        out_b[...] = value[cut:, :].astype(out_b.dtype)

    @pl.when(flags[0] == 0)
    def _():
        mate = whole(mate_a, mate_b)
        _, mate_coef = pair(mate, text[...], mate_ids[...], ids[...], params)
        copy.wait()
        give(accum[...] + dot(low(coef.T), image, (1, 0)) + dot(low(mate_coef.T), mate, (1, 0)))

    @pl.when(flags[0] == 1)
    def _():
        copy.wait()
        give(accum[...] + dot(low(coef.T), image, (1, 0)))


def ids_kernel(token, both_ids, out):
    out[...] = both_ids[...]


def relay_kernel(flags, token, before, text, far, out_a, out_b):
    cut = out_a.shape[0]

    def fill(source):
        out_a[...] = source[:cut, :]
        out_b[...] = source[cut:, :]

    pl.when(flags[0] == 0)(lambda: fill(text))
    pl.when(flags[0] == 1)(lambda: fill(far))


def far_kernel(flags, params, ids, mate_ids, both_ids, image_a, image_b, mate_a, mate_b, far, image_in,
               loss_in, late, image_sum, loss):
    image = whole(image_a, image_b)
    more, coef = pair(image, far[...], ids[...], both_ids[:1, :], params)
    loss[...] = loss_in[...] + more
    image_sum[...] = image_in[...] + dot(low(coef), far[...], (1, 0))
    part = dot(low(coef.T), image, (1, 0))

    @pl.when(flags[0] == 0)
    def _():
        late[...] = part

    @pl.when(flags[0] == 1)
    def _():
        mate = whole(mate_a, mate_b)
        _, mate_coef = pair(mate, far[...], mate_ids[...], both_ids[:1, :], params)
        late[...] = part + dot(low(mate_coef.T), mate, (1, 0))


def near_kernel(flags, params, ids, mate_ids, both_ids, image_a, image_b, near_a, near_b, image_in, loss_in,
                image_grad, loss):
    image = whole(image_a, image_b)
    near_ids = jnp.where(flags[0] == 0, both_ids[1:, :], mate_ids[...])
    near = whole(near_a, near_b)
    more, coef = pair(image, near, ids[...], near_ids, params)
    loss[...] = (loss_in[...] + more) * (1.0 / ((SHIFTS + 1) * image.shape[0]))
    image_grad[...] = (image_in[...] + dot(low(coef), near, (1, 0))).astype(image_grad.dtype)


def call(kernel, name, outs, scalars, *operands, flops=0):
    return pl.pallas_call(
        kernel,
        out_shape=[jax.ShapeDtypeStruct(s, d) for s, d in outs],
        in_specs=[SMEM] * len(scalars) + [VMEM] * len(operands),
        out_specs=[VMEM] * len(outs),
        compiler_params=pltpu.CompilerParams(vmem_limit_bytes=16 * 1024 * 1024),
        cost_estimate=pl.CostEstimate(flops=flops, bytes_accessed=0, transcendentals=0),
        name=name,
    )(*scalars, *operands)


def add_part(name, start, chunks, arrived, late, *before):
    return pl.pallas_call(
        functools.partial(add_kernel, start, chunks),
        out_shape=jax.ShapeDtypeStruct(late.shape, late.dtype),
        in_specs=[VMEM, VMEM] + [HBM] * len(before),
        out_specs=HBM,
        scratch_shapes=[pltpu.VMEM(arrived.shape, late.dtype), pltpu.SemaphoreType.DMA((chunks,))],
        input_output_aliases={2: 0} if before else {},
        compiler_params=pltpu.CompilerParams(vmem_limit_bytes=16 * 1024 * 1024),
        cost_estimate=pl.CostEstimate(flops=0, bytes_accessed=0, transcendentals=0),
        name=name,
    )(arrived, late, *before)


def body(image_emb, text_emb, text_accum, pair_ids, log_scale, bias):
    count = lax.axis_size(AXES)
    rows, width = image_emb.shape
    half = rows // 2
    f32, bf16 = jnp.float32, jnp.bfloat16
    flags = (lax.axis_index("group") % 2).astype(jnp.int32).reshape(1)
    params = jnp.concatenate([log_scale, bias])
    ids = pair_ids.reshape(1, rows)

    skip = [(i, (i + 2) % count) for i in range(count)]
    swap = [(i, i ^ 1) for i in range(count)]

    def ahead(value):
        return lax.ppermute(value, AXES, skip)

    def across(value):
        return lax.ppermute(value, AXES, swap)

    (text,) = call(cast_kernel, "cast", [((rows, width), bf16)], (), text_emb)
    far = ahead(text)

    image_a, image_b = pl.pallas_call(
        load_kernel,
        out_shape=[jax.ShapeDtypeStruct((n, width), bf16) for n in (half, rows - half)],
        in_specs=[ANY, HBM],
        out_specs=[VMEM] * 2,
        scratch_shapes=[pltpu.SemaphoreType.DMA((2,))],
        compiler_params=pltpu.CompilerParams(vmem_limit_bytes=16 * 1024 * 1024),
        cost_estimate=pl.CostEstimate(flops=0, bytes_accessed=0, transcendentals=0),
        name="load",
    )(text, pltpu.with_memory_space_constraint(image_emb, pltpu.HBM))
    mate_a, mate_b = across(image_a), across(image_b)
    mate_ids = across(ids)
    both_ids = ahead(jnp.concatenate([ids, mate_ids]))

    cut = rows - rows * 3 // 16
    out_a, out_b, image_sum, loss = pl.pallas_call(
        own_kernel,
        out_shape=[
            jax.ShapeDtypeStruct((cut, width), bf16),
            jax.ShapeDtypeStruct((rows - cut, width), bf16),
            jax.ShapeDtypeStruct((rows, width), f32),
            jax.ShapeDtypeStruct((1, rows), f32),
        ],
        in_specs=[SMEM] * 2 + [VMEM] * 7 + [HBM],
        out_specs=[VMEM] * 4,
        scratch_shapes=[pltpu.VMEM((rows, width), f32), pltpu.SemaphoreType.DMA],
        compiler_params=pltpu.CompilerParams(vmem_limit_bytes=16 * 1024 * 1024),
        cost_estimate=pl.CostEstimate(flops=0, bytes_accessed=0, transcendentals=0),
        name="own",
    )(flags, params, ids, mate_ids, image_a, image_b, mate_a, mate_b, text,
      pltpu.with_memory_space_constraint(text_accum, pltpu.HBM))
    crossed = [(i, target ^ 1) for i, target in skip]
    arrived_a = ahead(out_a)
    mate_rows = across(out_b)
    arrived_b = lax.ppermute(mate_rows, AXES, crossed)

    (both_ids,) = call(ids_kernel, "ids", [((2, rows), jnp.int32)], (), loss, both_ids, flops=2 << 30)
    passed_a, passed_b = call(
        relay_kernel, "relay", [((cut - 16, width), bf16), ((rows - cut + 16, width), bf16)],
        (flags,), both_ids, mate_rows, text, far, flops=1 << 30,
    )
    near_a, near_b = across(passed_a), across(passed_b)
    late, image_sum, loss = call(
        far_kernel, "far", [((rows, width), f32), ((rows, width), f32), ((1, rows), f32)],
        (flags, params), ids, mate_ids, both_ids, image_a, image_b, mate_a, mate_b, far, image_sum,
        loss,
    )
    image_grad, loss = call(
        near_kernel, "near", [((rows, width), bf16), ((1, rows), f32)],
        (flags, params), ids, mate_ids, both_ids, image_a, image_b, near_a, near_b, image_sum, loss,
    )
    late, image_grad = lax.optimization_barrier((late, image_grad))
    text_grad = add_part("add_a", 0, cut // STEP, arrived_a, late)
    text_grad = add_part("add_b", cut, (rows - cut) // STEP, arrived_b, late, text_grad)
    return (loss.reshape(rows), image_grad, text_grad)


def solution(mesh):
    in_specs = (P(AXES, None), P(AXES, None), P(AXES, None), P(AXES), P(), P())
    out_specs = (P(AXES), P(AXES, None), P(AXES, None))
    return jax.shard_map(body, mesh=mesh, in_specs=in_specs, out_specs=out_specs, check_vma=False)
```

```python
import functools

import jax
import jax.numpy as jnp
from jax import lax
from jax.experimental import pallas as pl
from jax.experimental.pallas import tpu as pltpu
from jax.sharding import PartitionSpec as P

SHIFTS = 2
AXES = ("dp", "group")
STEP = 16
VMEM = pl.BlockSpec(memory_space=pltpu.VMEM)
SMEM = pl.BlockSpec(memory_space=pltpu.SMEM)
ANY = pl.BlockSpec(memory_space=pl.ANY)
HBM = pl.BlockSpec(memory_space=pltpu.HBM)


def dot(a, b, contract):
    return lax.dot_general(a, b, ((contract[:1], contract[1:]), ((), ())), preferred_element_type=jnp.float32)


def pair(images, texts, image_ids, text_ids, params):
    raw = dot(images, texts, (1, 1))
    rows = raw.shape[0]
    scale = jnp.exp(jnp.full((1, rows), params[0], jnp.float32))
    logits = scale * raw + params[1]
    same = jnp.broadcast_to(image_ids, (rows, rows)).T == text_ids
    margin = jnp.where(same, -logits, logits)
    tail = jnp.exp(-jnp.abs(margin))
    loss = jnp.maximum(margin, 0.0) + jnp.log1p(tail)
    sigmoid = jnp.where(margin >= 0, 1.0, tail) / (1.0 + tail)
    coef = jnp.where(same, -sigmoid, sigmoid) * scale
    return jnp.sum(loss.T, axis=0, keepdims=True), coef


def whole(a, b):
    return jnp.concatenate([a[...], b[...]], axis=0)


def low(coef):
    return coef.astype(jnp.bfloat16)


def cast_kernel(text, out):
    out[...] = text[...].astype(out.dtype)


def load_kernel(text, image, out_a, out_b, sems):
    half = out_a.shape[0]
    copies = [
        pltpu.make_async_copy(image.at[pl.ds(0, half)], out_a, sems.at[0]),
        pltpu.make_async_copy(image.at[pl.ds(half, half)], out_b, sems.at[1]),
    ]
    for copy in copies:
        copy.start()
    for copy in copies:
        copy.wait()


def add_kernel(start, chunks, arrived, late, *refs):
    out, staged, sems = refs[-3:]
    step = arrived.shape[0] // chunks
    copies = []
    for k in range(chunks):
        here, there = pl.ds(k * step, step), pl.ds(start + k * step, step)
        staged[here, :] = arrived[here, :].astype(staged.dtype) + late[there, :]
        copies.append(pltpu.make_async_copy(staged.at[here], out.at[there], sems.at[k]))
        copies[-1].start()
    for copy in copies:
        copy.wait()


def own_kernel(flags, params, ids, mate_ids, image_a, image_b, mate_a, mate_b, text, accum_in, out_a, out_b, image_sum, loss,
               accum, sem):
    copy = pltpu.make_async_copy(accum_in, accum, sem)
    copy.start()
    image = whole(image_a, image_b)
    own_loss, coef = pair(image, text[...], ids[...], ids[...], params)
    loss[...] = own_loss
    copy.wait()
    total = accum[...] + dot(low(coef.T), image, (1, 0))
    cut = out_a.shape[0]

    def give(value):
        out_a[...] = value[:cut, :].astype(out_a.dtype)
        out_b[...] = value[cut:, :].astype(out_b.dtype)

    @pl.when(flags[0] == 0)
    def _():
        mate = whole(mate_a, mate_b)
        _, mate_coef = pair(mate, text[...], mate_ids[...], ids[...], params)
        give(total + dot(low(mate_coef.T), mate, (1, 0)))

    @pl.when(flags[0] == 1)
    def _():
        give(total)

    image_sum[...] = dot(low(coef), text[...], (1, 0))


def ids_kernel(token, both_ids, out):
    out[...] = both_ids[...]


def relay_kernel(flags, token, before, text, far, out_a, out_b):
    cut = out_a.shape[0]

    def fill(source):
        out_a[...] = source[:cut, :]
        out_b[...] = source[cut:, :]

    pl.when(flags[0] == 0)(lambda: fill(text))
    pl.when(flags[0] == 1)(lambda: fill(far))


def far_kernel(flags, params, ids, mate_ids, both_ids, image_a, image_b, mate_a, mate_b, far, image_in,
               loss_in, late, image_sum, loss):
    image = whole(image_a, image_b)
    more, coef = pair(image, far[...], ids[...], both_ids[:1, :], params)
    loss[...] = loss_in[...] + more
    image_sum[...] = image_in[...] + dot(low(coef), far[...], (1, 0))
    part = dot(low(coef.T), image, (1, 0))

    @pl.when(flags[0] == 0)
    def _():
        late[...] = part

    @pl.when(flags[0] == 1)
    def _():
        mate = whole(mate_a, mate_b)
        _, mate_coef = pair(mate, far[...], mate_ids[...], both_ids[:1, :], params)
        late[...] = part + dot(low(mate_coef.T), mate, (1, 0))


def near_kernel(flags, params, ids, mate_ids, both_ids, image_a, image_b, near_a, near_b, image_in, loss_in,
                image_grad, loss):
    image = whole(image_a, image_b)
    near_ids = jnp.where(flags[0] == 0, both_ids[1:, :], mate_ids[...])
    near = whole(near_a, near_b)
    more, coef = pair(image, near, ids[...], near_ids, params)
    loss[...] = (loss_in[...] + more) * (1.0 / ((SHIFTS + 1) * image.shape[0]))
    image_grad[...] = (image_in[...] + dot(low(coef), near, (1, 0))).astype(image_grad.dtype)


def call(kernel, name, outs, scalars, *operands, flops=0):
    return pl.pallas_call(
        kernel,
        out_shape=[jax.ShapeDtypeStruct(s, d) for s, d in outs],
        in_specs=[SMEM] * len(scalars) + [VMEM] * len(operands),
        out_specs=[VMEM] * len(outs),
        compiler_params=pltpu.CompilerParams(vmem_limit_bytes=16 * 1024 * 1024),
        cost_estimate=pl.CostEstimate(flops=flops, bytes_accessed=0, transcendentals=0),
        name=name,
    )(*scalars, *operands)


def add_part(name, start, chunks, arrived, late, *before):
    return pl.pallas_call(
        functools.partial(add_kernel, start, chunks),
        out_shape=jax.ShapeDtypeStruct(late.shape, late.dtype),
        in_specs=[VMEM, VMEM] + [HBM] * len(before),
        out_specs=HBM,
        scratch_shapes=[pltpu.VMEM(arrived.shape, late.dtype), pltpu.SemaphoreType.DMA((chunks,))],
        input_output_aliases={2: 0} if before else {},
        compiler_params=pltpu.CompilerParams(vmem_limit_bytes=16 * 1024 * 1024),
        cost_estimate=pl.CostEstimate(flops=0, bytes_accessed=0, transcendentals=0),
        name=name,
    )(arrived, late, *before)


def body(image_emb, text_emb, text_accum, pair_ids, log_scale, bias):
    count = lax.axis_size(AXES)
    rows, width = image_emb.shape
    half = rows // 2
    f32, bf16 = jnp.float32, jnp.bfloat16
    flags = (lax.axis_index("group") % 2).astype(jnp.int32).reshape(1)
    params = jnp.concatenate([log_scale, bias])
    ids = pair_ids.reshape(1, rows)

    skip = [(i, (i + 2) % count) for i in range(count)]
    swap = [(i, i ^ 1) for i in range(count)]

    def ahead(value):
        return lax.ppermute(value, AXES, skip)

    def across(value):
        return lax.ppermute(value, AXES, swap)

    (text,) = call(cast_kernel, "cast", [((rows, width), bf16)], (), text_emb)
    far = ahead(text)

    image_a, image_b = pl.pallas_call(
        load_kernel,
        out_shape=[jax.ShapeDtypeStruct((n, width), bf16) for n in (half, rows - half)],
        in_specs=[ANY, HBM],
        out_specs=[VMEM] * 2,
        scratch_shapes=[pltpu.SemaphoreType.DMA((2,))],
        compiler_params=pltpu.CompilerParams(vmem_limit_bytes=16 * 1024 * 1024),
        cost_estimate=pl.CostEstimate(flops=0, bytes_accessed=0, transcendentals=0),
        name="load",
    )(text, pltpu.with_memory_space_constraint(image_emb, pltpu.HBM))
    mate_a, mate_b = across(image_a), across(image_b)
    mate_ids = across(ids)
    both_ids = ahead(jnp.concatenate([ids, mate_ids]))

    cut = rows - rows // 4
    out_a, out_b, image_sum, loss = pl.pallas_call(
        own_kernel,
        out_shape=[
            jax.ShapeDtypeStruct((cut, width), bf16),
            jax.ShapeDtypeStruct((rows - cut, width), bf16),
            jax.ShapeDtypeStruct((rows, width), f32),
            jax.ShapeDtypeStruct((1, rows), f32),
        ],
        in_specs=[SMEM] * 2 + [VMEM] * 7 + [HBM],
        out_specs=[VMEM] * 4,
        scratch_shapes=[pltpu.VMEM((rows, width), f32), pltpu.SemaphoreType.DMA],
        compiler_params=pltpu.CompilerParams(vmem_limit_bytes=16 * 1024 * 1024),
        cost_estimate=pl.CostEstimate(flops=0, bytes_accessed=0, transcendentals=0),
        name="own",
    )(flags, params, ids, mate_ids, image_a, image_b, mate_a, mate_b, text,
      pltpu.with_memory_space_constraint(text_accum, pltpu.HBM))
    crossed = [(i, target ^ 1) for i, target in skip]
    arrived_a = ahead(out_a)
    mate_rows = across(out_b)
    arrived_b = lax.ppermute(mate_rows, AXES, crossed)

    (both_ids,) = call(ids_kernel, "ids", [((2, rows), jnp.int32)], (), loss, both_ids, flops=2 << 30)
    passed_a, passed_b = call(
        relay_kernel, "relay", [((cut - 16, width), bf16), ((rows - cut + 16, width), bf16)],
        (flags,), both_ids, mate_rows, text, far, flops=1 << 30,
    )
    near_a, near_b = across(passed_a), across(passed_b)
    late, image_sum, loss = call(
        far_kernel, "far", [((rows, width), f32), ((rows, width), f32), ((1, rows), f32)],
        (flags, params), ids, mate_ids, both_ids, image_a, image_b, mate_a, mate_b, far, image_sum,
        loss,
    )
    image_grad, loss = call(
        near_kernel, "near", [((rows, width), bf16), ((1, rows), f32)],
        (flags, params), ids, mate_ids, both_ids, image_a, image_b, near_a, near_b, image_sum, loss,
    )
    late, image_grad = lax.optimization_barrier((late, image_grad))
    text_grad = add_part("add_a", 0, cut // STEP, arrived_a, late)
    text_grad = add_part("add_b", cut, (rows - cut) // STEP, arrived_b, late, text_grad)
    return (loss.reshape(rows), image_grad, text_grad)


def solution(mesh):
    in_specs = (P(AXES, None), P(AXES, None), P(AXES, None), P(AXES), P(), P())
    out_specs = (P(AXES), P(AXES, None), P(AXES, None))
    return jax.shard_map(body, mesh=mesh, in_specs=in_specs, out_specs=out_specs, check_vma=False)
```

```python
import functools

import jax
import jax.numpy as jnp
from jax import lax
from jax.experimental import pallas as pl
from jax.experimental.pallas import tpu as pltpu
from jax.sharding import PartitionSpec as P

SHIFTS = 2
AXES = ("dp", "group")
STEP = 16
VMEM = pl.BlockSpec(memory_space=pltpu.VMEM)
SMEM = pl.BlockSpec(memory_space=pltpu.SMEM)
ANY = pl.BlockSpec(memory_space=pl.ANY)
HBM = pl.BlockSpec(memory_space=pltpu.HBM)


def dot(a, b, contract):
    return lax.dot_general(a, b, ((contract[:1], contract[1:]), ((), ())), preferred_element_type=jnp.float32)


def pair(images, texts, image_ids, text_ids, params):
    raw = dot(images, texts, (1, 1))
    rows = raw.shape[0]
    scale = jnp.exp(jnp.full((1, rows), params[0], jnp.float32))
    logits = scale * raw + params[1]
    same = jnp.broadcast_to(image_ids, (rows, rows)).T == text_ids
    margin = jnp.where(same, -logits, logits)
    tail = jnp.exp(-jnp.abs(margin))
    loss = jnp.maximum(margin, 0.0) + jnp.log1p(tail)
    sigmoid = jnp.where(margin >= 0, 1.0, tail) / (1.0 + tail)
    coef = jnp.where(same, -sigmoid, sigmoid) * scale
    return jnp.sum(loss.T, axis=0, keepdims=True), coef


def whole(a, b):
    return jnp.concatenate([a[...], b[...]], axis=0)


def low(coef):
    return coef.astype(jnp.bfloat16)


def cast_kernel(text, out):
    out[...] = text[...].astype(out.dtype)


def load_kernel(text, image, out_a, out_b, sems):
    half = out_a.shape[0]
    copies = [
        pltpu.make_async_copy(image.at[pl.ds(0, half)], out_a, sems.at[0]),
        pltpu.make_async_copy(image.at[pl.ds(half, half)], out_b, sems.at[1]),
    ]
    for copy in copies:
        copy.start()
    for copy in copies:
        copy.wait()


def add_kernel(start, chunks, arrived, late, *refs):
    out, staged, sems = refs[-3:]
    step = arrived.shape[0] // chunks
    copies = []
    for k in range(chunks):
        here, there = pl.ds(k * step, step), pl.ds(start + k * step, step)
        staged[here, :] = arrived[here, :].astype(staged.dtype) + late[there, :]
        copies.append(pltpu.make_async_copy(staged.at[here], out.at[there], sems.at[k]))
        copies[-1].start()
    for copy in copies:
        copy.wait()


def own_kernel(flags, params, ids, mate_ids, image_a, image_b, mate_a, mate_b, text, accum_in, out_a, out_b, out_c,
               image_sum, loss, accum, sem):
    copy = pltpu.make_async_copy(accum_in, accum, sem)
    copy.start()
    image = whole(image_a, image_b)
    own_loss, coef = pair(image, text[...], ids[...], ids[...], params)
    loss[...] = own_loss
    copy.wait()
    total = accum[...] + dot(low(coef.T), image, (1, 0))
    cut = out_a.shape[0]

    def give(value):
        out_a[...] = value[:cut, :].astype(out_a.dtype)
        out_b[...] = value[cut:cut + out_b.shape[0], :].astype(out_b.dtype)
        out_c[...] = value[cut + out_b.shape[0]:, :].astype(out_c.dtype)

    @pl.when(flags[0] == 0)
    def _():
        mate = whole(mate_a, mate_b)
        _, mate_coef = pair(mate, text[...], mate_ids[...], ids[...], params)
        give(total + dot(low(mate_coef.T), mate, (1, 0)))

    @pl.when(flags[0] == 1)
    def _():
        give(total)

    image_sum[...] = dot(low(coef), text[...], (1, 0))


def ids_kernel(token, both_ids, out):
    out[...] = both_ids[...]


def relay_kernel(flags, token, before_b, before_c, text, far, out_a, out_b):
    cut = out_a.shape[0]

    def fill(source):
        out_a[...] = source[:cut, :]
        out_b[...] = source[cut:, :]

    pl.when(flags[0] == 0)(lambda: fill(text))
    pl.when(flags[0] == 1)(lambda: fill(far))


def far_kernel(flags, params, ids, mate_ids, both_ids, image_a, image_b, mate_a, mate_b, far, image_in,
               loss_in, late, image_sum, loss):
    image = whole(image_a, image_b)
    more, coef = pair(image, far[...], ids[...], both_ids[:1, :], params)
    loss[...] = loss_in[...] + more
    image_sum[...] = image_in[...] + dot(low(coef), far[...], (1, 0))
    part = dot(low(coef.T), image, (1, 0))

    @pl.when(flags[0] == 0)
    def _():
        late[...] = part

    @pl.when(flags[0] == 1)
    def _():
        mate = whole(mate_a, mate_b)
        _, mate_coef = pair(mate, far[...], mate_ids[...], both_ids[:1, :], params)
        late[...] = part + dot(low(mate_coef.T), mate, (1, 0))


def near_kernel(flags, params, ids, mate_ids, both_ids, image_a, image_b, near_a, near_b, image_in, loss_in,
                image_grad, loss):
    image = whole(image_a, image_b)
    near_ids = jnp.where(flags[0] == 0, both_ids[1:, :], mate_ids[...])
    near = whole(near_a, near_b)
    more, coef = pair(image, near, ids[...], near_ids, params)
    loss[...] = (loss_in[...] + more) * (1.0 / ((SHIFTS + 1) * image.shape[0]))
    image_grad[...] = (image_in[...] + dot(low(coef), near, (1, 0))).astype(image_grad.dtype)


def call(kernel, name, outs, scalars, *operands, flops=0):
    return pl.pallas_call(
        kernel,
        out_shape=[jax.ShapeDtypeStruct(s, d) for s, d in outs],
        in_specs=[SMEM] * len(scalars) + [VMEM] * len(operands),
        out_specs=[VMEM] * len(outs),
        compiler_params=pltpu.CompilerParams(vmem_limit_bytes=16 * 1024 * 1024),
        cost_estimate=pl.CostEstimate(flops=flops, bytes_accessed=0, transcendentals=0),
        name=name,
    )(*scalars, *operands)


def add_part(name, start, chunks, arrived, late, *before):
    return pl.pallas_call(
        functools.partial(add_kernel, start, chunks),
        out_shape=jax.ShapeDtypeStruct(late.shape, late.dtype),
        in_specs=[VMEM, VMEM] + [HBM] * len(before),
        out_specs=HBM,
        scratch_shapes=[pltpu.VMEM(arrived.shape, late.dtype), pltpu.SemaphoreType.DMA((chunks,))],
        input_output_aliases={2: 0} if before else {},
        compiler_params=pltpu.CompilerParams(vmem_limit_bytes=16 * 1024 * 1024),
        cost_estimate=pl.CostEstimate(flops=0, bytes_accessed=0, transcendentals=0),
        name=name,
    )(arrived, late, *before)


def body(image_emb, text_emb, text_accum, pair_ids, log_scale, bias):
    count = lax.axis_size(AXES)
    rows, width = image_emb.shape
    half = rows // 2
    f32, bf16 = jnp.float32, jnp.bfloat16
    flags = (lax.axis_index("group") % 2).astype(jnp.int32).reshape(1)
    params = jnp.concatenate([log_scale, bias])
    ids = pair_ids.reshape(1, rows)

    skip = [(i, (i + 2) % count) for i in range(count)]
    swap = [(i, i ^ 1) for i in range(count)]

    def ahead(value):
        return lax.ppermute(value, AXES, skip)

    def across(value):
        return lax.ppermute(value, AXES, swap)

    (text,) = call(cast_kernel, "cast", [((rows, width), bf16)], (), text_emb)
    far = ahead(text)

    image_a, image_b = pl.pallas_call(
        load_kernel,
        out_shape=[jax.ShapeDtypeStruct((n, width), bf16) for n in (half, rows - half)],
        in_specs=[ANY, HBM],
        out_specs=[VMEM] * 2,
        scratch_shapes=[pltpu.SemaphoreType.DMA((2,))],
        compiler_params=pltpu.CompilerParams(vmem_limit_bytes=16 * 1024 * 1024),
        cost_estimate=pl.CostEstimate(flops=0, bytes_accessed=0, transcendentals=0),
        name="load",
    )(text, pltpu.with_memory_space_constraint(image_emb, pltpu.HBM))
    mate_a, mate_b = across(image_a), across(image_b)
    mate_ids = across(ids)
    both_ids = ahead(jnp.concatenate([ids, mate_ids]))

    cut = rows - rows // 4
    out_a, out_b, out_c, image_sum, loss = pl.pallas_call(
        own_kernel,
        out_shape=[
            jax.ShapeDtypeStruct((cut, width), bf16),
            jax.ShapeDtypeStruct((rows - cut - STEP, width), bf16),
            jax.ShapeDtypeStruct((STEP, width), bf16),
            jax.ShapeDtypeStruct((rows, width), f32),
            jax.ShapeDtypeStruct((1, rows), f32),
        ],
        in_specs=[SMEM] * 2 + [VMEM] * 7 + [HBM],
        out_specs=[VMEM] * 5,
        scratch_shapes=[pltpu.VMEM((rows, width), f32), pltpu.SemaphoreType.DMA],
        compiler_params=pltpu.CompilerParams(vmem_limit_bytes=16 * 1024 * 1024),
        cost_estimate=pl.CostEstimate(flops=0, bytes_accessed=0, transcendentals=0),
        name="own",
    )(flags, params, ids, mate_ids, image_a, image_b, mate_a, mate_b, text,
      pltpu.with_memory_space_constraint(text_accum, pltpu.HBM))
    crossed = [(i, target ^ 1) for i, target in skip]
    arrived_a = ahead(out_a)
    mate_rows, mate_last = across(out_b), across(out_c)
    arrived_b, arrived_c = (lax.ppermute(part, AXES, crossed) for part in (mate_rows, mate_last))

    (both_ids,) = call(ids_kernel, "ids", [((2, rows), jnp.int32)], (), loss, both_ids, flops=2 << 30)
    passed_a, passed_b = call(
        relay_kernel, "relay", [((cut - 16, width), bf16), ((rows - cut + 16, width), bf16)],
        (flags,), both_ids, mate_rows, mate_last, text, far, flops=1 << 30,
    )
    near_a, near_b = across(passed_a), across(passed_b)
    late, image_sum, loss = call(
        far_kernel, "far", [((rows, width), f32), ((rows, width), f32), ((1, rows), f32)],
        (flags, params), ids, mate_ids, both_ids, image_a, image_b, mate_a, mate_b, far, image_sum,
        loss,
    )
    image_grad, loss = call(
        near_kernel, "near", [((rows, width), bf16), ((1, rows), f32)],
        (flags, params), ids, mate_ids, both_ids, image_a, image_b, near_a, near_b, image_sum, loss,
    )
    late, image_grad = lax.optimization_barrier((late, image_grad))
    text_grad = add_part("add_a", 0, cut // STEP, arrived_a, late)
    text_grad = add_part("add_b", cut, (rows - cut) // STEP - 1, arrived_b, late, text_grad)
    text_grad = add_part("add_c", rows - STEP, 1, arrived_c, late, text_grad)
    return (loss.reshape(rows), image_grad, text_grad)


def solution(mesh):
    in_specs = (P(AXES, None), P(AXES, None), P(AXES, None), P(AXES), P(), P())
    out_specs = (P(AXES), P(AXES, None), P(AXES, None))
    return jax.shard_map(body, mesh=mesh, in_specs=in_specs, out_specs=out_specs, check_vma=False)
```

```python
import functools

import jax
import jax.numpy as jnp
from jax import lax
from jax.experimental import pallas as pl
from jax.experimental.pallas import tpu as pltpu
from jax.sharding import PartitionSpec as P

SHIFTS = 2
AXES = ("dp", "group")
STEP = 16
CHUNKS = 4
VMEM = pl.BlockSpec(memory_space=pltpu.VMEM)
SMEM = pl.BlockSpec(memory_space=pltpu.SMEM)
ANY = pl.BlockSpec(memory_space=pl.ANY)
HBM = pl.BlockSpec(memory_space=pltpu.HBM)


def dot(a, b, contract):
    return lax.dot_general(a, b, ((contract[:1], contract[1:]), ((), ())), preferred_element_type=jnp.float32)


def pair(images, texts, image_ids, text_ids, params):
    raw = dot(images, texts, (1, 1))
    rows = raw.shape[0]
    scale = jnp.exp(jnp.full((1, rows), params[0], jnp.float32))
    logits = scale * raw + params[1]
    same = jnp.broadcast_to(image_ids, (rows, rows)).T == text_ids
    margin = jnp.where(same, -logits, logits)
    tail = jnp.exp(-jnp.abs(margin))
    loss = jnp.maximum(margin, 0.0) + jnp.log1p(tail)
    sigmoid = jnp.where(margin >= 0, 1.0, tail) / (1.0 + tail)
    coef = jnp.where(same, -sigmoid, sigmoid) * scale
    return jnp.sum(loss.T, axis=0, keepdims=True), coef


def whole(a, b):
    return jnp.concatenate([a[...], b[...]], axis=0)


def low(coef):
    return coef.astype(jnp.bfloat16)


def cast_kernel(text, out, staged, sems):
    step = text.shape[0] // CHUNKS
    parts = [pl.ds(k * step, step) for k in range(CHUNKS)]
    copies = [pltpu.make_async_copy(text.at[part], staged.at[part], sems.at[k]) for k, part in enumerate(parts)]
    for k, copy in enumerate(copies):
        copy.start(priority=k % 2)
    for part, copy in zip(parts, copies):
        copy.wait()
        out[part, :] = staged[part, :].astype(out.dtype)


def load_kernel(text, image, out_a, out_b, sems):
    half = out_a.shape[0]
    copies = [
        pltpu.make_async_copy(image.at[pl.ds(0, half)], out_a, sems.at[0]),
        pltpu.make_async_copy(image.at[pl.ds(half, half)], out_b, sems.at[1]),
    ]
    for copy in copies:
        copy.start()
    for copy in copies:
        copy.wait()


def add_kernel(start, chunks, arrived, late, *refs):
    out, staged, sems = refs[-3:]
    step = arrived.shape[0] // chunks
    copies = []
    for k in range(chunks):
        here, there = pl.ds(k * step, step), pl.ds(start + k * step, step)
        staged[here, :] = arrived[here, :].astype(staged.dtype) + late[there, :]
        copies.append(pltpu.make_async_copy(staged.at[here], out.at[there], sems.at[k]))
        copies[-1].start()
    for copy in copies:
        copy.wait()


def own_kernel(flags, params, ids, mate_ids, image_a, image_b, mate_a, mate_b, text, accum_in, out_a, out_b, image_sum, loss,
               accum, sem):
    copy = pltpu.make_async_copy(accum_in, accum, sem)
    copy.start()
    image = whole(image_a, image_b)
    own_loss, coef = pair(image, text[...], ids[...], ids[...], params)
    loss[...] = own_loss
    copy.wait()
    total = accum[...] + dot(low(coef.T), image, (1, 0))
    cut = out_a.shape[0]

    def give(value):
        out_a[...] = value[:cut, :].astype(out_a.dtype)
        out_b[...] = value[cut:, :].astype(out_b.dtype)

    @pl.when(flags[0] == 0)
    def _():
        mate = whole(mate_a, mate_b)
        _, mate_coef = pair(mate, text[...], mate_ids[...], ids[...], params)
        give(total + dot(low(mate_coef.T), mate, (1, 0)))

    @pl.when(flags[0] == 1)
    def _():
        give(total)

    image_sum[...] = dot(low(coef), text[...], (1, 0))


def ids_kernel(token, both_ids, out):
    out[...] = both_ids[...]


def relay_kernel(flags, token, before, text, far, out_a, out_b):
    cut = out_a.shape[0]

    def fill(source):
        out_a[...] = source[:cut, :]
        out_b[...] = source[cut:, :]

    pl.when(flags[0] == 0)(lambda: fill(text))
    pl.when(flags[0] == 1)(lambda: fill(far))


def far_kernel(flags, params, ids, mate_ids, both_ids, image_a, image_b, mate_a, mate_b, far, image_in,
               loss_in, late, image_sum, loss):
    image = whole(image_a, image_b)
    more, coef = pair(image, far[...], ids[...], both_ids[:1, :], params)
    loss[...] = loss_in[...] + more
    image_sum[...] = image_in[...] + dot(low(coef), far[...], (1, 0))
    part = dot(low(coef.T), image, (1, 0))

    @pl.when(flags[0] == 0)
    def _():
        late[...] = part

    @pl.when(flags[0] == 1)
    def _():
        mate = whole(mate_a, mate_b)
        _, mate_coef = pair(mate, far[...], mate_ids[...], both_ids[:1, :], params)
        late[...] = part + dot(low(mate_coef.T), mate, (1, 0))


def near_kernel(flags, params, ids, mate_ids, both_ids, image_a, image_b, near_a, near_b, image_in, loss_in,
                image_grad, loss):
    image = whole(image_a, image_b)
    near_ids = jnp.where(flags[0] == 0, both_ids[1:, :], mate_ids[...])
    near = whole(near_a, near_b)
    more, coef = pair(image, near, ids[...], near_ids, params)
    loss[...] = (loss_in[...] + more) * (1.0 / ((SHIFTS + 1) * image.shape[0]))
    image_grad[...] = (image_in[...] + dot(low(coef), near, (1, 0))).astype(image_grad.dtype)


def call(kernel, name, outs, scalars, *operands, flops=0):
    return pl.pallas_call(
        kernel,
        out_shape=[jax.ShapeDtypeStruct(s, d) for s, d in outs],
        in_specs=[SMEM] * len(scalars) + [VMEM] * len(operands),
        out_specs=[VMEM] * len(outs),
        compiler_params=pltpu.CompilerParams(vmem_limit_bytes=16 * 1024 * 1024),
        cost_estimate=pl.CostEstimate(flops=flops, bytes_accessed=0, transcendentals=0),
        name=name,
    )(*scalars, *operands)


def add_part(name, start, chunks, arrived, late, *before):
    return pl.pallas_call(
        functools.partial(add_kernel, start, chunks),
        out_shape=jax.ShapeDtypeStruct(late.shape, late.dtype),
        in_specs=[VMEM, VMEM] + [HBM] * len(before),
        out_specs=HBM,
        scratch_shapes=[pltpu.VMEM(arrived.shape, late.dtype), pltpu.SemaphoreType.DMA((chunks,))],
        input_output_aliases={2: 0} if before else {},
        compiler_params=pltpu.CompilerParams(vmem_limit_bytes=16 * 1024 * 1024),
        cost_estimate=pl.CostEstimate(flops=0, bytes_accessed=0, transcendentals=0),
        name=name,
    )(arrived, late, *before)


def body(image_emb, text_emb, text_accum, pair_ids, log_scale, bias):
    count = lax.axis_size(AXES)
    rows, width = image_emb.shape
    half = rows // 2
    f32, bf16 = jnp.float32, jnp.bfloat16
    flags = (lax.axis_index("group") % 2).astype(jnp.int32).reshape(1)
    params = jnp.concatenate([log_scale, bias])
    ids = pair_ids.reshape(1, rows)

    skip = [(i, (i + 2) % count) for i in range(count)]
    swap = [(i, i ^ 1) for i in range(count)]

    def ahead(value):
        return lax.ppermute(value, AXES, skip)

    def across(value):
        return lax.ppermute(value, AXES, swap)

    text = pl.pallas_call(
        cast_kernel,
        out_shape=jax.ShapeDtypeStruct((rows, width), bf16),
        in_specs=[HBM],
        out_specs=VMEM,
        scratch_shapes=[pltpu.VMEM((rows, width), f32), pltpu.SemaphoreType.DMA((CHUNKS,))],
        compiler_params=pltpu.CompilerParams(vmem_limit_bytes=16 * 1024 * 1024),
        cost_estimate=pl.CostEstimate(flops=0, bytes_accessed=0, transcendentals=0),
        name="cast",
    )(pltpu.with_memory_space_constraint(text_emb, pltpu.HBM))
    far = ahead(text)

    image_a, image_b = pl.pallas_call(
        load_kernel,
        out_shape=[jax.ShapeDtypeStruct((n, width), bf16) for n in (half, rows - half)],
        in_specs=[ANY, HBM],
        out_specs=[VMEM] * 2,
        scratch_shapes=[pltpu.SemaphoreType.DMA((2,))],
        compiler_params=pltpu.CompilerParams(vmem_limit_bytes=16 * 1024 * 1024),
        cost_estimate=pl.CostEstimate(flops=0, bytes_accessed=0, transcendentals=0),
        name="load",
    )(text, pltpu.with_memory_space_constraint(image_emb, pltpu.HBM))
    mate_a, mate_b = across(image_a), across(image_b)
    mate_ids = across(ids)
    both_ids = ahead(jnp.concatenate([ids, mate_ids]))

    cut = rows - rows * 3 // 16
    out_a, out_b, image_sum, loss = pl.pallas_call(
        own_kernel,
        out_shape=[
            jax.ShapeDtypeStruct((cut, width), bf16),
            jax.ShapeDtypeStruct((rows - cut, width), bf16),
            jax.ShapeDtypeStruct((rows, width), f32),
            jax.ShapeDtypeStruct((1, rows), f32),
        ],
        in_specs=[SMEM] * 2 + [VMEM] * 7 + [HBM],
        out_specs=[VMEM] * 4,
        scratch_shapes=[pltpu.VMEM((rows, width), f32), pltpu.SemaphoreType.DMA],
        compiler_params=pltpu.CompilerParams(vmem_limit_bytes=16 * 1024 * 1024),
        cost_estimate=pl.CostEstimate(flops=0, bytes_accessed=0, transcendentals=0),
        name="own",
    )(flags, params, ids, mate_ids, image_a, image_b, mate_a, mate_b, text,
      pltpu.with_memory_space_constraint(text_accum, pltpu.HBM))
    crossed = [(i, target ^ 1) for i, target in skip]
    arrived_a = ahead(out_a)
    mate_rows = across(out_b)
    arrived_b = lax.ppermute(mate_rows, AXES, crossed)

    (both_ids,) = call(ids_kernel, "ids", [((2, rows), jnp.int32)], (), loss, both_ids, flops=2 << 30)
    passed_a, passed_b = call(
        relay_kernel, "relay", [((cut - 16, width), bf16), ((rows - cut + 16, width), bf16)],
        (flags,), both_ids, mate_rows, text, far, flops=1 << 30,
    )
    near_a, near_b = across(passed_a), across(passed_b)
    late, image_sum, loss = call(
        far_kernel, "far", [((rows, width), f32), ((rows, width), f32), ((1, rows), f32)],
        (flags, params), ids, mate_ids, both_ids, image_a, image_b, mate_a, mate_b, far, image_sum,
        loss,
    )
    image_grad, loss = call(
        near_kernel, "near", [((rows, width), bf16), ((1, rows), f32)],
        (flags, params), ids, mate_ids, both_ids, image_a, image_b, near_a, near_b, image_sum, loss,
    )
    late, image_grad = lax.optimization_barrier((late, image_grad))
    text_grad = add_part("add_a", 0, cut // STEP, arrived_a, late)
    text_grad = add_part("add_b", cut, (rows - cut) // STEP, arrived_b, late, text_grad)
    return (loss.reshape(rows), image_grad, text_grad)


def solution(mesh):
    in_specs = (P(AXES, None), P(AXES, None), P(AXES, None), P(AXES), P(), P())
    out_specs = (P(AXES), P(AXES, None), P(AXES, None))
    return jax.shard_map(body, mesh=mesh, in_specs=in_specs, out_specs=out_specs, check_vma=False)
```

```python
import functools

import jax
import jax.numpy as jnp
from jax import lax
from jax.experimental import pallas as pl
from jax.experimental.pallas import tpu as pltpu
from jax.sharding import PartitionSpec as P

SHIFTS = 2
AXES = ("dp", "group")
STEP = 32
VMEM = pl.BlockSpec(memory_space=pltpu.VMEM)
SMEM = pl.BlockSpec(memory_space=pltpu.SMEM)
ANY = pl.BlockSpec(memory_space=pl.ANY)
HBM = pl.BlockSpec(memory_space=pltpu.HBM)


def dot(a, b, contract):
    return lax.dot_general(a, b, ((contract[:1], contract[1:]), ((), ())), preferred_element_type=jnp.float32)


def pair(images, texts, image_ids, text_ids, params):
    raw = dot(images, texts, (1, 1))
    rows = raw.shape[0]
    scale = jnp.exp(jnp.full((1, rows), params[0], jnp.float32))
    logits = scale * raw + params[1]
    same = jnp.broadcast_to(image_ids, (rows, rows)).T == text_ids
    margin = jnp.where(same, -logits, logits)
    tail = jnp.exp(-jnp.abs(margin))
    loss = jnp.maximum(margin, 0.0) + jnp.log1p(tail)
    sigmoid = jnp.where(margin >= 0, 1.0, tail) / (1.0 + tail)
    coef = jnp.where(same, -sigmoid, sigmoid) * scale
    return jnp.sum(loss.T, axis=0, keepdims=True), coef


def whole(a, b):
    return jnp.concatenate([a[...], b[...]], axis=0)


def low(coef):
    return coef.astype(jnp.bfloat16)


def cast_kernel(text, out):
    out[...] = text[...].astype(out.dtype)


def load_kernel(text, image, out_a, out_b, sems):
    half = out_a.shape[0]
    copies = [
        pltpu.make_async_copy(image.at[pl.ds(0, half)], out_a, sems.at[0]),
        pltpu.make_async_copy(image.at[pl.ds(half, half)], out_b, sems.at[1]),
    ]
    for copy in copies:
        copy.start()
    for copy in copies:
        copy.wait()


def add_kernel(start, chunks, arrived, late, *refs):
    out, staged, sems = refs[-3:]
    step = arrived.shape[0] // chunks
    copies = []
    for k in range(chunks):
        here, there = pl.ds(k * step, step), pl.ds(start + k * step, step)
        staged[here, :] = arrived[here, :].astype(staged.dtype) + late[there, :]
        copies.append(pltpu.make_async_copy(staged.at[here], out.at[there], sems.at[k]))
        copies[-1].start()
    for copy in copies:
        copy.wait()


def own_kernel(flags, params, ids, mate_ids, image_a, image_b, mate_a, mate_b, text, accum_in, out_a, out_b, image_sum, loss,
               accum, sem):
    copy = pltpu.make_async_copy(accum_in, accum, sem)
    copy.start()
    image = whole(image_a, image_b)
    own_loss, coef = pair(image, text[...], ids[...], ids[...], params)
    loss[...] = own_loss
    copy.wait()
    total = accum[...] + dot(low(coef.T), image, (1, 0))
    cut = out_a.shape[0]

    def give(value):
        out_a[...] = value[:cut, :].astype(out_a.dtype)
        out_b[...] = value[cut:, :].astype(out_b.dtype)

    @pl.when(flags[0] == 0)
    def _():
        mate = whole(mate_a, mate_b)
        _, mate_coef = pair(mate, text[...], mate_ids[...], ids[...], params)
        give(total + dot(low(mate_coef.T), mate, (1, 0)))

    @pl.when(flags[0] == 1)
    def _():
        give(total)

    image_sum[...] = dot(low(coef), text[...], (1, 0))


def ids_kernel(token, both_ids, out):
    out[...] = both_ids[...]


def relay_kernel(flags, token, before, text, far, out_a, out_b):
    cut = out_a.shape[0]

    def fill(source):
        out_a[...] = source[:cut, :]
        out_b[...] = source[cut:, :]

    pl.when(flags[0] == 0)(lambda: fill(text))
    pl.when(flags[0] == 1)(lambda: fill(far))


def far_kernel(flags, params, ids, mate_ids, both_ids, image_a, image_b, mate_a, mate_b, far, image_in,
               loss_in, late, image_sum, loss):
    image = whole(image_a, image_b)
    more, coef = pair(image, far[...], ids[...], both_ids[:1, :], params)
    loss[...] = loss_in[...] + more
    image_sum[...] = image_in[...] + dot(low(coef), far[...], (1, 0))
    part = dot(low(coef.T), image, (1, 0))

    @pl.when(flags[0] == 0)
    def _():
        late[...] = part

    @pl.when(flags[0] == 1)
    def _():
        mate = whole(mate_a, mate_b)
        _, mate_coef = pair(mate, far[...], mate_ids[...], both_ids[:1, :], params)
        late[...] = part + dot(low(mate_coef.T), mate, (1, 0))


def near_kernel(flags, params, ids, mate_ids, both_ids, image_a, image_b, near_a, near_b, image_in, loss_in,
                image_grad, loss):
    image = whole(image_a, image_b)
    near_ids = jnp.where(flags[0] == 0, both_ids[1:, :], mate_ids[...])
    near = whole(near_a, near_b)
    more, coef = pair(image, near, ids[...], near_ids, params)
    loss[...] = (loss_in[...] + more) * (1.0 / ((SHIFTS + 1) * image.shape[0]))
    image_grad[...] = (image_in[...] + dot(low(coef), near, (1, 0))).astype(image_grad.dtype)


def call(kernel, name, outs, scalars, *operands, flops=0):
    return pl.pallas_call(
        kernel,
        out_shape=[jax.ShapeDtypeStruct(s, d) for s, d in outs],
        in_specs=[SMEM] * len(scalars) + [VMEM] * len(operands),
        out_specs=[VMEM] * len(outs),
        compiler_params=pltpu.CompilerParams(vmem_limit_bytes=16 * 1024 * 1024),
        cost_estimate=pl.CostEstimate(flops=flops, bytes_accessed=0, transcendentals=0),
        name=name,
    )(*scalars, *operands)


def add_part(name, start, chunks, arrived, late, *before):
    return pl.pallas_call(
        functools.partial(add_kernel, start, chunks),
        out_shape=jax.ShapeDtypeStruct(late.shape, late.dtype),
        in_specs=[VMEM, VMEM] + [HBM] * len(before),
        out_specs=HBM,
        scratch_shapes=[pltpu.VMEM(arrived.shape, late.dtype), pltpu.SemaphoreType.DMA((chunks,))],
        input_output_aliases={2: 0} if before else {},
        compiler_params=pltpu.CompilerParams(vmem_limit_bytes=16 * 1024 * 1024),
        cost_estimate=pl.CostEstimate(flops=0, bytes_accessed=0, transcendentals=0),
        name=name,
    )(arrived, late, *before)


def body(image_emb, text_emb, text_accum, pair_ids, log_scale, bias):
    count = lax.axis_size(AXES)
    rows, width = image_emb.shape
    half = rows // 2
    f32, bf16 = jnp.float32, jnp.bfloat16
    flags = (lax.axis_index("group") % 2).astype(jnp.int32).reshape(1)
    params = jnp.concatenate([log_scale, bias])
    ids = pair_ids.reshape(1, rows)

    skip = [(i, (i + 2) % count) for i in range(count)]
    swap = [(i, i ^ 1) for i in range(count)]

    def ahead(value):
        return lax.ppermute(value, AXES, skip)

    def across(value):
        return lax.ppermute(value, AXES, swap)

    (text,) = call(cast_kernel, "cast", [((rows, width), bf16)], (), text_emb)
    far = ahead(text)

    image_a, image_b = pl.pallas_call(
        load_kernel,
        out_shape=[jax.ShapeDtypeStruct((n, width), bf16) for n in (half, rows - half)],
        in_specs=[ANY, HBM],
        out_specs=[VMEM] * 2,
        scratch_shapes=[pltpu.SemaphoreType.DMA((2,))],
        compiler_params=pltpu.CompilerParams(vmem_limit_bytes=16 * 1024 * 1024),
        cost_estimate=pl.CostEstimate(flops=0, bytes_accessed=0, transcendentals=0),
        name="load",
    )(text, pltpu.with_memory_space_constraint(image_emb, pltpu.HBM))
    mate_a, mate_b = across(image_a), across(image_b)
    mate_ids = across(ids)
    both_ids = ahead(jnp.concatenate([ids, mate_ids]))

    cut = rows - rows // 4
    out_a, out_b, image_sum, loss = pl.pallas_call(
        own_kernel,
        out_shape=[
            jax.ShapeDtypeStruct((cut, width), bf16),
            jax.ShapeDtypeStruct((rows - cut, width), bf16),
            jax.ShapeDtypeStruct((rows, width), f32),
            jax.ShapeDtypeStruct((1, rows), f32),
        ],
        in_specs=[SMEM] * 2 + [VMEM] * 7 + [HBM],
        out_specs=[VMEM] * 4,
        scratch_shapes=[pltpu.VMEM((rows, width), f32), pltpu.SemaphoreType.DMA],
        compiler_params=pltpu.CompilerParams(vmem_limit_bytes=16 * 1024 * 1024),
        cost_estimate=pl.CostEstimate(flops=0, bytes_accessed=0, transcendentals=0),
        name="own",
    )(flags, params, ids, mate_ids, image_a, image_b, mate_a, mate_b, text,
      pltpu.with_memory_space_constraint(text_accum, pltpu.HBM))
    crossed = [(i, target ^ 1) for i, target in skip]
    arrived_a = ahead(out_a)
    mate_rows = across(out_b)
    arrived_b = lax.ppermute(mate_rows, AXES, crossed)

    (both_ids,) = call(ids_kernel, "ids", [((2, rows), jnp.int32)], (), loss, both_ids, flops=2 << 30)
    passed_a, passed_b = call(
        relay_kernel, "relay", [((cut - 16, width), bf16), ((rows - cut + 16, width), bf16)],
        (flags,), both_ids, mate_rows, text, far, flops=1 << 30,
    )
    near_a, near_b = across(passed_a), across(passed_b)
    late, image_sum, loss = call(
        far_kernel, "far", [((rows, width), f32), ((rows, width), f32), ((1, rows), f32)],
        (flags, params), ids, mate_ids, both_ids, image_a, image_b, mate_a, mate_b, far, image_sum,
        loss,
    )
    image_grad, loss = call(
        near_kernel, "near", [((rows, width), bf16), ((1, rows), f32)],
        (flags, params), ids, mate_ids, both_ids, image_a, image_b, near_a, near_b, image_sum, loss,
    )
    late, image_grad = lax.optimization_barrier((late, image_grad))
    text_grad = add_part("add_a", 0, cut // STEP, arrived_a, late)
    text_grad = add_part("add_b", cut, (rows - cut) // STEP, arrived_b, late, text_grad)
    return (loss.reshape(rows), image_grad, text_grad)


def solution(mesh):
    in_specs = (P(AXES, None), P(AXES, None), P(AXES, None), P(AXES), P(), P())
    out_specs = (P(AXES), P(AXES, None), P(AXES, None))
    return jax.shard_map(body, mesh=mesh, in_specs=in_specs, out_specs=out_specs, check_vma=False)
```

```python
import functools

import jax
import jax.numpy as jnp
from jax import lax
from jax.experimental import pallas as pl
from jax.experimental.pallas import tpu as pltpu
from jax.sharding import PartitionSpec as P

SHIFTS = 2
AXES = ("dp", "group")
STEP = 16
VMEM = pl.BlockSpec(memory_space=pltpu.VMEM)
SMEM = pl.BlockSpec(memory_space=pltpu.SMEM)
ANY = pl.BlockSpec(memory_space=pl.ANY)
HBM = pl.BlockSpec(memory_space=pltpu.HBM)


def dot(a, b, contract):
    return lax.dot_general(a, b, ((contract[:1], contract[1:]), ((), ())), preferred_element_type=jnp.float32)


def pair(images, texts, image_ids, text_ids, params):
    raw = dot(images, texts, (1, 1))
    rows = raw.shape[0]
    scale = jnp.exp(jnp.full((1, rows), params[0], jnp.float32))
    logits = scale * raw + params[1]
    same = jnp.broadcast_to(image_ids, (rows, rows)).T == text_ids
    margin = jnp.where(same, -logits, logits)
    tail = jnp.exp(-jnp.abs(margin))
    loss = jnp.maximum(margin, 0.0) + jnp.log1p(tail)
    sigmoid = jnp.where(margin >= 0, 1.0, tail) / (1.0 + tail)
    coef = jnp.where(same, -sigmoid, sigmoid) * scale
    return jnp.sum(loss.T, axis=0, keepdims=True), coef


def whole(a, b):
    return jnp.concatenate([a[...], b[...]], axis=0)


def low(coef):
    return coef.astype(jnp.bfloat16)


def cast_kernel(text, out):
    out[...] = text[...].astype(out.dtype)


def load_kernel(text, image, out_a, out_b, sems):
    half = out_a.shape[0]
    copies = [
        pltpu.make_async_copy(image.at[pl.ds(0, half)], out_a, sems.at[0]),
        pltpu.make_async_copy(image.at[pl.ds(half, half)], out_b, sems.at[1]),
    ]
    for copy in copies:
        copy.start()
    for copy in copies:
        copy.wait()


def add_kernel(start, chunks, arrived, late, *refs):
    out, staged, sems = refs[-3:]
    step = arrived.shape[0] // chunks
    copies = []
    for k in range(chunks):
        here, there = pl.ds(k * step, step), pl.ds(start + k * step, step)
        staged[here, :] = arrived[here, :].astype(staged.dtype) + late[there, :]
        copies.append(pltpu.make_async_copy(staged.at[here], out.at[there], sems.at[k]))
        copies[-1].start()
    for copy in copies:
        copy.wait()


def own_kernel(flags, params, ids, mate_ids, image_a, image_b, mate_a, mate_b, text, accum_in, out_a, out_b, image_sum, loss,
               accum, sem):
    copy = pltpu.make_async_copy(accum_in, accum, sem)
    copy.start()
    image = whole(image_a, image_b)
    own_loss, coef = pair(image, text[...], ids[...], ids[...], params)
    loss[...] = own_loss
    image_sum[...] = dot(low(coef), text[...], (1, 0))
    cut = out_a.shape[0]

    def give(value):
        out_a[...] = value[:cut, :].astype(out_a.dtype)
        out_b[...] = value[cut:, :].astype(out_b.dtype)

    @pl.when(flags[0] == 0)
    def _():
        mate = whole(mate_a, mate_b)
        _, mate_coef = pair(mate, text[...], mate_ids[...], ids[...], params)
        copy.wait()
        give(accum[...] + dot(low(coef.T), image, (1, 0)) + dot(low(mate_coef.T), mate, (1, 0)))

    @pl.when(flags[0] == 1)
    def _():
        copy.wait()
        give(accum[...] + dot(low(coef.T), image, (1, 0)))


def ids_kernel(token, both_ids, out):
    out[...] = both_ids[...]


def relay_kernel(flags, token, before, text, far, out_a, out_b):
    cut = out_a.shape[0]

    def fill(source):
        out_a[...] = source[:cut, :]
        out_b[...] = source[cut:, :]

    pl.when(flags[0] == 0)(lambda: fill(text))
    pl.when(flags[0] == 1)(lambda: fill(far))


def far_kernel(flags, params, ids, mate_ids, both_ids, image_a, image_b, mate_a, mate_b, far, image_in,
               loss_in, late, image_sum, loss):
    image = whole(image_a, image_b)
    more, coef = pair(image, far[...], ids[...], both_ids[:1, :], params)
    loss[...] = loss_in[...] + more
    image_sum[...] = image_in[...] + dot(low(coef), far[...], (1, 0))
    part = dot(low(coef.T), image, (1, 0))

    @pl.when(flags[0] == 0)
    def _():
        late[...] = part

    @pl.when(flags[0] == 1)
    def _():
        mate = whole(mate_a, mate_b)
        _, mate_coef = pair(mate, far[...], mate_ids[...], both_ids[:1, :], params)
        late[...] = part + dot(low(mate_coef.T), mate, (1, 0))


def near_kernel(flags, params, ids, mate_ids, both_ids, image_a, image_b, near_a, near_b, image_in, loss_in,
                image_grad, loss):
    image = whole(image_a, image_b)
    near_ids = jnp.where(flags[0] == 0, both_ids[1:, :], mate_ids[...])
    near = whole(near_a, near_b)
    more, coef = pair(image, near, ids[...], near_ids, params)
    loss[...] = (loss_in[...] + more) * (1.0 / ((SHIFTS + 1) * image.shape[0]))
    image_grad[...] = (image_in[...] + dot(low(coef), near, (1, 0))).astype(image_grad.dtype)


def call(kernel, name, outs, scalars, *operands, flops=0):
    return pl.pallas_call(
        kernel,
        out_shape=[jax.ShapeDtypeStruct(s, d) for s, d in outs],
        in_specs=[SMEM] * len(scalars) + [VMEM] * len(operands),
        out_specs=[VMEM] * len(outs),
        compiler_params=pltpu.CompilerParams(vmem_limit_bytes=16 * 1024 * 1024),
        cost_estimate=pl.CostEstimate(flops=flops, bytes_accessed=0, transcendentals=0),
        name=name,
    )(*scalars, *operands)


def add_part(name, start, chunks, arrived, late, *before):
    return pl.pallas_call(
        functools.partial(add_kernel, start, chunks),
        out_shape=jax.ShapeDtypeStruct(late.shape, late.dtype),
        in_specs=[VMEM, VMEM] + [HBM] * len(before),
        out_specs=HBM,
        scratch_shapes=[pltpu.VMEM(arrived.shape, late.dtype), pltpu.SemaphoreType.DMA((chunks,))],
        input_output_aliases={2: 0} if before else {},
        compiler_params=pltpu.CompilerParams(vmem_limit_bytes=16 * 1024 * 1024),
        cost_estimate=pl.CostEstimate(flops=0, bytes_accessed=0, transcendentals=0),
        name=name,
    )(arrived, late, *before)


def body(image_emb, text_emb, text_accum, pair_ids, log_scale, bias):
    count = lax.axis_size(AXES)
    rows, width = image_emb.shape
    half = rows // 2
    f32, bf16 = jnp.float32, jnp.bfloat16
    flags = (lax.axis_index("group") % 2).astype(jnp.int32).reshape(1)
    params = jnp.concatenate([log_scale, bias])
    ids = pair_ids.reshape(1, rows)

    skip = [(i, (i + 2) % count) for i in range(count)]
    swap = [(i, i ^ 1) for i in range(count)]

    def ahead(value):
        return lax.ppermute(value, AXES, skip)

    def across(value):
        return lax.ppermute(value, AXES, swap)

    (text,) = call(cast_kernel, "cast", [((rows, width), bf16)], (), text_emb)
    far = ahead(text)

    image_a, image_b = pl.pallas_call(
        load_kernel,
        out_shape=[jax.ShapeDtypeStruct((n, width), bf16) for n in (half, rows - half)],
        in_specs=[ANY, HBM],
        out_specs=[VMEM] * 2,
        scratch_shapes=[pltpu.SemaphoreType.DMA((2,))],
        compiler_params=pltpu.CompilerParams(vmem_limit_bytes=16 * 1024 * 1024),
        cost_estimate=pl.CostEstimate(flops=0, bytes_accessed=0, transcendentals=0),
        name="load",
    )(text, pltpu.with_memory_space_constraint(image_emb, pltpu.HBM))
    mate_a, mate_b = across(image_a), across(image_b)
    mate_ids = across(ids)
    both_ids = ahead(jnp.concatenate([ids, mate_ids]))

    cut = rows - rows // 4
    out_a, out_b, image_sum, loss = pl.pallas_call(
        own_kernel,
        out_shape=[
            jax.ShapeDtypeStruct((cut, width), bf16),
            jax.ShapeDtypeStruct((rows - cut, width), bf16),
            jax.ShapeDtypeStruct((rows, width), f32),
            jax.ShapeDtypeStruct((1, rows), f32),
        ],
        in_specs=[SMEM] * 2 + [VMEM] * 7 + [HBM],
        out_specs=[VMEM] * 4,
        scratch_shapes=[pltpu.VMEM((rows, width), f32), pltpu.SemaphoreType.DMA],
        compiler_params=pltpu.CompilerParams(vmem_limit_bytes=16 * 1024 * 1024),
        cost_estimate=pl.CostEstimate(flops=0, bytes_accessed=0, transcendentals=0),
        name="own",
    )(flags, params, ids, mate_ids, image_a, image_b, mate_a, mate_b, text,
      pltpu.with_memory_space_constraint(text_accum, pltpu.HBM))
    crossed = [(i, target ^ 1) for i, target in skip]
    arrived_a = ahead(out_a)
    mate_rows = across(out_b)
    arrived_b = lax.ppermute(mate_rows, AXES, crossed)

    (both_ids,) = call(ids_kernel, "ids", [((2, rows), jnp.int32)], (), loss, both_ids, flops=2 << 30)
    passed_a, passed_b = call(
        relay_kernel, "relay", [((cut - 16, width), bf16), ((rows - cut + 16, width), bf16)],
        (flags,), both_ids, mate_rows, text, far, flops=1 << 30,
    )
    near_a, near_b = across(passed_a), across(passed_b)
    late, image_sum, loss = call(
        far_kernel, "far", [((rows, width), f32), ((rows, width), f32), ((1, rows), f32)],
        (flags, params), ids, mate_ids, both_ids, image_a, image_b, mate_a, mate_b, far, image_sum,
        loss,
    )
    image_grad, loss = call(
        near_kernel, "near", [((rows, width), bf16), ((1, rows), f32)],
        (flags, params), ids, mate_ids, both_ids, image_a, image_b, near_a, near_b, image_sum, loss,
    )
    late, image_grad = lax.optimization_barrier((late, image_grad))
    text_grad = add_part("add_a", 0, cut // STEP, arrived_a, late)
    text_grad = add_part("add_b", cut, (rows - cut) // STEP, arrived_b, late, text_grad)
    return (loss.reshape(rows), image_grad, text_grad)


def solution(mesh):
    in_specs = (P(AXES, None), P(AXES, None), P(AXES, None), P(AXES), P(), P())
    out_specs = (P(AXES), P(AXES, None), P(AXES, None))
    return jax.shard_map(body, mesh=mesh, in_specs=in_specs, out_specs=out_specs, check_vma=False)
```
